256 devices in a mesh: ctx: 64 (over x, z, core), tp: 4 (over y).
Axes of the slice: x: 4, y: 4, z: 8, core: 2. Of those that a mesh axis runs over, the one named last changes fastest.
Arguments:
- x_raw: bfloat16 [8192, 4096], P('ctx', 'tp'), may hold values from -6 to 6
- b_raw: bfloat16 [8192, 512], P('ctx'), may hold values from -0.59765625 to 0.59765625
- c_raw: bfloat16 [8192, 512], P('ctx'), may hold values from -0.59765625 to 0.59765625
- z_gate: bfloat16 [8192, 4096], P('ctx', 'tp'), may hold values from -6 to 6
- dt_raw: float32 [8192, 128], P('ctx', 'tp'), may hold values from -4 to 4
- conv_x: float32 [4, 4096], P(None, 'tp'), may hold values from -3 to 3
- conv_b: float32 [4, 512], replicated, may hold values from -3 to 3
- conv_c: float32 [4, 512], replicated, may hold values from -3 to 3
- dt_bias: float32 [128], P('tp'), may hold values from -1 to 1
- a_log: float32 [128], P('tp'), may hold values from -14 to -3
- d_skip: float32 [128], P('tp'), may hold values from 0.5 to 1.5
- gain: float32 [4096], P('tp'), may hold values from 0.5 to 1.5
- grad_out: bfloat16 [8192, 4096], P('ctx', 'tp'), may hold values from -6 to 6
Outputs:
- grad_x_raw: bfloat16 [8192, 4096], P('ctx', 'tp')
- grad_b_raw: bfloat16 [8192, 512], P('ctx')
- grad_c_raw: bfloat16 [8192, 512], P('ctx')
- grad_z_gate: bfloat16 [8192, 4096], P('ctx', 'tp')
- grad_dt_raw: float32 [8192, 128], P('ctx', 'tp')
- grad_conv_x: float32 [4, 4096], P(None, 'tp')
- grad_conv_b: float32 [4, 512], replicated
- grad_conv_c: float32 [4, 512], replicated
- grad_dt_bias: float32 [128], P('tp')
- grad_a_log: float32 [128], P('tp')
- grad_d_skip: float32 [128], P('tp')
- grad_gain: float32 [4096], P('tp')
The draws below stay inside these ranges and needn't reach their ends.
All inputs are finite; a program needn't handle non-finite values.
Results may differ from the reference program's by a relative error of at most 0.00105.
Values may be sent and summed in bfloat16 or wider, within the bound.
No kernel may reach another device: no remote copies, remote signals or barrier semaphores. Data moves between devices by JAX's collectives and lax.ppermute only.
A program may use at most 192 MiB of HBM per device.

```python
import jax
import jax.numpy as jnp
from jax import lax

HEADS = 128
HEAD_DIM = 32
STATE = 128
GROUPS = 4
CONV = 4
SPAN = 128
TOKENS = 8192


def draw_a_log(key, part):
    pick_key, level_key = jax.random.split(jax.random.fold_in(key, 11))
    levels = jax.random.uniform(level_key, (HEADS,), jnp.float32)
    slow_share = 0.5
    slow_value = jnp.log(0.15 / TOKENS) + levels * jnp.log(10.0)
    fast_value = jnp.log(1.0 / 60.0) + levels * jnp.log(2.4)
    slow_pick = jax.random.uniform(pick_key, (HEADS,), jnp.float32) < slow_share
    return jnp.where(slow_pick, slow_value, fast_value).astype(jnp.float32)


def block_scale(own_key, dims, cuts, least, top_value):
    level = 1.0
    for position, blocks in cuts:
        heights = jax.random.uniform(jax.random.fold_in(jax.random.fold_in(own_key, 6), position), (blocks,), jnp.float32, least / len(cuts), top_value / len(cuts))
        level = level * jnp.repeat(jnp.exp(heights), dims[position] // blocks).reshape((-1,) + (1,) * (len(dims) - 1 - position))
    return level


def noise(key, dims, deviation, most, shards=(), kind=jnp.bfloat16):
    entries = deviation * jax.random.normal(key, dims, jnp.float32)
    if shards:
        entries = entries * block_scale(key, dims, shards, -0.22, 0.18)
    return jnp.clip(entries, -most, most).astype(kind)


def setup_inputs(seed: int = 0) -> dict:
    seeds = jax.random.split(jax.random.key(seed), 14)
    x_raw = noise(seeds[0], (TOKENS, HEADS * HEAD_DIM), 1.0, 6.0, ((0, 64), (1, 4)))
    b_raw = noise(seeds[1], (TOKENS, GROUPS * STATE), 0.1, 0.59765625, ((0, 64),))
    c_raw = noise(seeds[2], (TOKENS, GROUPS * STATE), 0.1, 0.59765625, ((0, 64),))
    z_gate = noise(seeds[3], (TOKENS, HEADS * HEAD_DIM), 1.0, 6.0, ((0, 64), (1, 4)))
    dt_raw = noise(seeds[4], (TOKENS, HEADS), 1.0, 4.0, ((0, 64), (1, 4)), jnp.float32)
    conv_x = noise(seeds[5], (CONV, HEADS * HEAD_DIM), CONV ** -0.5, 3.0, ((1, 4),), jnp.float32)
    conv_b = noise(seeds[6], (CONV, GROUPS * STATE), CONV ** -0.5, 3.0, (), jnp.float32)
    conv_c = noise(seeds[7], (CONV, GROUPS * STATE), CONV ** -0.5, 3.0, (), jnp.float32)
    dt_bias = jnp.clip(jax.random.uniform(seeds[8], (HEADS,), jnp.float32, -1.0, 1.0) * block_scale(seeds[8], (HEADS,), ((0, 4),), -0.4, 0.0), -1.0, 1.0)
    a_log = draw_a_log(jax.random.fold_in(seeds[13], 71), 0)
    d_skip = jnp.clip(0.5 + 1.0 * jax.random.uniform(seeds[10], (HEADS,), jnp.float32) ** block_scale(seeds[10], (HEADS,), ((0, 4),), -0.2, 0.2), 0.5, 1.5)
    gain = jnp.clip(0.5 + 1.0 * jax.random.uniform(seeds[11], (HEADS * HEAD_DIM,), jnp.float32) ** block_scale(seeds[11], (HEADS * HEAD_DIM,), ((0, 4),), -0.2, 0.2), 0.5, 1.5)
    grad_out = noise(seeds[12], (TOKENS, HEADS * HEAD_DIM), 1.0, 6.0, ((0, 64), (1, 4)))
    return {"x_raw": x_raw, "b_raw": b_raw, "c_raw": c_raw, "z_gate": z_gate, "dt_raw": dt_raw, "conv_x": conv_x, "conv_b": conv_b, "conv_c": conv_c, "dt_bias": dt_bias, "a_log": a_log, "d_skip": d_skip, "gain": gain, "grad_out": grad_out}


PRECISE = lax.Precision.HIGHEST
EPSILON = 1e-05

def shifted_conv(extended, weight):
    tap_count = weight.shape[0]
    length = extended.shape[0] - tap_count + 1
    total = weight[0] * extended[0:length]
    for offset in range(1, tap_count):
        total = total + weight[offset] * extended[offset:offset + length]
    return jax.nn.silu(total)

def causal_conv(raw_rows, weight):
    padding = jnp.zeros((weight.shape[0] - 1, raw_rows.shape[1]), raw_rows.dtype)
    return shifted_conv(jnp.concatenate([padding, raw_rows], axis=0), weight)

def span_output(x_blk, b_blk, c_blk, dt_blk, cum_decay, skip_gain, states):
    length = x_blk.shape[1]
    causal = jnp.arange(length)[:, None] >= jnp.arange(length)[None, :]
    pair_inner = jnp.einsum('cqgn,csgn->cgqs', c_blk, b_blk, precision=PRECISE)
    cum_cols = jnp.transpose(cum_decay, (0, 2, 3, 1))
    spread = cum_cols[..., :, None] - cum_cols[..., None, :]
    weights = jnp.where(causal, jnp.exp(jnp.where(causal, spread, 0.0)), 0.0)
    dt_cols = jnp.transpose(dt_blk, (0, 2, 3, 1))
    weights = weights * pair_inner[:, None] * dt_cols[..., None, :]
    diagonal = jnp.einsum('crgqs,csrgp->cqrgp', weights, x_blk, precision=PRECISE)
    carried = jnp.einsum('cqgn,crgpn->cqrgp', c_blk, states, precision=PRECISE)
    carried = carried * jnp.exp(cum_decay)[..., None]
    return diagonal + carried + skip_gain[:, :, None] * x_blk

def span_state(x_blk, b_blk, dt_blk, cum_decay):
    weight_rows = jnp.exp(cum_decay[:, -1:] - cum_decay) * dt_blk
    weighted = weight_rows[..., None] * x_blk
    return jnp.einsum('cqrgp,cqgn->crgpn', weighted, b_blk, precision=PRECISE)

def forward(x_raw, b_raw, c_raw, z_gate, dt_raw, conv_x, conv_b, conv_c, dt_bias, a_log, d_skip, gain):
    length = x_raw.shape[0]
    per_group = HEADS // GROUPS
    blocks = length // SPAN
    x_act = causal_conv(x_raw, conv_x).reshape(blocks, SPAN, per_group, GROUPS, HEAD_DIM)
    b_act = causal_conv(b_raw, conv_b).reshape(blocks, SPAN, GROUPS, STATE)
    c_act = causal_conv(c_raw, conv_c).reshape(blocks, SPAN, GROUPS, STATE)
    step_dt = jax.nn.softplus(dt_raw + dt_bias).reshape(blocks, SPAN, per_group, GROUPS)
    decay_rate = jnp.exp(a_log).reshape(per_group, GROUPS)
    skip_gain = d_skip.reshape(per_group, GROUPS)

    def advance_plain(carry_state, pieces):
        x_blk = pieces[0][None]
        b_blk = pieces[1][None]
        c_blk = pieces[2][None]
        dt_blk = pieces[3][None]
        cum_decay = jnp.cumsum(-decay_rate * dt_blk, axis=1)
        output = span_output(x_blk, b_blk, c_blk, dt_blk, cum_decay, skip_gain, carry_state[None])
        own_state = span_state(x_blk, b_blk, dt_blk, cum_decay)[0]
        carry_state = jnp.exp(cum_decay[0, -1])[..., None, None] * carry_state + own_state
        return (carry_state, output[0])
    advance = jax.checkpoint(advance_plain)
    initial = jnp.zeros((per_group, GROUPS, HEAD_DIM, STATE), jnp.float32)
    finished, outputs = lax.scan(advance, initial, (x_act, b_act, c_act, step_dt))
    ssd_out = outputs.reshape(length, HEADS * HEAD_DIM)
    gated_out = ssd_out * jax.nn.silu(z_gate)
    grouped = gated_out.reshape(length, per_group, GROUPS, HEAD_DIM)
    mean_square = lax.optimization_barrier(jnp.mean(grouped * grouped, axis=(1, 3), keepdims=True))
    normed = (grouped * lax.rsqrt(mean_square + EPSILON)).reshape(length, HEADS * HEAD_DIM)
    return normed * gain

def reference(x_raw, b_raw, c_raw, z_gate, dt_raw, conv_x, conv_b, conv_c, dt_bias, a_log, d_skip, gain, grad_out):
    primals = (x_raw.astype(jnp.float32), b_raw.astype(jnp.float32), c_raw.astype(jnp.float32), z_gate.astype(jnp.float32), dt_raw, conv_x, conv_b, conv_c, dt_bias, a_log, d_skip, gain)
    normed, pullback = jax.vjp(forward, *primals)
    grads = pullback(grad_out.astype(jnp.float32))
    return (grads[0].astype(jnp.bfloat16), grads[1].astype(jnp.bfloat16), grads[2].astype(jnp.bfloat16), grads[3].astype(jnp.bfloat16), grads[4], grads[5], grads[6], grads[7], grads[8], grads[9], grads[10], grads[11])
```

```python
import jax
import jax.numpy as jnp
from jax import lax
from jax.experimental import pallas as pl
from jax.experimental.pallas import tpu as pltpu
from jax.sharding import PartitionSpec as P

HEADS = 128
HEAD_DIM = 32
STATE = 128
GROUPS = 4
CONV = 4
SPAN = 128


PRECISE = lax.Precision.HIGHEST
EPSILON = 1e-05


def from_behind(x, axis, by):
    peers = lax.axis_size(axis)
    pairs = [(i, i + by) for i in range(peers) if 0 <= i + by < peers]
    return lax.ppermute(x, axis, pairs)


def scan_kernel(backward, s_ref, d_ref, o_ref):
    count = s_ref.shape[0]
    carry = jnp.zeros(s_ref.shape[1:], jnp.float32)
    for step in range(count):
        at = count - 1 - step if backward else step
        o_ref[at] = carry
        carry = d_ref[at] * carry + s_ref[at]


def prefix(decay, state, axis, backward):
    count = lax.axis_size(axis)
    shape = state.shape
    own = state.reshape(count, -1, 128)
    owned = jnp.broadcast_to(
        jnp.repeat(decay.reshape(-1), count // decay.size)[:, None, None], (count, 1, 128)
    )
    pieces = lax.all_to_all(own, axis, 0, 0)
    decays = lax.all_to_all(owned, axis, 0, 0)
    entering = pl.pallas_call(
        lambda *refs: scan_kernel(backward, *refs),
        out_shape=jax.ShapeDtypeStruct(pieces.shape, jnp.float32),
        name="block_scan",
    )(pieces, decays)
    return lax.all_to_all(entering, axis, 0, 0).reshape(shape)


def butterfly(x, axis):
    peers = lax.axis_size(axis)
    by = 1
    while by < peers:
        x = x + lax.ppermute(x, axis, [(i, i ^ by) for i in range(peers)])
        by *= 2
    return x


def shifted_conv(extended, weight):
    tap_count = weight.shape[0]
    length = extended.shape[0] - tap_count + 1
    total = weight[0] * extended[0:length]
    for offset in range(1, tap_count):
        total = total + weight[offset] * extended[offset : offset + length]
    return jax.nn.silu(total)


def soft_step(raw_step, step_bias):
    return jax.nn.softplus(raw_step + step_bias)


def gate_product(ssd_out, gate_in):
    return ssd_out * jax.nn.silu(gate_in)


def span_output(x_blk, b_blk, c_blk, dt_blk, cum_decay, skip_gain, states):
    length = x_blk.shape[1]
    causal = jnp.arange(length)[:, None] >= jnp.arange(length)[None, :]
    pair_inner = jnp.einsum("cqgn,csgn->cgqs", c_blk, b_blk, precision=PRECISE)
    cum_cols = jnp.transpose(cum_decay, (0, 2, 3, 1))
    spread = cum_cols[..., :, None] - cum_cols[..., None, :]
    weights = jnp.where(causal, jnp.exp(jnp.where(causal, spread, 0.0)), 0.0)
    dt_cols = jnp.transpose(dt_blk, (0, 2, 3, 1))
    weights = weights * pair_inner[:, None] * dt_cols[..., None, :]
    diagonal = jnp.einsum("crgqs,csrgp->cqrgp", weights, x_blk, precision=PRECISE)
    carried = jnp.einsum("cqgn,crgpn->cqrgp", c_blk, states, precision=PRECISE)
    carried = carried * jnp.exp(cum_decay)[..., None]
    return diagonal + carried + skip_gain[:, :, None] * x_blk


def span_state(x_blk, b_blk, dt_blk, cum_decay):
    weight_rows = jnp.exp(cum_decay[:, -1:] - cum_decay) * dt_blk
    weighted = weight_rows[..., None] * x_blk
    return jnp.einsum("cqrgp,cqgn->crgpn", weighted, b_blk, precision=PRECISE)


def body(
    x_raw,
    b_raw,
    c_raw,
    z_gate,
    dt_raw,
    conv_x,
    conv_b,
    conv_c,
    dt_bias,
    a_log,
    d_skip,
    gain,
    grad_out,
):
    rows = x_raw.shape[0]
    halo_rows = CONV - 1
    per_local = x_raw.shape[1] // HEAD_DIM // GROUPS
    blocks_here = rows // SPAN
    group_width = HEADS // GROUPS * HEAD_DIM
    tails = (x_raw[rows - halo_rows :], b_raw[rows - halo_rows :], c_raw[rows - halo_rows :])
    before = from_behind((tails[0], tails[1], tails[2]), "ctx", 1)
    x_ext = jnp.concatenate([before[0], x_raw], axis=0).astype(jnp.float32)
    b_ext = jnp.concatenate([before[1], b_raw], axis=0).astype(jnp.float32)
    c_ext = jnp.concatenate([before[2], c_raw], axis=0).astype(jnp.float32)
    x_flat, x_conv_back = jax.vjp(shifted_conv, x_ext, conv_x)
    b_flat, b_conv_back = jax.vjp(shifted_conv, b_ext, conv_b)
    c_flat, c_conv_back = jax.vjp(shifted_conv, c_ext, conv_c)
    step_dt, step_back = jax.vjp(soft_step, dt_raw, dt_bias)

    def shaped(x_rows, b_rows, dt_rows, log_rate):
        x_blk = x_rows.reshape(blocks_here, SPAN, per_local, GROUPS, HEAD_DIM)
        b_blk = b_rows.reshape(blocks_here, SPAN, GROUPS, STATE)
        dt_blk = dt_rows.reshape(blocks_here, SPAN, per_local, GROUPS)
        decay_rate = jnp.exp(log_rate).reshape(per_local, GROUPS)
        lower = jnp.tril(jnp.ones((SPAN, SPAN), jnp.float32))
        cum_decay = jnp.einsum("qs,csrg->cqrg", lower, -decay_rate * dt_blk, precision=PRECISE)
        return (x_blk, b_blk, dt_blk, cum_decay)

    def summarize(x_rows, b_rows, dt_rows, log_rate):
        x_blk, b_blk, dt_blk, cum_decay = shaped(x_rows, b_rows, dt_rows, log_rate)
        own_states = span_state(x_blk, b_blk, dt_blk, cum_decay)
        block_ends = cum_decay[:, -1]

        def advance(carry_state, pieces):
            return (jnp.exp(pieces[0])[..., None, None] * carry_state + pieces[1], carry_state)

        initial = jnp.zeros(own_states.shape[1:], jnp.float32)
        finished, entering = lax.scan(advance, initial, (block_ends, own_states))
        return (entering, jnp.exp(jnp.sum(block_ends, axis=0)), finished)

    def produce(x_rows, b_rows, c_rows, dt_rows, log_rate, skip_rows, entering, enter_state):
        x_blk, b_blk, dt_blk, cum_decay = shaped(x_rows, b_rows, dt_rows, log_rate)
        c_blk = c_rows.reshape(blocks_here, SPAN, GROUPS, STATE)
        block_ends = cum_decay[:, -1]
        earlier = jnp.concatenate(
            [jnp.zeros_like(block_ends), jnp.cumsum(block_ends[:-1], axis=0)], axis=0
        )
        states = entering + jnp.exp(earlier)[..., None, None] * enter_state[None]
        skip_gain = skip_rows.reshape(per_local, GROUPS)
        result = span_output(x_blk, b_blk, c_blk, dt_blk, cum_decay, skip_gain, states)
        return result.reshape(rows, per_local * GROUPS * HEAD_DIM)

    def group_sums(values):
        return jnp.sum(values.reshape(rows, per_local, GROUPS, HEAD_DIM), axis=(1, 3))

    def spread_groups(values):
        return jnp.broadcast_to(
            values[:, None, :, None], (rows, per_local, GROUPS, HEAD_DIM)
        ).reshape(rows, -1)

    (entering, dev_decay, dev_state), summary_back = jax.vjp(
        summarize, x_flat, b_flat, step_dt, a_log
    )
    enter_state = prefix(dev_decay, dev_state, "ctx", False)
    ssd_out, produce_back = jax.vjp(
        produce, x_flat, b_flat, c_flat, step_dt, a_log, d_skip, entering, enter_state
    )
    gated_out, gate_back = jax.vjp(gate_product, ssd_out, z_gate.astype(jnp.float32))
    square_sums = lax.psum(group_sums(gated_out * gated_out), "tp")
    inverse = lax.rsqrt(square_sums / group_width + EPSILON)
    inverse_cols = spread_groups(inverse)
    out_grad = grad_out.astype(jnp.float32)
    gain_part = jnp.sum(out_grad * gated_out * inverse_cols, axis=0)
    scaled_grad = out_grad * gain
    inner_total = lax.psum(group_sums(scaled_grad * gated_out), "tp")
    correction = spread_groups(inverse * inverse * inverse * inner_total / group_width)
    gated_grad = inverse_cols * scaled_grad - gated_out * correction
    ssd_grad, gate_grad = gate_back(gated_grad)
    (
        x_grad_one,
        b_grad_one,
        c_grad_part,
        step_grad_one,
        rate_grad_one,
        skip_grad,
        entering_grad,
        state_grad,
    ) = produce_back(ssd_grad)
    later_grad = prefix(dev_decay, state_grad, "ctx", True)
    decay_grad = jnp.sum(later_grad * enter_state, axis=(2, 3))
    x_grad_two, b_grad_two, step_grad_two, rate_grad_two = summary_back(
        (entering_grad, decay_grad, later_grad)
    )
    rate_grad = rate_grad_one + rate_grad_two
    raw_step_grad, bias_grad = step_back(step_grad_one + step_grad_two)
    b_grad, c_grad = (b_grad_one + b_grad_two, c_grad_part)
    x_ext_grad, weight_x_grad = x_conv_back(x_grad_one + x_grad_two)
    b_ext_grad, weight_b_grad = b_conv_back(b_grad)
    c_ext_grad, weight_c_grad = c_conv_back(c_grad)
    returned = from_behind(
        (x_ext_grad[:halo_rows], b_ext_grad[:halo_rows], c_ext_grad[:halo_rows]), "ctx", -1
    )

    def settle(ext_grad, incoming):
        own_rows = ext_grad[halo_rows:]
        return jnp.concatenate(
            [own_rows[: rows - halo_rows], own_rows[rows - halo_rows :] + incoming], axis=0
        )

    grad_x_raw = settle(x_ext_grad, returned[0]).astype(jnp.bfloat16)
    bc_part = jnp.concatenate([settle(b_ext_grad, returned[1]), settle(c_ext_grad, returned[2])], axis=0)
    slices = jnp.stack(jnp.split(bc_part, GROUPS, axis=1))
    mine = jnp.sum(lax.all_to_all(slices, "tp", 0, 0), axis=0).astype(jnp.bfloat16)
    spread = lax.all_to_all(jnp.broadcast_to(mine, slices.shape), "tp", 0, 0)
    bc_grad = jnp.concatenate([spread[g] for g in range(GROUPS)], axis=1)
    grad_b_raw, grad_c_raw = bc_grad[:rows], bc_grad[rows:]
    parts = (weight_b_grad, weight_c_grad, weight_x_grad, gain_part, bias_grad, rate_grad, skip_grad)
    packed = jnp.concatenate([part.reshape(-1) for part in parts])
    packed = butterfly(jnp.pad(packed, (0, -packed.size % 1024)).reshape(-1, 128), "ctx")
    shared = 2 * CONV * GROUPS * STATE // 128
    packed = jnp.concatenate([butterfly(packed[:shared], "tp").reshape(-1), packed[shared:].reshape(-1)])
    totals, start = [], 0
    for part in parts:
        totals.append(packed[start : start + part.size].reshape(part.shape))
        start += part.size
    conv_b_total, conv_c_total, conv_x_total, gain_total, bias_total, rate_total, skip_total = totals
    return (
        grad_x_raw,
        grad_b_raw,
        grad_c_raw,
        gate_grad.astype(jnp.bfloat16),
        raw_step_grad,
        conv_x_total,
        conv_b_total,
        conv_c_total,
        bias_total,
        rate_total,
        skip_total,
        gain_total,
    )


def solution(mesh):
    return jax.shard_map(
        body,
        mesh=mesh,
        in_specs=(
            P("ctx", "tp"),
            P("ctx", None),
            P("ctx", None),
            P("ctx", "tp"),
            P("ctx", "tp"),
            P(None, "tp"),
            P(),
            P(),
            P("tp"),
            P("tp"),
            P("tp"),
            P("tp"),
            P("ctx", "tp"),
        ),
        out_specs=(
            P("ctx", "tp"),
            P("ctx", None),
            P("ctx", None),
            P("ctx", "tp"),
            P("ctx", "tp"),
            P(None, "tp"),
            P(),
            P(),
            P("tp"),
            P("tp"),
            P("tp"),
            P("tp"),
        ),
        check_vma=False,
    )
```

```python
import functools

import jax
import jax.numpy as jnp
from jax import lax
from jax.experimental import pallas as pl
from jax.experimental.pallas import tpu as pltpu
from jax.sharding import PartitionSpec as P

HEAD_DIM = 32
STATE = 128
GROUPS = 4
CONV = 4
SPAN = 128
TILE = 128
PER = 8
LOCAL = PER * GROUPS
ROWS = PER * HEAD_DIM
ALL = LOCAL * HEAD_DIM
HALF = ALL // 2
CHUNK = 2048
LEAD = 16
GROUP_WIDTH = 1024
EPSILON = 1e-05
F32 = jnp.float32
PARAMS = pltpu.CompilerParams(vmem_limit_bytes=48 << 20)


def dot(a, b, ca=1, cb=0):
    return lax.dot_general(
        a, b, (((ca,), (cb,)), ((), ())), precision=lax.Precision.HIGHEST, preferred_element_type=F32
    )


def group(g):
    return slice(g * ROWS, (g + 1) * ROWS)


def lanes(r):
    return slice(r * TILE, (r + 1) * TILE)


def spot(g, r):
    return slice(g * ROWS + r * HEAD_DIM, g * ROWS + (r + 1) * HEAD_DIM)


def put(dst, r, tile):
    turned = tile.T
    for g in range(GROUPS):
        dst[spot(g, r), :] = turned[g * HEAD_DIM : (g + 1) * HEAD_DIM]


def take(values, r):
    rows = slice(r * HEAD_DIM, (r + 1) * HEAD_DIM)
    return jnp.concatenate([v[rows] for v in values], axis=0).T


def heads_out(v, g):
    return jnp.concatenate(
        [jnp.broadcast_to(v[g * PER + r : g * PER + r + 1], (HEAD_DIM, v.shape[1])) for r in range(PER)], axis=0
    )


def heads_in(v):
    return jnp.concatenate(
        [jnp.sum(v[r * HEAD_DIM : (r + 1) * HEAD_DIM], axis=0, keepdims=True) for r in range(PER)], axis=0
    )


def sigmoid(v):
    return 1.0 / (1.0 + jnp.exp(-v))


def silu_slope(v):
    s = sigmoid(v)
    return s * (1.0 + v * (1.0 - s))


def extend(ext, raw, before):
    ext[0:LEAD, :] = before[...].astype(F32)
    ext[LEAD : LEAD + SPAN, :] = raw[...].astype(F32)


def conv_tile(ext, w, cols):
    total = w[0:1, cols] * ext[LEAD - 3 : LEAD - 3 + SPAN, cols]
    for k in range(1, CONV):
        total = total + w[k : k + 1, cols] * ext[LEAD - 3 + k : LEAD - 3 + k + SPAN, cols]
    return total


def conv_back_tile(ext, pad, w, cols, grad, own, head, wgrad):
    dpre = grad * silu_slope(conv_tile(ext, w, cols))
    pad[8 : 8 + SPAN, cols] = dpre
    for k in range(CONV):
        wgrad[k : k + 1, cols] = jnp.sum(
            dpre * ext[LEAD - 3 + k : LEAD - 3 + k + SPAN, cols], axis=0, keepdims=True
        )
    mine = w[0:1, cols] * pad[11 : 11 + SPAN, cols]
    ahead = w[0:1, cols] * pad[3:11, cols]
    for k in range(1, CONV):
        mine = mine + w[k : k + 1, cols] * pad[11 - k : 11 - k + SPAN, cols]
        ahead = ahead + w[k : k + 1, cols] * pad[3 - k : 11 - k, cols]
    own[:, cols] = mine
    head[:, cols] = ahead


def clear_pad(pad):
    pad[0:8, :] = jnp.zeros((8, pad.shape[1]), F32)
    pad[8 + SPAN : 16 + SPAN, :] = jnp.zeros((8, pad.shape[1]), F32)


def halves(core, full, keep, give):
    keep[...] = full[pl.ds(pl.multiple_of(core * HALF, HALF), HALF), :]
    give[0:HALF, :] = full[pl.ds(pl.multiple_of((1 - core) * HALF, HALF), HALF), :]


def unite(core, full, own, got):
    full[pl.ds(pl.multiple_of(core * HALF, HALF), HALF), :] = own[...]
    full[pl.ds(pl.multiple_of((1 - core) * HALF, HALF), HALF), :] = got[...]


def triangle(upper):
    rows = lax.broadcasted_iota(jnp.int32, (SPAN, SPAN), 0)
    cols = lax.broadcasted_iota(jnp.int32, (SPAN, SPAN), 1)
    return rows <= cols if upper else rows >= cols


def steps_kernel(dt, bias, alog, step, cum, ends):
    v = dt[...] + bias[...]
    step[...] = jnp.maximum(v, 0.0) + jnp.log1p(jnp.exp(-jnp.abs(v)))
    rates = -jnp.exp(alog[...]) * step[...]
    cum[...] = dot(rates, jnp.where(triangle(True), 1.0, 0.0))
    ends[...] = jnp.broadcast_to(jnp.exp(jnp.sum(rates, axis=1, keepdims=True)), ends.shape)


def turn_kernel(z, og, gain, zt, ogt, sgt):
    for r in range(PER):
        put(zt, r, z[:, lanes(r)].astype(F32))
        tile = og[:, lanes(r)].astype(F32)
        put(ogt, r, tile)
        put(sgt, r, tile * gain[:, lanes(r)])


def state_kernel(core, x, hx, b, hb, wx, wb, step, cum, ends, xt, zs, bc, keep, give, ext, extb, full):
    extend(ext, x, hx)
    extend(extb, b, hb)
    for g in range(GROUPS):
        pre = conv_tile(extb, wb, lanes(g))
        bc[:, lanes(g)] = pre * sigmoid(pre)
    for r in range(PER):
        pre = conv_tile(ext, wx, lanes(r))
        put(xt, r, pre * sigmoid(pre))
    scale = jnp.exp(-cum[...]) * step[...]
    for g in range(GROUPS):
        zg = xt[group(g), :] * heads_out(scale, g)
        zs[group(g), :] = zg
        full[group(g), :] = heads_out(ends[...], g) * dot(zg, bc[:, lanes(g)])
    halves(core[0], full, keep, give)
    give[HALF : HALF + LOCAL, :] = ends[...]


def local_kernel(c, hc, wc, bc, xt, zs, cum, skip, cc, mt, y, extc):
    extend(extc, c, hc)
    alpha = jnp.exp(cum[...])
    causal = triangle(True)
    for g in range(GROUPS):
        pre = conv_tile(extc, wc, lanes(g))
        cg = pre * sigmoid(pre)
        cc[:, lanes(g)] = cg
        m = jnp.where(causal, dot(bc[:, lanes(g)], cg, 1, 1), 0.0)
        mt[lanes(g), :] = m
        y[group(g), :] = heads_out(alpha, g) * dot(zs[group(g), :], m) + heads_out(skip[...], g) * xt[group(g), :]


def output_kernel(core, own, got, cc, y1, cum, zt, sgt, full, y, sums):
    unite(core[0], full, own, got)
    alpha = jnp.exp(cum[...])
    for g in range(GROUPS):
        yg = y1[group(g), :] + heads_out(alpha, g) * dot(full[group(g), :], cc[:, lanes(g)], 1, 1)
        y[group(g), :] = yg
        z = zt[group(g), :]
        gated = yg * z * sigmoid(z)
        sums[g : g + 1, :] = jnp.sum(gated * gated, axis=0, keepdims=True)
        sums[GROUPS + g : GROUPS + g + 1, :] = jnp.sum(sgt[group(g), :] * gated, axis=0, keepdims=True)


def gate_kernel(core, sums, y, zt, sgt, cum, cc, keep, give, dy, dg, full):
    alpha = jnp.exp(cum[...])
    for g in range(GROUPS):
        inv = lax.rsqrt(sums[g : g + 1, :] / GROUP_WIDTH + EPSILON)
        fix = inv * inv * inv * sums[GROUPS + g : GROUPS + g + 1, :] / GROUP_WIDTH
        z = zt[group(g), :]
        act = z * sigmoid(z)
        dgated = inv * sgt[group(g), :] - y[group(g), :] * act * fix
        dg[group(g), :] = dgated
        dyg = dgated * act
        dy[group(g), :] = dyg
        full[group(g), :] = dot(heads_out(alpha, g) * dyg, cc[:, lanes(g)])
    halves(core[0], full, keep, give)


def middle_kernel(
    sums, y, zt, ogt, dy, dg, full, mt, zs, xt, bc, cc, cum, skip, c, hc, wc,
    dz, db, dcum, dskip, gz, dgain, cown, chead, wcg, extc, padc, dc,
):
    alpha = jnp.exp(cum[...])
    causal = triangle(True)
    slope, shares = [], []
    for g in range(GROUPS):
        z, yg, dyg = zt[group(g), :], y[group(g), :], dy[group(g), :]
        inv = lax.rsqrt(sums[g : g + 1, :] / GROUP_WIDTH + EPSILON)
        slope.append(dg[group(g), :] * yg * silu_slope(z))
        shares.append(ogt[group(g), :] * yg * z * sigmoid(z) * inv)
        heads = slice(g * PER, (g + 1) * PER)
        x = xt[group(g), :]
        passed = heads_in(dyg * x)
        dskip[heads, :] = passed
        dcum[heads, :] = heads_in(dyg * (yg - heads_out(skip[...], g) * x))
        u = heads_out(alpha, g) * dyg
        dz[group(g), :] = dot(u, mt[lanes(g), :], 1, 1)
        dm = jnp.where(causal, dot(zs[group(g), :], u, 0, 0), 0.0)
        dc[:, lanes(g)] = dot(dm, bc[:, lanes(g)], 0, 0) + dot(u, full[group(g), :], 0, 0)
        db[:, lanes(g)] = dot(dm, cc[:, lanes(g)])
    for r in range(PER):
        gz[:, lanes(r)] = take(slope, r).astype(jnp.bfloat16)
        dgain[:, lanes(r)] = jnp.sum(take(shares, r), axis=0, keepdims=True)
    extend(extc, c, hc)
    clear_pad(padc)
    for g in range(GROUPS):
        conv_back_tile(extc, padc, wc, lanes(g), dc[:, lanes(g)], cown, chead, wcg)


def last_kernel(
    core, own, got, full, ends, dz1, db1, dcum1, dy, zs, xt, bc, cum, step, skip, dt, bias, alog, x, hx, wx, b, hb, wb,
    xown, xhead, wxg, bown, bhead, wbg, ddt, drate, later, ext, extb, pad, padb,
):
    unite(core[0], later, own, got)
    gamma = jnp.exp(-cum[...])
    scale = gamma * step[...]
    clear_pad(pad)
    clear_pad(padb)
    extend(ext, x, hx)
    extend(extb, b, hb)
    dxs, turned, straight = [], [], []
    at_end = lax.broadcasted_iota(jnp.int32, (PER, SPAN), 1) == SPAN - 1
    for g in range(GROUPS):
        heads = slice(g * PER, (g + 1) * PER)
        zg, xg = zs[group(g), :], xt[group(g), :]
        d = heads_out(ends[...], g) * later[group(g), :]
        second = dot(d, bc[:, lanes(g)], 1, 1)
        dzg = dz1[group(g), :] + second
        dxs.append(heads_out(scale, g) * dzg + heads_out(skip[...], g) * dy[group(g), :])
        edge = heads_in(zg * second + d * full[group(g), :])
        edge = jnp.sum(edge, axis=1, keepdims=True)
        turned.append(dcum1[heads, :] - heads_in(dzg * zg) + jnp.where(at_end, edge, 0.0))
        straight.append(heads_in(dzg * xg))
        dbg = db1[:, lanes(g)] + dot(zg, d, 0, 0)
        conv_back_tile(extb, padb, wb, lanes(g), dbg, bown, bhead, wbg)
    dlog = dot(jnp.concatenate(turned, axis=0), jnp.where(triangle(False), 1.0, 0.0))
    rate = -jnp.exp(alog[...])
    drate[...] = dlog * rate * step[...]
    dstep = jnp.concatenate(straight, axis=0) * gamma + dlog * rate
    ddt[...] = dstep * sigmoid(dt[...] + bias[...])
    for r in range(PER):
        conv_back_tile(ext, pad, wx, lanes(r), take(dxs, r), xown, xhead, wxg)


def scan_kernel(backward, s, d, o):
    count = s.shape[0]
    at = d.shape[2] - TILE
    carry = [jnp.zeros((1, TILE), F32)] * (CHUNK // TILE)
    for j in range(count):
        j = count - 1 - j if backward else j
        decay = d[j, :, at:]
        for k in range(CHUNK // TILE):
            o[j, :, lanes(k)] = carry[k]
            carry[k] = decay * carry[k] + s[j, :, lanes(k)]


def call(kernel, name, outs, args, scratch=(), scalars=0, flops=20_000_000):
    smem = pl.BlockSpec(memory_space=pltpu.SMEM)
    vmem = pl.BlockSpec(memory_space=pltpu.VMEM)
    return pl.pallas_call(
        kernel,
        out_shape=[jax.ShapeDtypeStruct(s, d) for s, d in outs],
        in_specs=[smem if i < scalars else vmem for i in range(len(args))],
        out_specs=[vmem] * len(outs),
        scratch_shapes=[pltpu.VMEM(s, F32) for s in scratch],
        compiler_params=PARAMS,
        cost_estimate=pl.CostEstimate(flops=flops, bytes_accessed=4 << 20, transcendentals=1 << 18),
        name=name,
    )(*args)


def swap_cores(v):
    return lax.ppermute(v, "ctx", [(i, i ^ 1) for i in range(lax.axis_size("ctx"))])


def alike(size, by):
    return [(i, i ^ by) for i in range(size)]


def over_chips(v):
    size = lax.axis_size("ctx")
    return lax.all_to_all(
        v, "ctx", 0, 0, axis_index_groups=[list(range(c, size, 2)) for c in range(2)]
    )


def wide(a):
    return jnp.repeat(a, HEAD_DIM, axis=0)


def pair_scan(keep, got, first, second, is_first, decays, backward):
    lead = jnp.where(is_first, keep, got)
    follow = jnp.where(is_first, got, keep)
    joint = (wide(second) * lead + follow).reshape(-1, 1, CHUNK)
    if decays is None:
        both = jnp.repeat(first * second, HALF // (LOCAL // 2) * STATE // CHUNK, axis=0)[:, None]
        joint = jnp.concatenate([joint, both], axis=2)
    pieces = over_chips(joint)
    decays = pieces if decays is None else decays
    (entering,) = call(
        functools.partial(scan_kernel, backward),
        "block_scan",
        [((pieces.shape[0], 1, CHUNK), F32)],
        (pieces, decays),
    )
    ahead = over_chips(entering).reshape(HALF, STATE)
    between = wide(first) * ahead + lead
    other = swap_cores(jnp.where(is_first, between, ahead))
    return jnp.where(is_first, ahead, between), other, decays


def butterfly(x, axis):
    by = 1
    while by < lax.axis_size(axis):
        x = x + lax.ppermute(x, axis, alike(lax.axis_size(axis), by))
        by *= 2
    return x


def by_group(v):
    return v.reshape((PER, GROUPS) + v.shape[1:]).swapaxes(0, 1).reshape(v.shape)


def by_head(v):
    return v.reshape((GROUPS, PER) + v.shape[1:]).swapaxes(0, 1).reshape(v.shape)


def body(
    x_raw, b_raw, c_raw, z_gate, dt_raw, conv_x, conv_b, conv_c, dt_bias, a_log, d_skip, gain, grad_out
):
    size = lax.axis_size("ctx")
    core = lax.axis_index("ctx") % 2
    cores = core.reshape(1)
    is_even = core == 0
    t_shape = ((ALL, SPAN), F32)
    bc_shape = ((SPAN, GROUPS * STATE), F32)
    h_shape = ((LOCAL, SPAN), F32)
    tails = jnp.concatenate([v[SPAN - LEAD :] for v in (x_raw, b_raw, c_raw)], axis=1)
    before = lax.ppermute(tails, "ctx", [(i, i + 1) for i in range(size - 1)])
    wx, wb = x_raw.shape[1], b_raw.shape[1]
    hx, hb, hc = before[:, :wx], before[:, wx : wx + wb], before[:, wx + wb :]

    dt = by_group(dt_raw.T)
    bias, alog, skip_col = (by_group(v)[:, None] for v in (dt_bias, a_log, d_skip))
    skip = jnp.broadcast_to(skip_col, h_shape[0])
    step, cum, ends = call(steps_kernel, "steps", [h_shape] * 3, (dt, bias, alog))
    zt, ogt, sgt = call(turn_kernel, "turn", [t_shape] * 3, (z_gate, grad_out, gain[None]))
    xt, zs, bc, keep, give = call(
        state_kernel,
        "state",
        [t_shape, t_shape, bc_shape, ((HALF, STATE), F32), ((HALF + LOCAL, STATE), F32)],
        (cores, x_raw, hx, b_raw, hb, conv_x, conv_b, step, cum, ends),
        [(LEAD + SPAN, wx), (LEAD + SPAN, wb), (ALL, STATE)],
        scalars=1,
    )
    got = swap_cores(give)
    mine = lax.dynamic_slice_in_dim(ends, core * (LOCAL // 2), LOCAL // 2)
    theirs = lax.dynamic_slice_in_dim(got[HALF:], core * (LOCAL // 2), LOCAL // 2)
    even, odd = jnp.where(is_even, mine, theirs), jnp.where(is_even, theirs, mine)
    enter_own, enter_got, decays = pair_scan(keep, got[:HALF], even, odd, is_even, None, False)

    cc, mt, y1 = call(
        local_kernel,
        "local",
        [bc_shape, ((GROUPS * SPAN, SPAN), F32), t_shape],
        (c_raw, hc, conv_c, bc, xt, zs, cum, skip),
        [(LEAD + SPAN, wb)],
    )
    enter, y, sums = call(
        output_kernel,
        "output",
        [t_shape, t_shape, ((2 * GROUPS, SPAN), F32)],
        (cores, enter_own, enter_got, cc, y1, cum, zt, sgt),
        scalars=1,
    )
    sums = butterfly(sums, "tp")
    keep, give, dy, dg = call(
        gate_kernel,
        "gate",
        [((HALF, STATE), F32)] * 2 + [t_shape, t_shape],
        (cores, sums, y, zt, sgt, cum, cc),
        [(ALL, STATE)],
        scalars=1,
    )
    got = swap_cores(give)
    later_own, later_got, _ = pair_scan(keep, got, odd, even, ~is_even, decays, True)
    own_shape, head_shape, w_shape = bc_shape, ((8, wb), F32), ((CONV, wb), F32)
    dz, db, dcum, dskip, grad_z, dgain, cown, chead, wcg = call(
        middle_kernel,
        "middle",
        [t_shape, bc_shape, h_shape, h_shape, ((SPAN, wx), jnp.bfloat16), ((1, wx), F32)]
        + [own_shape, head_shape, w_shape],
        (sums, y, zt, ogt, dy, dg, enter, mt, zs, xt, bc, cc, cum, skip, c_raw, hc, conv_c),
        [(LEAD + SPAN, wb), (LEAD + SPAN, wb), (SPAN, wb)],
    )
    xown, xhead, wxg, bown, bhead, wbg, ddt, drate = call(
        last_kernel,
        "last",
        [((SPAN, wx), F32), ((8, wx), F32), ((CONV, wx), F32), own_shape, head_shape, w_shape, h_shape, h_shape],
        (cores, later_own, later_got, enter, ends, dz, db, dcum, dy, zs, xt, bc, cum, step, skip, dt, bias, alog)
        + (x_raw, hx, conv_x, b_raw, hb, conv_b),
        [(ALL, STATE), (LEAD + SPAN, wx), (LEAD + SPAN, wb), (LEAD + SPAN, wx), (LEAD + SPAN, wb)],
        scalars=1,
    )
    heads = jnp.concatenate([xhead, bhead, chead], axis=1)
    heads = lax.ppermute(heads, "ctx", [(i + 1, i) for i in range(size - 1)])

    def settle(own, incoming):
        return jnp.concatenate([own[: SPAN - 8], own[SPAN - 8 :] + incoming], axis=0)

    grad_x_raw = settle(xown, heads[:, :wx]).astype(jnp.bfloat16)
    bc_part = jnp.concatenate(
        [settle(bown, heads[:, wx : wx + wb]), settle(cown, heads[:, wx + wb :])], axis=0
    )
    slices = jnp.stack(jnp.split(bc_part, GROUPS, axis=1))
    mine = jnp.sum(lax.all_to_all(slices, "tp", 0, 0), axis=0).astype(jnp.bfloat16)
    spread = lax.all_to_all(jnp.broadcast_to(mine, slices.shape), "tp", 0, 0)
    bc_grad = jnp.concatenate([spread[g] for g in range(GROUPS)], axis=1)
    grad_b_raw, grad_c_raw = bc_grad[:SPAN], bc_grad[SPAN:]
    small = by_head(jnp.stack([jnp.sum(v, axis=1) for v in (ddt, drate, dskip)], axis=1))
    parts = (wbg, wcg, wxg, dgain, small)
    packed = jnp.concatenate([part.reshape(-1) for part in parts])
    packed = butterfly(jnp.pad(packed, (0, -packed.size % 1024)).reshape(-1, TILE), "ctx")
    shared = (wbg.size + wcg.size) // TILE
    packed = jnp.concatenate([butterfly(packed[:shared], "tp").reshape(-1), packed[shared:].reshape(-1)])
    totals, start = [], 0
    for part in parts:
        totals.append(packed[start : start + part.size].reshape(part.shape))
        start += part.size
    conv_b_total, conv_c_total, conv_x_total, gain_total, small = totals
    return (
        grad_x_raw,
        grad_b_raw,
        grad_c_raw,
        grad_z,
        by_head(ddt).T,
        conv_x_total,
        conv_b_total,
        conv_c_total,
        small[:, 0],
        small[:, 1],
        small[:, 2],
        gain_total.reshape(-1),
    )


def solution(mesh):
    rows, cols, some = P("ctx", "tp"), P(None, "tp"), P("tp")
    return jax.shard_map(
        body,
        mesh=mesh,
        in_specs=(rows, P("ctx", None), P("ctx", None), rows, rows, cols, P(), P(), some, some, some, some, rows),
        out_specs=(rows, P("ctx", None), P("ctx", None), rows, rows, cols, P(), P(), some, some, some, some),
        check_vma=False,
    )
```

```python
import functools

import jax
import jax.numpy as jnp
from jax import lax
from jax.experimental import pallas as pl
from jax.experimental.pallas import tpu as pltpu
from jax.sharding import Mesh, PartitionSpec as P

HEAD_DIM = 32
STATE = 128
GROUPS = 4
CONV = 4
SPAN = 128
TILE = 128
PER = 8
LOCAL = PER * GROUPS
ROWS = PER * HEAD_DIM
ALL = LOCAL * HEAD_DIM
HALF = ALL // 2
CHUNK = 2048
LEAD = 16
GROUP_WIDTH = 1024
EPSILON = 1e-05
F32 = jnp.float32
CTX = ("chip", "core")
PARAMS = pltpu.CompilerParams(vmem_limit_bytes=16 << 20)


def dot(a, b, ca=1, cb=0):
    return lax.dot_general(
        a, b, (((ca,), (cb,)), ((), ())), precision=lax.Precision.HIGHEST, preferred_element_type=F32
    )


def group(g):
    return slice(g * ROWS, (g + 1) * ROWS)


def lanes(r):
    return slice(r * TILE, (r + 1) * TILE)


def spot(g, r):
    return slice(g * ROWS + r * HEAD_DIM, g * ROWS + (r + 1) * HEAD_DIM)


def put(dst, r, tile):
    turned = tile.T
    for g in range(GROUPS):
        dst[spot(g, r), :] = turned[g * HEAD_DIM : (g + 1) * HEAD_DIM]


def take(values, r):
    rows = slice(r * HEAD_DIM, (r + 1) * HEAD_DIM)
    return jnp.concatenate([v[rows] for v in values], axis=0).T


def heads_out(v, g):
    return jnp.concatenate(
        [jnp.broadcast_to(v[g * PER + r : g * PER + r + 1], (HEAD_DIM, v.shape[1])) for r in range(PER)], axis=0
    )


def heads_in(v):
    return jnp.concatenate(
        [jnp.sum(v[r * HEAD_DIM : (r + 1) * HEAD_DIM], axis=0, keepdims=True) for r in range(PER)], axis=0
    )


def sigmoid(v):
    return 1.0 / (1.0 + jnp.exp(-v))


def silu_slope(v):
    s = sigmoid(v)
    return s * (1.0 + v * (1.0 - s))


def extend(ext, raw, before):
    ext[0:LEAD, :] = before[...].astype(F32)
    ext[LEAD : LEAD + SPAN, :] = raw[...].astype(F32)


def conv_tile(ext, w, cols):
    total = w[0:1, cols] * ext[LEAD - 3 : LEAD - 3 + SPAN, cols]
    for k in range(1, CONV):
        total = total + w[k : k + 1, cols] * ext[LEAD - 3 + k : LEAD - 3 + k + SPAN, cols]
    return total


def conv_back_tile(ext, pad, w, cols, grad):
    dpre = grad * silu_slope(conv_tile(ext, w, cols))
    pad[8 : 8 + SPAN, cols] = dpre
    taps = [
        jnp.sum(dpre * ext[LEAD - 3 + k : LEAD - 3 + k + SPAN, cols], axis=0, keepdims=True) for k in range(CONV)
    ]
    mine = w[0:1, cols] * pad[11 : 11 + SPAN, cols]
    ahead = w[0:1, cols] * pad[3:11, cols]
    for k in range(1, CONV):
        mine = mine + w[k : k + 1, cols] * pad[11 - k : 11 - k + SPAN, cols]
        ahead = ahead + w[k : k + 1, cols] * pad[3 - k : 11 - k, cols]
    return mine, ahead, taps


def clear_pad(pad):
    pad[0:8, :] = jnp.zeros((8, pad.shape[1]), F32)
    pad[8 + SPAN : 16 + SPAN, :] = jnp.zeros((8, pad.shape[1]), F32)


def halves(core, full, keep, give):
    keep[...] = full[pl.ds(pl.multiple_of(core * HALF, HALF), HALF), :]
    give[0:HALF, :] = full[pl.ds(pl.multiple_of((1 - core) * HALF, HALF), HALF), :]


def unite(core, full, own, got):
    full[pl.ds(pl.multiple_of(core * HALF, HALF), HALF), :] = own[...]
    full[pl.ds(pl.multiple_of((1 - core) * HALF, HALF), HALF), :] = got[...]


def triangle(upper):
    rows = lax.broadcasted_iota(jnp.int32, (SPAN, SPAN), 0)
    cols = lax.broadcasted_iota(jnp.int32, (SPAN, SPAN), 1)
    return rows <= cols if upper else rows >= cols


def steps_kernel(dt, bias, alog, step, cum, ends):
    v = dt[...] + bias[...]
    step[...] = jnp.maximum(v, 0.0) + jnp.log1p(jnp.exp(-jnp.abs(v)))
    rates = -jnp.exp(alog[...]) * step[...]
    cum[...] = dot(rates, jnp.where(triangle(True), 1.0, 0.0))
    ends[...] = jnp.broadcast_to(jnp.exp(jnp.sum(rates, axis=1, keepdims=True)), ends.shape)


def turn_kernel(z, og, gain, zt, ogt, sgt):
    for r in range(PER):
        put(zt, r, z[:, lanes(r)].astype(F32))
        tile = og[:, lanes(r)].astype(F32)
        put(ogt, r, tile)
        put(sgt, r, tile * gain[:, lanes(r)])


def state_kernel(core, x, hx, b, hb, wx, wb, step, cum, ends, xt, zs, bc, keep, give, ext, extb, full):
    extend(ext, x, hx)
    extend(extb, b, hb)
    for g in range(GROUPS):
        pre = conv_tile(extb, wb, lanes(g))
        bc[:, lanes(g)] = pre * sigmoid(pre)
    for r in range(PER):
        pre = conv_tile(ext, wx, lanes(r))
        put(xt, r, pre * sigmoid(pre))
    scale = jnp.exp(-cum[...]) * step[...]
    for g in range(GROUPS):
        zg = xt[group(g), :] * heads_out(scale, g)
        zs[group(g), :] = zg
        full[group(g), :] = heads_out(ends[...], g) * dot(zg, bc[:, lanes(g)])
    halves(core[0], full, keep, give)
    give[HALF : HALF + LOCAL, :] = ends[...]


def local_kernel(c, hc, wc, bc, xt, zs, cum, skip, cc, mt, y, extc):
    extend(extc, c, hc)
    alpha = jnp.exp(cum[...])
    causal = triangle(True)
    for g in range(GROUPS):
        pre = conv_tile(extc, wc, lanes(g))
        cg = pre * sigmoid(pre)
        cc[:, lanes(g)] = cg
        m = jnp.where(causal, dot(bc[:, lanes(g)], cg, 1, 1), 0.0)
        mt[lanes(g), :] = m
        y[group(g), :] = heads_out(alpha, g) * dot(zs[group(g), :], m) + heads_out(skip[...], g) * xt[group(g), :]


def output_kernel(core, own, got, cc, y1, cum, zt, sgt, full, y, sums):
    unite(core[0], full, own, got)
    alpha = jnp.exp(cum[...])
    for g in range(GROUPS):
        yg = y1[group(g), :] + heads_out(alpha, g) * dot(full[group(g), :], cc[:, lanes(g)], 1, 1)
        y[group(g), :] = yg
        z = zt[group(g), :]
        gated = yg * z * sigmoid(z)
        sums[g : g + 1, :] = jnp.sum(gated * gated, axis=0, keepdims=True)
        sums[GROUPS + g : GROUPS + g + 1, :] = jnp.sum(sgt[group(g), :] * gated, axis=0, keepdims=True)


def gate_kernel(core, sums, y, zt, sgt, cum, cc, keep, give, dy, dg, full):
    alpha = jnp.exp(cum[...])
    for g in range(GROUPS):
        inv = lax.rsqrt(sums[g : g + 1, :] / GROUP_WIDTH + EPSILON)
        fix = inv * inv * inv * sums[GROUPS + g : GROUPS + g + 1, :] / GROUP_WIDTH
        z = zt[group(g), :]
        act = z * sigmoid(z)
        dgated = inv * sgt[group(g), :] - y[group(g), :] * act * fix
        dg[group(g), :] = dgated
        dyg = dgated * act
        dy[group(g), :] = dyg
        full[group(g), :] = dot(heads_out(alpha, g) * dyg, cc[:, lanes(g)])
    halves(core[0], full, keep, give)


def middle_kernel(
    sums, y, zt, ogt, dy, dg, full, mt, zs, xt, bc, cc, cum, skip, c, hc, wc,
    dz, db, dcum, dskip, gz, early, cpart, extc, padc, dc,
):
    alpha = jnp.exp(cum[...])
    causal = triangle(True)
    slope, shares = [], []
    for g in range(GROUPS):
        z, yg, dyg = zt[group(g), :], y[group(g), :], dy[group(g), :]
        inv = lax.rsqrt(sums[g : g + 1, :] / GROUP_WIDTH + EPSILON)
        slope.append(dg[group(g), :] * yg * silu_slope(z))
        shares.append(ogt[group(g), :] * yg * z * sigmoid(z) * inv)
        heads = slice(g * PER, (g + 1) * PER)
        x = xt[group(g), :]
        passed = heads_in(dyg * x)
        dskip[heads, :] = passed
        dcum[heads, :] = heads_in(dyg * (yg - heads_out(skip[...], g) * x))
        u = heads_out(alpha, g) * dyg
        dz[group(g), :] = dot(u, mt[lanes(g), :], 1, 1)
        dm = jnp.where(causal, dot(zs[group(g), :], u, 0, 0), 0.0)
        dc[:, lanes(g)] = dot(dm, bc[:, lanes(g)], 0, 0) + dot(u, full[group(g), :], 0, 0)
        db[:, lanes(g)] = dot(dm, cc[:, lanes(g)])
    for r in range(PER):
        gz[:, lanes(r)] = take(slope, r).astype(jnp.bfloat16)
        early[16 + r : 17 + r, :] = jnp.sum(take(shares, r), axis=0, keepdims=True)
    extend(extc, c, hc)
    clear_pad(padc)
    for g in range(GROUPS):
        mine, ahead, taps = conv_back_tile(extc, padc, wc, lanes(g), dc[:, lanes(g)])
        cpart[g, 0:SPAN, :] = mine
        cpart[g, SPAN : SPAN + 8, :] = ahead
        for k in range(CONV):
            early[k * GROUPS + g : k * GROUPS + g + 1, :] = taps[k]


def last_kernel(
    core, own, got, full, ends, dz1, db1, dcum1, dskip, early, cpart, dy, zs, xt, bc, cum, step, skip, dt, bias, alog,
    x, hx, wx, b, hb, wb,
    xown, heads, parts, packed, ddt, later, ext, extb, pad, padb,
):
    unite(core[0], later, own, got)
    gamma = jnp.exp(-cum[...])
    scale = gamma * step[...]
    clear_pad(pad)
    clear_pad(padb)
    extend(ext, x, hx)
    extend(extb, b, hb)
    dxs, turned, straight = [], [], []
    at_end = lax.broadcasted_iota(jnp.int32, (PER, SPAN), 1) == SPAN - 1
    for g in range(GROUPS):
        here = slice(g * PER, (g + 1) * PER)
        zg, xg = zs[group(g), :], xt[group(g), :]
        d = heads_out(ends[...], g) * later[group(g), :]
        second = dot(d, bc[:, lanes(g)], 1, 1)
        dzg = dz1[group(g), :] + second
        dxs.append(heads_out(scale, g) * dzg + heads_out(skip[...], g) * dy[group(g), :])
        edge = heads_in(zg * second + d * full[group(g), :])
        edge = jnp.sum(edge, axis=1, keepdims=True)
        turned.append(dcum1[here, :] - heads_in(dzg * zg) + jnp.where(at_end, edge, 0.0))
        straight.append(heads_in(dzg * xg))
        dbg = db1[:, lanes(g)] + dot(zg, d, 0, 0)
        mine, ahead, taps = conv_back_tile(extb, padb, wb, lanes(g), dbg)
        parts[g, 0:SPAN, :] = mine
        parts[g, SPAN : 2 * SPAN, :] = cpart[g, 0:SPAN, :]
        parts[g, 2 * SPAN : 2 * SPAN + 8, :] = ahead
        parts[g, 2 * SPAN + 8 : 2 * SPAN + 16, :] = cpart[g, SPAN : SPAN + 8, :]
        for k in range(CONV):
            packed[k * GROUPS + g : k * GROUPS + g + 1, :] = taps[k]
    dlog = dot(jnp.concatenate(turned, axis=0), jnp.where(triangle(False), 1.0, 0.0))
    rate = -jnp.exp(alog[...])
    dstep = jnp.concatenate(straight, axis=0) * gamma + dlog * rate
    draw = dstep * sigmoid(dt[...] + bias[...])
    ddt[...] = draw
    each = jnp.concatenate([draw, dlog * rate * step[...], dskip[...], jnp.zeros((LOCAL, SPAN), F32)], axis=0)
    packed[72:80, :] = dot(jnp.ones((8, SPAN), F32), each, 1, 1)
    packed[16:32, :] = early[0:16, :]
    packed[64:72, :] = early[16:24, :]
    for r in range(PER):
        mine, ahead, taps = conv_back_tile(ext, pad, wx, lanes(r), take(dxs, r))
        xown[:, lanes(r)] = mine
        heads[8 * r : 8 * r + 8, :] = ahead
        for k in range(CONV):
            packed[32 + k * PER + r : 33 + k * PER + r, :] = taps[k]


def pair_decays(core, pair, lead):
    mine, theirs = pair[0 : LOCAL // 2, :], pair[LOCAL // 2 : LOCAL, :]
    leads = core == lead
    return jnp.where(leads, mine, theirs), jnp.where(leads, theirs, mine), leads


def join_first_kernel(core, keep, got, ends, joint, pair):
    half = LOCAL // 2
    pair[0:half, :] = ends[pl.ds(pl.multiple_of(core[0] * half, half), half), :]
    pair[half:LOCAL, :] = got[pl.ds(pl.multiple_of(HALF + core[0] * half, half), half), :]
    first, second, leads = pair_decays(core[0], pair, 0)
    for h in range(half):
        rows = slice(h * HEAD_DIM, (h + 1) * HEAD_DIM)
        mine, theirs = keep[rows, :], got[rows, :]
        both = second[h : h + 1] * jnp.where(leads, mine, theirs) + jnp.where(leads, theirs, mine)
        for i in range(HEAD_DIM):
            joint[2 * h + i // 16, :, lanes(i % 16)] = both[i : i + 1]
        for i in range(2):
            joint[2 * h + i, :, CHUNK:] = first[h : h + 1] * second[h : h + 1]


def join_again_kernel(core, keep, got, pair, joint):
    _, second, leads = pair_decays(core[0], pair, 1)
    for h in range(LOCAL // 2):
        rows = slice(h * HEAD_DIM, (h + 1) * HEAD_DIM)
        mine, theirs = keep[rows, :], got[rows, :]
        joint[rows, :] = second[h : h + 1] * jnp.where(leads, mine, theirs) + jnp.where(leads, theirs, mine)


def split_kernel(lead, core, ahead, keep, got, pair, own, give):
    first, _, leads = pair_decays(core[0], pair, lead)
    for h in range(LOCAL // 2):
        rows = slice(h * HEAD_DIM, (h + 1) * HEAD_DIM)
        far = ahead[rows, :]
        near = first[h : h + 1] * far + jnp.where(leads, keep[rows, :], got[rows, :])
        own[rows, :] = jnp.where(leads, far, near)
        give[rows, :] = jnp.where(leads, near, far)


def add_kernel(slices, xheads, mine, heads):
    total = slices[0]
    for g in range(1, GROUPS):
        total = total + slices[g]
    mine[...] = total[0 : 2 * SPAN]
    heads[0:64, :] = xheads[...]
    heads[64:80, :] = total[2 * SPAN :]


def settle_kernel(xown, mine, heads, gx, spread):
    last = slice(SPAN - LEAD, SPAN)
    none = jnp.zeros((LEAD - 8, TILE), F32)
    for r in range(PER):
        gx[0 : SPAN - LEAD, lanes(r)] = xown[0 : SPAN - LEAD, lanes(r)].astype(jnp.bfloat16)
        more = jnp.concatenate([none, heads[8 * r : 8 * r + 8, :]], axis=0)
        gx[last, lanes(r)] = (xown[last, lanes(r)] + more).astype(jnp.bfloat16)
    for i in range(2):
        more = jnp.concatenate([none, heads[64 + 8 * i : 72 + 8 * i, :]], axis=0)
        body_rows = mine[i * SPAN : (i + 1) * SPAN - LEAD, :].astype(jnp.bfloat16)
        last_rows = (mine[(i + 1) * SPAN - LEAD : (i + 1) * SPAN, :] + more).astype(jnp.bfloat16)
        for g in range(GROUPS):
            spread[g, i * SPAN : (i + 1) * SPAN - LEAD, :] = body_rows
            spread[g, (i + 1) * SPAN - LEAD : (i + 1) * SPAN, :] = last_rows


def finish_kernel(spread, bc_taps, packed, gb, gc, tx, tb, tc, tgain, small):
    for g in range(GROUPS):
        gb[:, lanes(g)] = spread[g, 0:SPAN, :]
        gc[:, lanes(g)] = spread[g, SPAN : 2 * SPAN, :]
    for k in range(CONV):
        for g in range(GROUPS):
            tb[k : k + 1, lanes(g)] = bc_taps[k * GROUPS + g : k * GROUPS + g + 1, :]
            tc[k : k + 1, lanes(g)] = bc_taps[16 + k * GROUPS + g : 17 + k * GROUPS + g, :]
        for r in range(PER):
            tx[k : k + 1, lanes(r)] = packed[32 + k * PER + r : 33 + k * PER + r, :]
    for r in range(PER):
        tgain[:, lanes(r)] = packed[64 + r : 65 + r, :]
    small[...] = packed[72:80, :]


def scan_kernel(backward, s, d, o):
    count = s.shape[0]
    at = d.shape[2] - TILE
    carry = [jnp.zeros((1, TILE), F32)] * (CHUNK // TILE)
    for j in range(count):
        j = count - 1 - j if backward else j
        decay = d[j, :, at:]
        for k in range(CHUNK // TILE):
            o[j, :, lanes(k)] = carry[k]
            carry[k] = decay * carry[k] + s[j, :, lanes(k)]


def call(kernel, name, outs, args, scratch=(), scalars=0, flops=20_000_000):
    smem = pl.BlockSpec(memory_space=pltpu.SMEM)
    vmem = pl.BlockSpec(memory_space=pltpu.VMEM)
    return pl.pallas_call(
        kernel,
        out_shape=[jax.ShapeDtypeStruct(s, d) for s, d in outs],
        in_specs=[smem if i < scalars else vmem for i in range(len(args))],
        out_specs=[vmem] * len(outs),
        scratch_shapes=[pltpu.VMEM(s, F32) for s in scratch],
        compiler_params=PARAMS,
        cost_estimate=pl.CostEstimate(flops=flops, bytes_accessed=4 << 20, transcendentals=1 << 18),
        name=name,
    )(*args)


def swap_cores(v):
    return lax.ppermute(v, "core", [(0, 1), (1, 0)])


def alike(size, by):
    return [(i, i ^ by) for i in range(size)]


def over_chips(v):
    return lax.all_to_all(v, "chip", 0, 0)


def butterfly(x, axis):
    by = 1
    while by < lax.axis_size(axis):
        x = x + lax.ppermute(x, axis, alike(lax.axis_size(axis), by))
        by *= 2
    return x


def by_group(v):
    return v.reshape((PER, GROUPS) + v.shape[1:]).swapaxes(0, 1).reshape(v.shape)


def by_head(v):
    return v.reshape((GROUPS, PER) + v.shape[1:]).swapaxes(0, 1).reshape(v.shape)


def body(
    x_raw, b_raw, c_raw, z_gate, dt_raw, conv_x, conv_b, conv_c, dt_bias, a_log, d_skip, gain, grad_out
):
    size = lax.axis_size(CTX)
    core = lax.axis_index("core")
    cores = core.reshape(1)
    is_even = core == 0
    t_shape = ((ALL, SPAN), F32)
    bc_shape = ((SPAN, GROUPS * STATE), F32)
    h_shape = ((LOCAL, SPAN), F32)
    tails = jnp.concatenate([v[SPAN - LEAD :] for v in (x_raw, b_raw, c_raw)], axis=1)
    before = lax.ppermute(tails, CTX, [(i, i + 1) for i in range(size - 1)])
    wx, wb = x_raw.shape[1], b_raw.shape[1]
    hx, hb, hc = before[:, :wx], before[:, wx : wx + wb], before[:, wx + wb :]

    dt = by_group(dt_raw.T)
    bias, alog, skip_col = (by_group(v)[:, None] for v in (dt_bias, a_log, d_skip))
    skip = jnp.broadcast_to(skip_col, h_shape[0])
    step, cum, ends = call(steps_kernel, "steps", [h_shape] * 3, (dt, bias, alog))
    zt, ogt, sgt = call(turn_kernel, "turn", [t_shape] * 3, (z_gate, grad_out, gain[None]))
    xt, zs, bc, keep, give = call(
        state_kernel,
        "state",
        [t_shape, t_shape, bc_shape, ((HALF, STATE), F32), ((HALF + LOCAL, STATE), F32)],
        (cores, x_raw, hx, b_raw, hb, conv_x, conv_b, step, cum, ends),
        [(LEAD + SPAN, wx), (LEAD + SPAN, wb), (ALL, STATE)],
        scalars=1,
    )
    got = swap_cores(give)
    half_shape = ((HALF, STATE), F32)
    chips = lax.axis_size("chip")
    joint, pair = call(
        join_first_kernel,
        "join",
        [((chips, 1, CHUNK + TILE), F32), h_shape],
        (cores, keep, got, ends),
        scalars=1,
    )
    firsts = over_chips(joint)
    (entering,) = call(
        functools.partial(scan_kernel, False), "block_scan", [((chips, 1, CHUNK), F32)], (firsts, firsts)
    )
    ahead = over_chips(entering).reshape(HALF, STATE)
    enter_own, enter_give = call(
        functools.partial(split_kernel, 0), "split", [half_shape] * 2, (cores, ahead, keep, got, pair), scalars=1
    )
    enter_got = swap_cores(enter_give)

    cc, mt, y1 = call(
        local_kernel,
        "local",
        [bc_shape, ((GROUPS * SPAN, SPAN), F32), t_shape],
        (c_raw, hc, conv_c, bc, xt, zs, cum, skip),
        [(LEAD + SPAN, wb)],
    )
    enter, y, sums = call(
        output_kernel,
        "output",
        [t_shape, t_shape, ((2 * GROUPS, SPAN), F32)],
        (cores, enter_own, enter_got, cc, y1, cum, zt, sgt),
        scalars=1,
    )
    peers = lax.axis_size("tp")
    sums = sums + sum(lax.ppermute(sums, "tp", [(i, (i + k) % peers) for i in range(peers)]) for k in range(1, peers))
    keep, give, dy, dg = call(
        gate_kernel,
        "gate",
        [((HALF, STATE), F32)] * 2 + [t_shape, t_shape],
        (cores, sums, y, zt, sgt, cum, cc),
        [(ALL, STATE)],
        scalars=1,
    )
    got = swap_cores(give)
    (joint,) = call(join_again_kernel, "join", [half_shape], (cores, keep, got, pair), scalars=1)
    pieces = over_chips(joint.reshape(chips, 1, CHUNK))
    (leaving,) = call(
        functools.partial(scan_kernel, True), "block_scan", [((chips, 1, CHUNK), F32)], (pieces, firsts)
    )
    ahead = over_chips(leaving).reshape(HALF, STATE)
    later_own, later_give = call(
        functools.partial(split_kernel, 1), "split", [half_shape] * 2, (cores, ahead, keep, got, pair), scalars=1
    )
    later_got = swap_cores(later_give)
    dz, db, dcum, dskip, grad_z, early, cpart = call(
        middle_kernel,
        "middle",
        [t_shape, bc_shape, h_shape, h_shape, ((SPAN, wx), jnp.bfloat16), ((24, TILE), F32)]
        + [((GROUPS, SPAN + 8, TILE), F32)],
        (sums, y, zt, ogt, dy, dg, enter, mt, zs, xt, bc, cc, cum, skip, c_raw, hc, conv_c),
        [(LEAD + SPAN, wb), (LEAD + SPAN, wb), (SPAN, wb)],
    )
    xown, xheads, parts, packed, ddt = call(
        last_kernel,
        "last",
        [((SPAN, wx), F32), ((64, TILE), F32), ((GROUPS, 2 * SPAN + 16, TILE), F32), ((80, TILE), F32), h_shape],
        (cores, later_own, later_got, enter, ends, dz, db, dcum, dskip, early, cpart)
        + (dy, zs, xt, bc, cum, step, skip, dt, bias, alog, x_raw, hx, conv_x, b_raw, hb, conv_b),
        [(ALL, STATE), (LEAD + SPAN, wx), (LEAD + SPAN, wb), (LEAD + SPAN, wx), (LEAD + SPAN, wb)],
        scalars=1,
    )
    slices = lax.all_to_all(parts, "tp", 0, 0)
    packed = butterfly(packed, CTX)
    bc_taps = butterfly(packed[:32], "tp")
    mine, heads = call(add_kernel, "add", [((2 * SPAN, TILE), F32), ((80, TILE), F32)], (slices, xheads))
    heads = lax.ppermute(heads, CTX, [(i + 1, i) for i in range(size - 1)])
    grad_x_raw, spread = call(
        settle_kernel,
        "settle",
        [((SPAN, wx), jnp.bfloat16), ((GROUPS, 2 * SPAN, TILE), jnp.bfloat16)],
        (xown, mine, heads),
    )
    spread = lax.all_to_all(spread, "tp", 0, 0)
    half_bc = ((SPAN, wb), jnp.bfloat16)
    grad_b_raw, grad_c_raw, conv_x_total, conv_b_total, conv_c_total, gain_total, small = call(
        finish_kernel,
        "finish",
        [half_bc, half_bc, ((CONV, wx), F32), ((CONV, wb), F32), ((CONV, wb), F32), ((1, wx), F32), ((8, TILE), F32)],
        (spread, bc_taps, packed),
    )
    small = [by_head(small[0, i * LOCAL : (i + 1) * LOCAL]) for i in range(3)]
    return (
        grad_x_raw,
        grad_b_raw,
        grad_c_raw,
        grad_z,
        by_head(ddt).T,
        conv_x_total,
        conv_b_total,
        conv_c_total,
        *small,
        gain_total.reshape(-1),
    )


def solution(mesh):
    rows, cols, some = P(CTX, "tp"), P(None, "tp"), P("tp")
    chips, tp = mesh.shape["ctx"] // 2, mesh.shape["tp"]
    mesh = Mesh(mesh.devices.reshape(chips, 2, tp), (*CTX, "tp"))
    return jax.shard_map(
        body,
        mesh=mesh,
        in_specs=(rows, P(CTX, None), P(CTX, None), rows, rows, cols, P(), P(), some, some, some, some, rows),
        out_specs=(rows, P(CTX, None), P(CTX, None), rows, rows, cols, P(), P(), some, some, some, some),
        check_vma=False,
    )
```

```python
import functools

import jax
import jax.numpy as jnp
from jax import lax
from jax.experimental import pallas as pl
from jax.experimental.pallas import tpu as pltpu
from jax.sharding import Mesh, PartitionSpec as P

HEAD_DIM = 32
STATE = 128
GROUPS = 4
CONV = 4
SPAN = 128
TILE = 128
PER = 8
LOCAL = PER * GROUPS
ROWS = PER * HEAD_DIM
ALL = LOCAL * HEAD_DIM
HALF = ALL // 2
CHUNK = 2048
LEAD = 16
GROUP_WIDTH = 1024
EPSILON = 1e-05
F32 = jnp.float32
CTX = ("chip", "core")
RING = 8
PARAMS = pltpu.CompilerParams(vmem_limit_bytes=16 << 20)


def dot(a, b, ca=1, cb=0):
    return lax.dot_general(
        a, b, (((ca,), (cb,)), ((), ())), precision=lax.Precision.HIGHEST, preferred_element_type=F32
    )


def group(g):
    return slice(g * ROWS, (g + 1) * ROWS)


def lanes(r):
    return slice(r * TILE, (r + 1) * TILE)


def spot(g, r):
    return slice(g * ROWS + r * HEAD_DIM, g * ROWS + (r + 1) * HEAD_DIM)


def put(dst, r, tile):
    turned = tile.T
    for g in range(GROUPS):
        dst[spot(g, r), :] = turned[g * HEAD_DIM : (g + 1) * HEAD_DIM]


def take(values, r):
    rows = slice(r * HEAD_DIM, (r + 1) * HEAD_DIM)
    return jnp.concatenate([v[rows] for v in values], axis=0).T


def heads_out(v, g):
    return jnp.concatenate(
        [jnp.broadcast_to(v[g * PER + r : g * PER + r + 1], (HEAD_DIM, v.shape[1])) for r in range(PER)], axis=0
    )


def heads_in(v):
    return jnp.concatenate(
        [jnp.sum(v[r * HEAD_DIM : (r + 1) * HEAD_DIM], axis=0, keepdims=True) for r in range(PER)], axis=0
    )


def sigmoid(v):
    return 1.0 / (1.0 + jnp.exp(-v))


def silu_slope(v):
    s = sigmoid(v)
    return s * (1.0 + v * (1.0 - s))


def extend(ext, raw, before):
    ext[0:LEAD, :] = before[...].astype(F32)
    ext[LEAD : LEAD + SPAN, :] = raw[...].astype(F32)


def conv_tile(ext, w, cols):
    total = w[0:1, cols] * ext[LEAD - 3 : LEAD - 3 + SPAN, cols]
    for k in range(1, CONV):
        total = total + w[k : k + 1, cols] * ext[LEAD - 3 + k : LEAD - 3 + k + SPAN, cols]
    return total


def conv_back_tile(ext, pad, w, cols, grad):
    dpre = grad * silu_slope(conv_tile(ext, w, cols))
    pad[8 : 8 + SPAN, cols] = dpre
    taps = [
        jnp.sum(dpre * ext[LEAD - 3 + k : LEAD - 3 + k + SPAN, cols], axis=0, keepdims=True) for k in range(CONV)
    ]
    mine = w[0:1, cols] * pad[11 : 11 + SPAN, cols]
    ahead = w[0:1, cols] * pad[3:11, cols]
    for k in range(1, CONV):
        mine = mine + w[k : k + 1, cols] * pad[11 - k : 11 - k + SPAN, cols]
        ahead = ahead + w[k : k + 1, cols] * pad[3 - k : 11 - k, cols]
    return mine, ahead, taps


def clear_pad(pad):
    pad[0:8, :] = jnp.zeros((8, pad.shape[1]), F32)
    pad[8 + SPAN : 16 + SPAN, :] = jnp.zeros((8, pad.shape[1]), F32)


def halves(core, full, keep, give):
    keep[...] = full[pl.ds(pl.multiple_of(core * HALF, HALF), HALF), :]
    give[0:HALF, :] = full[pl.ds(pl.multiple_of((1 - core) * HALF, HALF), HALF), :]


def unite(core, full, own, got):
    full[pl.ds(pl.multiple_of(core * HALF, HALF), HALF), :] = own[...]
    full[pl.ds(pl.multiple_of((1 - core) * HALF, HALF), HALF), :] = got[...]


def triangle(upper):
    rows = lax.broadcasted_iota(jnp.int32, (SPAN, SPAN), 0)
    cols = lax.broadcasted_iota(jnp.int32, (SPAN, SPAN), 1)
    return rows <= cols if upper else rows >= cols


def steps_kernel(dt, bias, alog, step, cum, ends):
    v = dt[...] + bias[...]
    step[...] = jnp.maximum(v, 0.0) + jnp.log1p(jnp.exp(-jnp.abs(v)))
    rates = -jnp.exp(alog[...]) * step[...]
    cum[...] = dot(rates, jnp.where(triangle(True), 1.0, 0.0))
    ends[...] = jnp.broadcast_to(jnp.exp(jnp.sum(rates, axis=1, keepdims=True)), ends.shape)


def turn_kernel(z, og, gain, zt, ogt, sgt):
    for r in range(PER):
        put(zt, r, z[:, lanes(r)].astype(F32))
        tile = og[:, lanes(r)].astype(F32)
        put(ogt, r, tile)
        put(sgt, r, tile * gain[:, lanes(r)])


def state_kernel(core, x, hx, b, hb, wx, wb, step, cum, ends, xt, zs, bc, keep, give, ext, extb, full):
    extend(ext, x, hx)
    extend(extb, b, hb)
    for g in range(GROUPS):
        pre = conv_tile(extb, wb, lanes(g))
        bc[:, lanes(g)] = pre * sigmoid(pre)
    for r in range(PER):
        pre = conv_tile(ext, wx, lanes(r))
        put(xt, r, pre * sigmoid(pre))
    scale = jnp.exp(-cum[...]) * step[...]
    for g in range(GROUPS):
        zg = xt[group(g), :] * heads_out(scale, g)
        zs[group(g), :] = zg
        full[group(g), :] = heads_out(ends[...], g) * dot(zg, bc[:, lanes(g)])
    halves(core[0], full, keep, give)
    give[HALF : HALF + LOCAL, :] = ends[...]


def local_kernel(c, hc, wc, bc, xt, zs, cum, skip, cc, mt, y, extc):
    extend(extc, c, hc)
    alpha = jnp.exp(cum[...])
    causal = triangle(True)
    for g in range(GROUPS):
        pre = conv_tile(extc, wc, lanes(g))
        cg = pre * sigmoid(pre)
        cc[:, lanes(g)] = cg
        m = jnp.where(causal, dot(bc[:, lanes(g)], cg, 1, 1), 0.0)
        mt[lanes(g), :] = m
        y[group(g), :] = heads_out(alpha, g) * dot(zs[group(g), :], m) + heads_out(skip[...], g) * xt[group(g), :]


def output_kernel(core, own, got, cc, y1, cum, zt, sgt, full, y, sums):
    unite(core[0], full, own, got)
    alpha = jnp.exp(cum[...])
    for g in range(GROUPS):
        yg = y1[group(g), :] + heads_out(alpha, g) * dot(full[group(g), :], cc[:, lanes(g)], 1, 1)
        y[group(g), :] = yg
        z = zt[group(g), :]
        gated = yg * z * sigmoid(z)
        sums[g : g + 1, :] = jnp.sum(gated * gated, axis=0, keepdims=True)
        sums[GROUPS + g : GROUPS + g + 1, :] = jnp.sum(sgt[group(g), :] * gated, axis=0, keepdims=True)


def gate_kernel(core, sums, y, zt, sgt, cum, cc, keep, give, dy, dg, full):
    alpha = jnp.exp(cum[...])
    for g in range(GROUPS):
        inv = lax.rsqrt(sums[g : g + 1, :] / GROUP_WIDTH + EPSILON)
        fix = inv * inv * inv * sums[GROUPS + g : GROUPS + g + 1, :] / GROUP_WIDTH
        z = zt[group(g), :]
        act = z * sigmoid(z)
        dgated = inv * sgt[group(g), :] - y[group(g), :] * act * fix
        dg[group(g), :] = dgated
        dyg = dgated * act
        dy[group(g), :] = dyg
        full[group(g), :] = dot(heads_out(alpha, g) * dyg, cc[:, lanes(g)])
    halves(core[0], full, keep, give)


def middle_kernel(
    sums, y, zt, ogt, dy, dg, full, mt, zs, xt, bc, cc, cum, skip, c, hc, wc,
    dz, db, dcum, dskip, gz, early, cpart, extc, padc, dc,
):
    alpha = jnp.exp(cum[...])
    causal = triangle(True)
    slope, shares = [], []
    for g in range(GROUPS):
        z, yg, dyg = zt[group(g), :], y[group(g), :], dy[group(g), :]
        inv = lax.rsqrt(sums[g : g + 1, :] / GROUP_WIDTH + EPSILON)
        slope.append(dg[group(g), :] * yg * silu_slope(z))
        shares.append(ogt[group(g), :] * yg * z * sigmoid(z) * inv)
        heads = slice(g * PER, (g + 1) * PER)
        x = xt[group(g), :]
        passed = heads_in(dyg * x)
        dskip[heads, :] = passed
        dcum[heads, :] = heads_in(dyg * (yg - heads_out(skip[...], g) * x))
        u = heads_out(alpha, g) * dyg
        dz[group(g), :] = dot(u, mt[lanes(g), :], 1, 1)
        dm = jnp.where(causal, dot(zs[group(g), :], u, 0, 0), 0.0)
        dc[:, lanes(g)] = dot(dm, bc[:, lanes(g)], 0, 0) + dot(u, full[group(g), :], 0, 0)
        db[:, lanes(g)] = dot(dm, cc[:, lanes(g)])
    for r in range(PER):
        gz[:, lanes(r)] = take(slope, r).astype(jnp.bfloat16)
        early[16 + r : 17 + r, :] = jnp.sum(take(shares, r), axis=0, keepdims=True)
    extend(extc, c, hc)
    clear_pad(padc)
    for g in range(GROUPS):
        mine, ahead, taps = conv_back_tile(extc, padc, wc, lanes(g), dc[:, lanes(g)])
        cpart[g, 0:SPAN, :] = mine
        cpart[g, SPAN : SPAN + 8, :] = ahead
        for k in range(CONV):
            early[k * GROUPS + g : k * GROUPS + g + 1, :] = taps[k]


def last_kernel(
    core, own, got, full, ends, dz1, db1, dcum1, dskip, early, cpart, dy, zs, xt, bc, cum, step, skip, dt, bias, alog,
    x, hx, wx, b, hb, wb,
    xown, heads, keep, give, packed, ddt, parts, later, ext, extb, pad, padb,
):
    unite(core[0], later, own, got)
    gamma = jnp.exp(-cum[...])
    scale = gamma * step[...]
    clear_pad(pad)
    clear_pad(padb)
    extend(ext, x, hx)
    extend(extb, b, hb)
    dxs, turned, straight = [], [], []
    at_end = lax.broadcasted_iota(jnp.int32, (PER, SPAN), 1) == SPAN - 1
    for g in range(GROUPS):
        here = slice(g * PER, (g + 1) * PER)
        zg, xg = zs[group(g), :], xt[group(g), :]
        d = heads_out(ends[...], g) * later[group(g), :]
        second = dot(d, bc[:, lanes(g)], 1, 1)
        dzg = dz1[group(g), :] + second
        dxs.append(heads_out(scale, g) * dzg + heads_out(skip[...], g) * dy[group(g), :])
        edge = heads_in(zg * second + d * full[group(g), :])
        edge = jnp.sum(edge, axis=1, keepdims=True)
        turned.append(dcum1[here, :] - heads_in(dzg * zg) + jnp.where(at_end, edge, 0.0))
        straight.append(heads_in(dzg * xg))
        dbg = db1[:, lanes(g)] + dot(zg, d, 0, 0)
        mine, ahead, taps = conv_back_tile(extb, padb, wb, lanes(g), dbg)
        parts[g, 0:SPAN, :] = mine
        parts[g, SPAN : 2 * SPAN, :] = cpart[g, 0:SPAN, :]
        parts[g, 2 * SPAN : 2 * SPAN + 8, :] = ahead
        parts[g, 2 * SPAN + 8 : 2 * SPAN + 16, :] = cpart[g, SPAN : SPAN + 8, :]
        for k in range(CONV):
            packed[k * GROUPS + g : k * GROUPS + g + 1, :] = taps[k]
    dlog = dot(jnp.concatenate(turned, axis=0), jnp.where(triangle(False), 1.0, 0.0))
    rate = -jnp.exp(alog[...])
    dstep = jnp.concatenate(straight, axis=0) * gamma + dlog * rate
    draw = dstep * sigmoid(dt[...] + bias[...])
    ddt[...] = draw
    each = jnp.concatenate([draw, dlog * rate * step[...], dskip[...], jnp.zeros((LOCAL, SPAN), F32)], axis=0)
    at = lax.broadcasted_iota(jnp.int32, (SPAN, SPAN), 0)
    to = lax.broadcasted_iota(jnp.int32, (SPAN, SPAN), 1)
    source = to // LOCAL * LOCAL + to % GROUPS * PER + to % LOCAL // GROUPS
    packed[72:80, :] = dot(dot(jnp.ones((8, SPAN), F32), each, 1, 1), jnp.where(at == source, 1.0, 0.0))
    packed[16:32, :] = early[0:16, :]
    packed[64:72, :] = early[16:24, :]
    side = core[1]
    keep[...] = parts[pl.ds(side * 2, 2)]
    give[...] = parts[pl.ds((1 - side) * 2, 2)]
    for r in range(PER):
        mine, ahead, taps = conv_back_tile(ext, pad, wx, lanes(r), take(dxs, r))
        xown[:, lanes(r)] = mine
        heads[8 * r : 8 * r + 8, :] = ahead
        for k in range(CONV):
            packed[32 + k * PER + r : 33 + k * PER + r, :] = taps[k]


def pair_decays(core, pair, lead):
    mine, theirs = pair[0 : LOCAL // 2, :], pair[LOCAL // 2 : LOCAL, :]
    leads = core == lead
    return jnp.where(leads, mine, theirs), jnp.where(leads, theirs, mine), leads


def join_first_kernel(core, keep, got, ends, joint, pair):
    half = LOCAL // 2
    pair[0:half, :] = ends[pl.ds(pl.multiple_of(core[0] * half, half), half), :]
    pair[half:LOCAL, :] = got[pl.ds(pl.multiple_of(HALF + core[0] * half, half), half), :]
    first, second, leads = pair_decays(core[0], pair, 0)
    for h in range(half):
        rows = slice(h * HEAD_DIM, (h + 1) * HEAD_DIM)
        mine, theirs = keep[rows, :], got[rows, :]
        both = second[h : h + 1] * jnp.where(leads, mine, theirs) + jnp.where(leads, theirs, mine)
        for i in range(HEAD_DIM):
            joint[2 * h + i // 16, :, lanes(i % 16)] = both[i : i + 1]
        for i in range(2):
            joint[2 * h + i, :, CHUNK:] = first[h : h + 1] * second[h : h + 1]


def join_again_kernel(core, keep, got, pair, joint):
    _, second, leads = pair_decays(core[0], pair, 1)
    for h in range(LOCAL // 2):
        rows = slice(h * HEAD_DIM, (h + 1) * HEAD_DIM)
        mine, theirs = keep[rows, :], got[rows, :]
        joint[rows, :] = second[h : h + 1] * jnp.where(leads, mine, theirs) + jnp.where(leads, theirs, mine)


def split_kernel(lead, core, ahead, keep, got, pair, own, give):
    first, _, leads = pair_decays(core[0], pair, lead)
    for h in range(LOCAL // 2):
        rows = slice(h * HEAD_DIM, (h + 1) * HEAD_DIM)
        far = ahead[rows, :]
        near = first[h : h + 1] * far + jnp.where(leads, keep[rows, :], got[rows, :])
        own[rows, :] = jnp.where(leads, far, near)
        give[rows, :] = jnp.where(leads, near, far)


def settle_kernel(xown, mine, heads, gx, half):
    last = slice(SPAN - LEAD, SPAN)
    none = jnp.zeros((LEAD - 8, TILE), F32)
    for r in range(PER):
        gx[0 : SPAN - LEAD, lanes(r)] = xown[0 : SPAN - LEAD, lanes(r)].astype(jnp.bfloat16)
        more = jnp.concatenate([none, heads[8 * r : 8 * r + 8, :]], axis=0)
        gx[last, lanes(r)] = (xown[last, lanes(r)] + more).astype(jnp.bfloat16)
    for g in range(2):
        for i in range(2):
            at = 64 + 16 * g + 8 * i
            more = jnp.concatenate([none, heads[at : at + 8, :]], axis=0)
            start, stop = i * SPAN, (i + 1) * SPAN
            half[g, start : stop - LEAD, :] = mine[g, start : stop - LEAD, :].astype(jnp.bfloat16)
            half[g, stop - LEAD : stop, :] = (mine[g, stop - LEAD : stop, :] + more).astype(jnp.bfloat16)


def finish_kernel(core, half, other, bc_taps, packed, gb, gc, tx, tb, tc, tgain, bias, rate, skip):
    left = core[1] == 0
    for g in range(GROUPS):
        first, second = (half, other) if g < 2 else (other, half)
        both = jnp.where(left, first[g % 2].astype(F32), second[g % 2].astype(F32)).astype(jnp.bfloat16)
        gb[:, lanes(g)] = both[0:SPAN]
        gc[:, lanes(g)] = both[SPAN : 2 * SPAN]
    for k in range(CONV):
        for g in range(GROUPS):
            tb[k : k + 1, lanes(g)] = bc_taps[k * GROUPS + g : k * GROUPS + g + 1, :]
            tc[k : k + 1, lanes(g)] = bc_taps[16 + k * GROUPS + g : 17 + k * GROUPS + g, :]
        for r in range(PER):
            tx[k : k + 1, lanes(r)] = packed[32 + k * PER + r : 33 + k * PER + r, :]
    for r in range(PER):
        tgain[:, lanes(r)] = packed[64 + r : 65 + r, :]
    bias[...] = packed[72:73, 0:LOCAL]
    rate[...] = packed[72:73, LOCAL : 2 * LOCAL]
    skip[...] = packed[72:73, 2 * LOCAL : 3 * LOCAL]


def scan_kernel(backward, s, d, o):
    count = s.shape[0]
    at = d.shape[2] - TILE
    carry = [jnp.zeros((1, TILE), F32)] * (CHUNK // TILE)
    for j in range(count):
        j = count - 1 - j if backward else j
        decay = d[j, :, at:]
        for k in range(CHUNK // TILE):
            o[j, :, lanes(k)] = carry[k]
            carry[k] = decay * carry[k] + s[j, :, lanes(k)]


def call(kernel, name, outs, args, scratch=(), scalars=0, flops=20_000_000):
    smem = pl.BlockSpec(memory_space=pltpu.SMEM)
    vmem = pl.BlockSpec(memory_space=pltpu.VMEM)
    return pl.pallas_call(
        kernel,
        out_shape=[jax.ShapeDtypeStruct(s, d) for s, d in outs],
        in_specs=[smem if i < scalars else vmem for i in range(len(args))],
        out_specs=[vmem] * len(outs),
        scratch_shapes=[pltpu.VMEM(s, F32) for s in scratch],
        compiler_params=PARAMS,
        cost_estimate=pl.CostEstimate(flops=flops, bytes_accessed=4 << 20, transcendentals=1 << 18),
        name=name,
    )(*args)


def swap_cores(v):
    return lax.ppermute(v, "core", [(0, 1), (1, 0)])


def alike(size, by):
    return [(i, i ^ by) for i in range(size)]


def over_chips(v):
    return lax.all_to_all(v, "chip", 0, 0)


def fold(x, axis, partner):
    return x + lax.ppermute(x, axis, [(i, partner(i)) for i in range(lax.axis_size(axis))])


def mirror(within, block=1):
    return lambda i: (i // block // within * within + within - 1 - i // block % within) * block + i % block


def sum_steps(axis):
    size = lax.axis_size(axis)
    ring = min(RING, size)
    steps, within = [], 2
    while within <= ring:
        half = within // 2
        steps.append(mirror(within) if within in (2, ring) else (lambda i, half=half: i ^ half))
        within *= 2
    within = 2
    while within * ring <= size:
        steps.append(mirror(within, ring))
        within *= 2
    return steps


def sum_over(x, axis):
    for partner in sum_steps(axis):
        x = fold(x, axis, partner)
    return x


def by_group(v):
    return v.reshape((PER, GROUPS) + v.shape[1:]).swapaxes(0, 1).reshape(v.shape)


def by_head(v):
    return v.reshape((GROUPS, PER) + v.shape[1:]).swapaxes(0, 1).reshape(v.shape)


def body(
    x_raw, b_raw, c_raw, z_gate, dt_raw, conv_x, conv_b, conv_c, dt_bias, a_log, d_skip, gain, grad_out
):
    size = lax.axis_size(CTX)
    core = lax.axis_index("core")
    side = lax.axis_index("tp") // (lax.axis_size("tp") // 2)
    cores = jnp.stack([core, side])
    is_even = core == 0
    t_shape = ((ALL, SPAN), F32)
    bc_shape = ((SPAN, GROUPS * STATE), F32)
    h_shape = ((LOCAL, SPAN), F32)
    tails = jnp.concatenate([v[SPAN - LEAD :] for v in (x_raw, b_raw, c_raw)], axis=1)
    before = lax.ppermute(tails, CTX, [(i, i + 1) for i in range(size - 1)])
    wx, wb = x_raw.shape[1], b_raw.shape[1]
    hx, hb, hc = before[:, :wx], before[:, wx : wx + wb], before[:, wx + wb :]

    dt = by_group(dt_raw.T)
    bias, alog, skip_col = (by_group(v)[:, None] for v in (dt_bias, a_log, d_skip))
    skip = jnp.broadcast_to(skip_col, h_shape[0])
    step, cum, ends = call(steps_kernel, "steps", [h_shape] * 3, (dt, bias, alog))
    zt, ogt, sgt = call(turn_kernel, "turn", [t_shape] * 3, (z_gate, grad_out, gain[None]))
    xt, zs, bc, keep, give = call(
        state_kernel,
        "state",
        [t_shape, t_shape, bc_shape, ((HALF, STATE), F32), ((HALF + LOCAL, STATE), F32)],
        (cores, x_raw, hx, b_raw, hb, conv_x, conv_b, step, cum, ends),
        [(LEAD + SPAN, wx), (LEAD + SPAN, wb), (ALL, STATE)],
        scalars=1,
    )
    got = swap_cores(give)
    half_shape = ((HALF, STATE), F32)
    chips = lax.axis_size("chip")
    joint, pair = call(
        join_first_kernel,
        "join",
        [((chips, 1, CHUNK + TILE), F32), h_shape],
        (cores, keep, got, ends),
        scalars=1,
    )
    firsts = over_chips(joint)
    (entering,) = call(
        functools.partial(scan_kernel, False), "block_scan", [((chips, 1, CHUNK), F32)], (firsts, firsts)
    )
    ahead = over_chips(entering).reshape(HALF, STATE)
    enter_own, enter_give = call(
        functools.partial(split_kernel, 0), "split", [half_shape] * 2, (cores, ahead, keep, got, pair), scalars=1
    )
    enter_got = swap_cores(enter_give)

    cc, mt, y1 = call(
        local_kernel,
        "local",
        [bc_shape, ((GROUPS * SPAN, SPAN), F32), t_shape],
        (c_raw, hc, conv_c, bc, xt, zs, cum, skip),
        [(LEAD + SPAN, wb)],
    )
    enter, y, sums = call(
        output_kernel,
        "output",
        [t_shape, t_shape, ((2 * GROUPS, SPAN), F32)],
        (cores, enter_own, enter_got, cc, y1, cum, zt, sgt),
        scalars=1,
    )
    sums = sum_over(sums, "tp")
    keep, give, dy, dg = call(
        gate_kernel,
        "gate",
        [((HALF, STATE), F32)] * 2 + [t_shape, t_shape],
        (cores, sums, y, zt, sgt, cum, cc),
        [(ALL, STATE)],
        scalars=1,
    )
    got = swap_cores(give)
    (joint,) = call(join_again_kernel, "join", [half_shape], (cores, keep, got, pair), scalars=1)
    pieces = over_chips(joint.reshape(chips, 1, CHUNK))
    (leaving,) = call(
        functools.partial(scan_kernel, True), "block_scan", [((chips, 1, CHUNK), F32)], (pieces, firsts)
    )
    ahead = over_chips(leaving).reshape(HALF, STATE)
    later_own, later_give = call(
        functools.partial(split_kernel, 1), "split", [half_shape] * 2, (cores, ahead, keep, got, pair), scalars=1
    )
    later_got = swap_cores(later_give)
    dz, db, dcum, dskip, grad_z, early, cpart = call(
        middle_kernel,
        "middle",
        [t_shape, bc_shape, h_shape, h_shape, ((SPAN, wx), jnp.bfloat16), ((24, TILE), F32)]
        + [((GROUPS, SPAN + 8, TILE), F32)],
        (sums, y, zt, ogt, dy, dg, enter, mt, zs, xt, bc, cc, cum, skip, c_raw, hc, conv_c),
        [(LEAD + SPAN, wb), (LEAD + SPAN, wb), (SPAN, wb)],
    )
    half_parts = ((2, 2 * SPAN + 16, TILE), F32)
    xown, xheads, keep, give, packed, ddt = call(
        last_kernel,
        "last",
        [((SPAN, wx), F32), ((64, TILE), F32), half_parts, half_parts, ((80, TILE), F32), h_shape],
        (cores, later_own, later_got, enter, ends, dz, db, dcum, dskip, early, cpart)
        + (dy, zs, xt, bc, cum, step, skip, dt, bias, alog, x_raw, hx, conv_x, b_raw, hb, conv_b),
        [(GROUPS, 2 * SPAN + 16, TILE), (ALL, STATE)]
        + [(LEAD + SPAN, wx), (LEAD + SPAN, wb), (LEAD + SPAN, wx), (LEAD + SPAN, wb)],
        scalars=1,
    )
    peers = lax.axis_size("tp")
    across = [(i, peers - 1 - i) for i in range(peers)]
    arrived = lax.ppermute(give, "tp", across)
    packed = packed + swap_cores(packed)
    steps = sum_steps("chip")
    packed = fold(packed, "chip", steps[0])
    arrived, packed = lax.optimization_barrier((arrived, packed))
    mine = keep + arrived
    arrived = lax.ppermute(mine, "tp", [(i, i ^ 1) for i in range(peers)])
    for partner in steps[1:3]:
        packed = fold(packed, "chip", partner)
    arrived, packed = lax.optimization_barrier((arrived, packed))
    mine = mine + arrived
    heads = jnp.concatenate([xheads, mine[:, 2 * SPAN :].reshape(32, TILE)], axis=0)
    heads = lax.ppermute(heads, CTX, [(i + 1, i) for i in range(size - 1)])
    for partner in steps[3:4]:
        packed = fold(packed, "chip", partner)
    heads, packed = lax.optimization_barrier((heads, packed))
    grad_x_raw, half = call(
        settle_kernel,
        "settle",
        [((SPAN, wx), jnp.bfloat16), ((2, 2 * SPAN, TILE), jnp.bfloat16)],
        (xown, mine, heads),
    )
    other = lax.ppermute(half, "tp", across)
    for partner in steps[4:]:
        packed = fold(packed, "chip", partner)
    bc_taps = sum_over(packed[:32], "tp")
    half_bc, each = ((SPAN, wb), jnp.bfloat16), ((1, LOCAL), F32)
    grad_b_raw, grad_c_raw, conv_x_total, conv_b_total, conv_c_total, gain_total, *small = call(
        finish_kernel,
        "finish",
        [half_bc, half_bc, ((CONV, wx), F32), ((CONV, wb), F32), ((CONV, wb), F32), ((1, wx), F32)] + [each] * 3,
        (cores, half, other, bc_taps, packed),
        scalars=1,
    )
    return (
        grad_x_raw,
        grad_b_raw,
        grad_c_raw,
        grad_z,
        by_head(ddt).T,
        conv_x_total,
        conv_b_total,
        conv_c_total,
        *(v.reshape(-1) for v in small),
        gain_total.reshape(-1),
    )


def solution(mesh):
    rows, cols, some = P(CTX, "tp"), P(None, "tp"), P("tp")
    chips, tp = mesh.shape["ctx"] // 2, mesh.shape["tp"]
    mesh = Mesh(mesh.devices.reshape(chips, 2, tp), (*CTX, "tp"))
    return jax.shard_map(
        body,
        mesh=mesh,
        in_specs=(rows, P(CTX, None), P(CTX, None), rows, rows, cols, P(), P(), some, some, some, some, rows),
        out_specs=(rows, P(CTX, None), P(CTX, None), rows, rows, cols, P(), P(), some, some, some, some),
        check_vma=False,
    )
```

```python
import functools

import jax
import jax.numpy as jnp
from jax import lax
from jax.experimental import pallas as pl
from jax.experimental.pallas import tpu as pltpu
from jax.sharding import Mesh, PartitionSpec as P

HEAD_DIM = 32
STATE = 128
GROUPS = 4
CONV = 4
SPAN = 128
TILE = 128
PER = 8
LOCAL = PER * GROUPS
ROWS = PER * HEAD_DIM
ALL = LOCAL * HEAD_DIM
HALF = ALL // 2
CHUNK = 2048
LEAD = 16
GROUP_WIDTH = 1024
EPSILON = 1e-05
F32 = jnp.float32
CTX = ("chip", "core")
RING = 8
PARAMS = pltpu.CompilerParams(vmem_limit_bytes=16 << 20)


def dot(a, b, ca=1, cb=0):
    return lax.dot_general(
        a, b, (((ca,), (cb,)), ((), ())), precision=lax.Precision.HIGHEST, preferred_element_type=F32
    )


def group(g):
    return slice(g * ROWS, (g + 1) * ROWS)


def lanes(r):
    return slice(r * TILE, (r + 1) * TILE)


def spot(g, r):
    return slice(g * ROWS + r * HEAD_DIM, g * ROWS + (r + 1) * HEAD_DIM)


def put(dst, r, tile):
    turned = tile.T
    for g in range(GROUPS):
        dst[spot(g, r), :] = turned[g * HEAD_DIM : (g + 1) * HEAD_DIM]


def take(values, r):
    rows = slice(r * HEAD_DIM, (r + 1) * HEAD_DIM)
    return jnp.concatenate([v[rows] for v in values], axis=0).T


def heads_out(v, g):
    return jnp.concatenate(
        [jnp.broadcast_to(v[g * PER + r : g * PER + r + 1], (HEAD_DIM, v.shape[1])) for r in range(PER)], axis=0
    )


def heads_in(v):
    return jnp.concatenate(
        [jnp.sum(v[r * HEAD_DIM : (r + 1) * HEAD_DIM], axis=0, keepdims=True) for r in range(PER)], axis=0
    )


def sigmoid(v):
    return 1.0 / (1.0 + jnp.exp(-v))


def silu_slope(v):
    s = sigmoid(v)
    return s * (1.0 + v * (1.0 - s))


def extend(ext, raw, before):
    ext[0:LEAD, :] = before[...].astype(F32)
    ext[LEAD : LEAD + SPAN, :] = raw[...].astype(F32)


def conv_tile(ext, w, cols):
    total = w[0:1, cols] * ext[LEAD - 3 : LEAD - 3 + SPAN, cols]
    for k in range(1, CONV):
        total = total + w[k : k + 1, cols] * ext[LEAD - 3 + k : LEAD - 3 + k + SPAN, cols]
    return total


def conv_back_tile(ext, pad, w, cols, grad):
    dpre = grad * silu_slope(conv_tile(ext, w, cols))
    pad[8 : 8 + SPAN, cols] = dpre
    taps = [
        jnp.sum(dpre * ext[LEAD - 3 + k : LEAD - 3 + k + SPAN, cols], axis=0, keepdims=True) for k in range(CONV)
    ]
    mine = w[0:1, cols] * pad[11 : 11 + SPAN, cols]
    ahead = w[0:1, cols] * pad[3:11, cols]
    for k in range(1, CONV):
        mine = mine + w[k : k + 1, cols] * pad[11 - k : 11 - k + SPAN, cols]
        ahead = ahead + w[k : k + 1, cols] * pad[3 - k : 11 - k, cols]
    return mine, ahead, taps


def clear_pad(pad):
    pad[0:8, :] = jnp.zeros((8, pad.shape[1]), F32)
    pad[8 + SPAN : 16 + SPAN, :] = jnp.zeros((8, pad.shape[1]), F32)


def halves(core, full, keep, give):
    keep[...] = full[pl.ds(pl.multiple_of(core * HALF, HALF), HALF), :]
    give[0:HALF, :] = full[pl.ds(pl.multiple_of((1 - core) * HALF, HALF), HALF), :]


def unite(core, full, own, got):
    full[pl.ds(pl.multiple_of(core * HALF, HALF), HALF), :] = own[...]
    full[pl.ds(pl.multiple_of((1 - core) * HALF, HALF), HALF), :] = got[...]


def triangle(upper):
    rows = lax.broadcasted_iota(jnp.int32, (SPAN, SPAN), 0)
    cols = lax.broadcasted_iota(jnp.int32, (SPAN, SPAN), 1)
    return rows <= cols if upper else rows >= cols


def steps_kernel(dt, heads, step, cum, ends, skip):
    v = dt[...] + heads[:, 0:1]
    skip[...] = jnp.broadcast_to(heads[:, 2:3], skip.shape)
    step[...] = jnp.maximum(v, 0.0) + jnp.log1p(jnp.exp(-jnp.abs(v)))
    rates = -jnp.exp(heads[:, 1:2]) * step[...]
    cum[...] = dot(rates, jnp.where(triangle(True), 1.0, 0.0))
    ends[...] = jnp.broadcast_to(jnp.exp(jnp.sum(rates, axis=1, keepdims=True)), ends.shape)


def turn_kernel(z, og, gain, zt, ogt, sgt):
    for r in range(PER):
        put(zt, r, z[:, lanes(r)].astype(F32))
        tile = og[:, lanes(r)].astype(F32)
        put(ogt, r, tile)
        put(sgt, r, tile * gain[:, lanes(r)])


def state_kernel(core, x, hx, b, hb, wx, wb, step, cum, ends, xt, zs, bc, keep, give, ext, extb, full):
    extend(ext, x, hx)
    extend(extb, b, hb)
    for g in range(GROUPS):
        pre = conv_tile(extb, wb, lanes(g))
        bc[:, lanes(g)] = pre * sigmoid(pre)
    for r in range(PER):
        pre = conv_tile(ext, wx, lanes(r))
        put(xt, r, pre * sigmoid(pre))
    scale = jnp.exp(-cum[...]) * step[...]
    for g in range(GROUPS):
        zg = xt[group(g), :] * heads_out(scale, g)
        zs[group(g), :] = zg
        full[group(g), :] = heads_out(ends[...], g) * dot(zg, bc[:, lanes(g)])
    halves(core[0], full, keep, give)
    give[HALF : HALF + LOCAL, :] = ends[...]


def local_kernel(c, hc, wc, bc, xt, zs, cum, skip, cc, mt, y, extc):
    extend(extc, c, hc)
    alpha = jnp.exp(cum[...])
    causal = triangle(True)
    for g in range(GROUPS):
        pre = conv_tile(extc, wc, lanes(g))
        cg = pre * sigmoid(pre)
        cc[:, lanes(g)] = cg
        m = jnp.where(causal, dot(bc[:, lanes(g)], cg, 1, 1), 0.0)
        mt[lanes(g), :] = m
        y[group(g), :] = heads_out(alpha, g) * dot(zs[group(g), :], m) + heads_out(skip[...], g) * xt[group(g), :]


def output_kernel(core, own, got, cc, y1, cum, zt, sgt, full, y, sums):
    unite(core[0], full, own, got)
    alpha = jnp.exp(cum[...])
    for g in range(GROUPS):
        yg = y1[group(g), :] + heads_out(alpha, g) * dot(full[group(g), :], cc[:, lanes(g)], 1, 1)
        y[group(g), :] = yg
        z = zt[group(g), :]
        gated = yg * z * sigmoid(z)
        sums[g : g + 1, :] = jnp.sum(gated * gated, axis=0, keepdims=True)
        sums[GROUPS + g : GROUPS + g + 1, :] = jnp.sum(sgt[group(g), :] * gated, axis=0, keepdims=True)


def gate_kernel(core, sums, y, zt, sgt, cum, cc, keep, give, dy, dg, full):
    alpha = jnp.exp(cum[...])
    for g in range(GROUPS):
        inv = lax.rsqrt(sums[g : g + 1, :] / GROUP_WIDTH + EPSILON)
        fix = inv * inv * inv * sums[GROUPS + g : GROUPS + g + 1, :] / GROUP_WIDTH
        z = zt[group(g), :]
        act = z * sigmoid(z)
        dgated = inv * sgt[group(g), :] - y[group(g), :] * act * fix
        dg[group(g), :] = dgated
        dyg = dgated * act
        dy[group(g), :] = dyg
        full[group(g), :] = dot(heads_out(alpha, g) * dyg, cc[:, lanes(g)])
    halves(core[0], full, keep, give)


def middle_kernel(
    sums, y, zt, ogt, dy, dg, full, mt, zs, xt, bc, cc, cum, skip, c, hc, wc,
    dz, db, dcum, dskip, gz, early, cpart, extc, padc, dc,
):
    alpha = jnp.exp(cum[...])
    causal = triangle(True)
    slope, shares = [], []
    for g in range(GROUPS):
        z, yg, dyg = zt[group(g), :], y[group(g), :], dy[group(g), :]
        inv = lax.rsqrt(sums[g : g + 1, :] / GROUP_WIDTH + EPSILON)
        slope.append(dg[group(g), :] * yg * silu_slope(z))
        shares.append(ogt[group(g), :] * yg * z * sigmoid(z) * inv)
        heads = slice(g * PER, (g + 1) * PER)
        x = xt[group(g), :]
        passed = heads_in(dyg * x)
        dskip[heads, :] = passed
        dcum[heads, :] = heads_in(dyg * (yg - heads_out(skip[...], g) * x))
        u = heads_out(alpha, g) * dyg
        dz[group(g), :] = dot(u, mt[lanes(g), :], 1, 1)
        dm = jnp.where(causal, dot(zs[group(g), :], u, 0, 0), 0.0)
        dc[:, lanes(g)] = dot(dm, bc[:, lanes(g)], 0, 0) + dot(u, full[group(g), :], 0, 0)
        db[:, lanes(g)] = dot(dm, cc[:, lanes(g)])
    for r in range(PER):
        gz[:, lanes(r)] = take(slope, r).astype(jnp.bfloat16)
        early[16 + r : 17 + r, :] = jnp.sum(take(shares, r), axis=0, keepdims=True)
    extend(extc, c, hc)
    clear_pad(padc)
    for g in range(GROUPS):
        mine, ahead, taps = conv_back_tile(extc, padc, wc, lanes(g), dc[:, lanes(g)])
        cpart[g, 0:SPAN, :] = mine
        cpart[g, SPAN : SPAN + 8, :] = ahead
        for k in range(CONV):
            early[k * GROUPS + g : k * GROUPS + g + 1, :] = taps[k]


def last_kernel(
    core, which, own, got, full, ends, dz1, db1, dcum1, dskip, early, cpart, dy, zs, xt, bc, cum, step, skip, dt, per_head,
    x, hx, wx, b, hb, wb,
    xown, heads, keep, give, packed, ddt, parts, later, ext, extb, pad, padb,
):
    unite(core[0], later, own, got)
    gamma = jnp.exp(-cum[...])
    scale = gamma * step[...]
    clear_pad(pad)
    clear_pad(padb)
    extend(ext, x, hx)
    extend(extb, b, hb)
    dxs, turned, straight = [], [], []
    at_end = lax.broadcasted_iota(jnp.int32, (PER, SPAN), 1) == SPAN - 1
    for g in range(GROUPS):
        here = slice(g * PER, (g + 1) * PER)
        zg, xg = zs[group(g), :], xt[group(g), :]
        d = heads_out(ends[...], g) * later[group(g), :]
        second = dot(d, bc[:, lanes(g)], 1, 1)
        dzg = dz1[group(g), :] + second
        dxs.append(heads_out(scale, g) * dzg + heads_out(skip[...], g) * dy[group(g), :])
        edge = heads_in(zg * second + d * full[group(g), :])
        edge = jnp.sum(edge, axis=1, keepdims=True)
        turned.append(dcum1[here, :] - heads_in(dzg * zg) + jnp.where(at_end, edge, 0.0))
        straight.append(heads_in(dzg * xg))
        dbg = db1[:, lanes(g)] + dot(zg, d, 0, 0)
        mine, ahead, taps = conv_back_tile(extb, padb, wb, lanes(g), dbg)
        parts[g, 0:SPAN, :] = mine
        parts[g, SPAN : 2 * SPAN, :] = cpart[g, 0:SPAN, :]
        parts[g, 2 * SPAN : 2 * SPAN + 8, :] = ahead
        parts[g, 2 * SPAN + 8 : 2 * SPAN + 16, :] = cpart[g, SPAN : SPAN + 8, :]
        for k in range(CONV):
            packed[k * GROUPS + g : k * GROUPS + g + 1, :] = taps[k]
    dlog = dot(jnp.concatenate(turned, axis=0), jnp.where(triangle(False), 1.0, 0.0))
    rate = -jnp.exp(per_head[:, 1:2])
    dstep = jnp.concatenate(straight, axis=0) * gamma + dlog * rate
    draw = dstep * sigmoid(dt[...] + per_head[:, 0:1])
    ddt[...] = draw
    each = jnp.concatenate([draw, dlog * rate * step[...], dskip[...], jnp.zeros((LOCAL, SPAN), F32)], axis=0)
    at = lax.broadcasted_iota(jnp.int32, (SPAN, SPAN), 0)
    to = lax.broadcasted_iota(jnp.int32, (SPAN, SPAN), 1)
    source = to // LOCAL * LOCAL + to % GROUPS * PER + to % LOCAL // GROUPS
    packed[72:80, :] = dot(dot(jnp.ones((8, SPAN), F32), each, 1, 1), jnp.where(at == source, 1.0, 0.0))
    packed[16:32, :] = early[0:16, :]
    packed[64:72, :] = early[16:24, :]
    side = which[0]
    keep[...] = parts[pl.ds(side * 2, 2)]
    give[...] = parts[pl.ds((1 - side) * 2, 2)]
    for r in range(PER):
        mine, ahead, taps = conv_back_tile(ext, pad, wx, lanes(r), take(dxs, r))
        xown[:, lanes(r)] = mine
        heads[8 * r : 8 * r + 8, :] = ahead
        for k in range(CONV):
            packed[32 + k * PER + r : 33 + k * PER + r, :] = taps[k]


def pair_decays(core, pair, lead):
    mine, theirs = pair[0 : LOCAL // 2, :], pair[LOCAL // 2 : LOCAL, :]
    leads = core == lead
    return jnp.where(leads, mine, theirs), jnp.where(leads, theirs, mine), leads


def join_first_kernel(core, keep, got, ends, joint, pair):
    half = LOCAL // 2
    pair[0:half, :] = ends[pl.ds(pl.multiple_of(core[0] * half, half), half), :]
    pair[half:LOCAL, :] = got[pl.ds(pl.multiple_of(HALF + core[0] * half, half), half), :]
    first, second, leads = pair_decays(core[0], pair, 0)
    for h in range(half):
        rows = slice(h * HEAD_DIM, (h + 1) * HEAD_DIM)
        mine, theirs = keep[rows, :], got[rows, :]
        both = second[h : h + 1] * jnp.where(leads, mine, theirs) + jnp.where(leads, theirs, mine)
        for i in range(HEAD_DIM):
            joint[2 * h + i // 16, :, lanes(i % 16)] = both[i : i + 1]
        for i in range(2):
            joint[2 * h + i, :, CHUNK:] = first[h : h + 1] * second[h : h + 1]


def join_again_kernel(core, keep, got, pair, joint):
    _, second, leads = pair_decays(core[0], pair, 1)
    for h in range(LOCAL // 2):
        rows = slice(h * HEAD_DIM, (h + 1) * HEAD_DIM)
        mine, theirs = keep[rows, :], got[rows, :]
        joint[rows, :] = second[h : h + 1] * jnp.where(leads, mine, theirs) + jnp.where(leads, theirs, mine)


def split_kernel(lead, core, ahead, keep, got, pair, own, give):
    first, _, leads = pair_decays(core[0], pair, lead)
    for h in range(LOCAL // 2):
        rows = slice(h * HEAD_DIM, (h + 1) * HEAD_DIM)
        far = ahead[rows, :]
        near = first[h : h + 1] * far + jnp.where(leads, keep[rows, :], got[rows, :])
        own[rows, :] = jnp.where(leads, far, near)
        give[rows, :] = jnp.where(leads, near, far)


def settle_kernel(xown, mine, heads, gx, half):
    last = slice(SPAN - LEAD, SPAN)
    none = jnp.zeros((LEAD - 8, TILE), F32)
    for r in range(PER):
        gx[0 : SPAN - LEAD, lanes(r)] = xown[0 : SPAN - LEAD, lanes(r)].astype(jnp.bfloat16)
        more = jnp.concatenate([none, heads[8 * r : 8 * r + 8, :]], axis=0)
        gx[last, lanes(r)] = (xown[last, lanes(r)] + more).astype(jnp.bfloat16)
    for g in range(2):
        for i in range(2):
            at = 64 + 16 * g + 8 * i
            more = jnp.concatenate([none, heads[at : at + 8, :]], axis=0)
            start, stop = i * SPAN, (i + 1) * SPAN
            half[g, start : stop - LEAD, :] = mine[g, start : stop - LEAD, :].astype(jnp.bfloat16)
            half[g, stop - LEAD : stop, :] = (mine[g, stop - LEAD : stop, :] + more).astype(jnp.bfloat16)


def finish_kernel(which, half, other, bc_taps, packed, gb, gc, tx, tb, tc, tgain, bias, rate, skip):
    left = which[0] == 0
    for g in range(GROUPS):
        first, second = (half, other) if g < 2 else (other, half)
        both = jnp.where(left, first[g % 2].astype(F32), second[g % 2].astype(F32)).astype(jnp.bfloat16)
        gb[:, lanes(g)] = both[0:SPAN]
        gc[:, lanes(g)] = both[SPAN : 2 * SPAN]
    for k in range(CONV):
        for g in range(GROUPS):
            tb[k : k + 1, lanes(g)] = bc_taps[k * GROUPS + g : k * GROUPS + g + 1, :]
            tc[k : k + 1, lanes(g)] = bc_taps[16 + k * GROUPS + g : 17 + k * GROUPS + g, :]
        for r in range(PER):
            tx[k : k + 1, lanes(r)] = packed[32 + k * PER + r : 33 + k * PER + r, :]
    for r in range(PER):
        tgain[:, lanes(r)] = packed[64 + r : 65 + r, :]
    bias[...] = packed[72:73, 0:LOCAL]
    rate[...] = packed[72:73, LOCAL : 2 * LOCAL]
    skip[...] = packed[72:73, 2 * LOCAL : 3 * LOCAL]


def scan_kernel(backward, s, d, o):
    count = s.shape[0]
    at = d.shape[2] - TILE
    carry = [jnp.zeros((1, TILE), F32)] * (CHUNK // TILE)
    for j in range(count):
        j = count - 1 - j if backward else j
        decay = d[j, :, at:]
        for k in range(CHUNK // TILE):
            o[j, :, lanes(k)] = carry[k]
            carry[k] = decay * carry[k] + s[j, :, lanes(k)]


def call(kernel, name, outs, args, scratch=(), scalars=0, flops=20_000_000):
    smem = pl.BlockSpec(memory_space=pltpu.SMEM)
    vmem = pl.BlockSpec(memory_space=pltpu.VMEM)
    return pl.pallas_call(
        kernel,
        out_shape=[jax.ShapeDtypeStruct(s, d) for s, d in outs],
        in_specs=[smem if i < scalars else vmem for i in range(len(args))],
        out_specs=[vmem] * len(outs),
        scratch_shapes=[pltpu.VMEM(s, F32) for s in scratch],
        compiler_params=PARAMS,
        cost_estimate=pl.CostEstimate(flops=flops, bytes_accessed=4 << 20, transcendentals=1 << 18),
        name=name,
    )(*args)


def swap_cores(v):
    return lax.ppermute(v, "core", [(0, 1), (1, 0)])


def alike(size, by):
    return [(i, i ^ by) for i in range(size)]


def over_chips(v):
    return lax.all_to_all(v, "chip", 0, 0)


def fold(x, axis, partner):
    return x + lax.ppermute(x, axis, [(i, partner(i)) for i in range(lax.axis_size(axis))])


def sum_four(x, axis, block=1):
    near, far, last = (
        lax.ppermute(x, axis, [(i, (i // block ^ k) * block + i % block) for i in range(lax.axis_size(axis))])
        for k in range(1, 4)
    )
    return (x + near) + (far + last)


def mirror(within):
    return lambda i: i // within * within + within - 1 - i % within


def by_group(v):
    return v.reshape((PER, GROUPS) + v.shape[1:]).swapaxes(0, 1).reshape(v.shape)


def by_head(v):
    return v.reshape((GROUPS, PER) + v.shape[1:]).swapaxes(0, 1).reshape(v.shape)


def body(
    x_raw, b_raw, c_raw, z_gate, dt_raw, conv_x, conv_b, conv_c, dt_bias, a_log, d_skip, gain, grad_out
):
    size = lax.axis_size(CTX)
    core = lax.axis_index("core")
    side = lax.axis_index("tp") // (lax.axis_size("tp") // 2)
    cores, sides = lax.optimization_barrier((core.reshape(1), side.reshape(1)))
    is_even = core == 0
    t_shape = ((ALL, SPAN), F32)
    bc_shape = ((SPAN, GROUPS * STATE), F32)
    h_shape = ((LOCAL, SPAN), F32)
    tails = jnp.concatenate([v[SPAN - LEAD :] for v in (x_raw, b_raw, c_raw)], axis=1)
    before = lax.ppermute(tails, CTX, [(i, i + 1) for i in range(size - 1)])
    wx, wb = x_raw.shape[1], b_raw.shape[1]
    hx, hb, hc = before[:, :wx], before[:, wx : wx + wb], before[:, wx + wb :]

    dt = by_group(dt_raw.T)
    per_head = by_group(jnp.stack([dt_bias, a_log, d_skip], axis=1))
    step, cum, ends, skip = call(steps_kernel, "steps", [h_shape] * 4, (dt, per_head))
    zt, ogt, sgt = call(turn_kernel, "turn", [t_shape] * 3, (z_gate, grad_out, gain[None]))
    xt, zs, bc, keep, give = call(
        state_kernel,
        "state",
        [t_shape, t_shape, bc_shape, ((HALF, STATE), F32), ((HALF + LOCAL, STATE), F32)],
        (cores, x_raw, hx, b_raw, hb, conv_x, conv_b, step, cum, ends),
        [(LEAD + SPAN, wx), (LEAD + SPAN, wb), (ALL, STATE)],
        scalars=1,
    )
    got = swap_cores(give)
    half_shape = ((HALF, STATE), F32)
    chips = lax.axis_size("chip")
    joint, pair = call(
        join_first_kernel,
        "join",
        [((chips, 1, CHUNK + TILE), F32), h_shape],
        (cores, keep, got, ends),
        scalars=1,
    )
    firsts = over_chips(joint)
    (entering,) = call(
        functools.partial(scan_kernel, False), "block_scan", [((chips, 1, CHUNK), F32)], (firsts, firsts)
    )
    ahead = over_chips(entering).reshape(HALF, STATE)
    enter_own, enter_give = call(
        functools.partial(split_kernel, 0), "split", [half_shape] * 2, (cores, ahead, keep, got, pair), scalars=1
    )
    enter_got = swap_cores(enter_give)

    cc, mt, y1 = call(
        local_kernel,
        "local",
        [bc_shape, ((GROUPS * SPAN, SPAN), F32), t_shape],
        (c_raw, hc, conv_c, bc, xt, zs, cum, skip),
        [(LEAD + SPAN, wb)],
    )
    enter, y, sums = call(
        output_kernel,
        "output",
        [t_shape, t_shape, ((2 * GROUPS, SPAN), F32)],
        (cores, enter_own, enter_got, cc, y1, cum, zt, sgt),
        scalars=1,
    )
    sums = sum_four(sums, "tp")
    keep, give, dy, dg = call(
        gate_kernel,
        "gate",
        [((HALF, STATE), F32)] * 2 + [t_shape, t_shape],
        (cores, sums, y, zt, sgt, cum, cc),
        [(ALL, STATE)],
        scalars=1,
    )
    got = swap_cores(give)
    (joint,) = call(join_again_kernel, "join", [half_shape], (cores, keep, got, pair), scalars=1)
    pieces = over_chips(joint.reshape(chips, 1, CHUNK))
    (leaving,) = call(
        functools.partial(scan_kernel, True), "block_scan", [((chips, 1, CHUNK), F32)], (pieces, firsts)
    )
    ahead = over_chips(leaving).reshape(HALF, STATE)
    later_own, later_give = call(
        functools.partial(split_kernel, 1), "split", [half_shape] * 2, (cores, ahead, keep, got, pair), scalars=1
    )
    later_got = swap_cores(later_give)
    dz, db, dcum, dskip, grad_z, early, cpart = call(
        middle_kernel,
        "middle",
        [t_shape, bc_shape, h_shape, h_shape, ((SPAN, wx), jnp.bfloat16), ((24, TILE), F32)]
        + [((GROUPS, SPAN + 8, TILE), F32)],
        (sums, y, zt, ogt, dy, dg, enter, mt, zs, xt, bc, cc, cum, skip, c_raw, hc, conv_c),
        [(LEAD + SPAN, wb), (LEAD + SPAN, wb), (SPAN, wb)],
    )
    half_parts = ((2, 2 * SPAN + 16, TILE), F32)
    xown, xheads, keep, give, packed, ddt = call(
        last_kernel,
        "last",
        [((SPAN, wx), F32), ((64, TILE), F32), half_parts, half_parts, ((80, TILE), F32), h_shape],
        (cores, sides, later_own, later_got, enter, ends, dz, db, dcum, dskip, early, cpart)
        + (dy, zs, xt, bc, cum, step, skip, dt, per_head, x_raw, hx, conv_x, b_raw, hb, conv_b),
        [(GROUPS, 2 * SPAN + 16, TILE), (ALL, STATE)]
        + [(LEAD + SPAN, wx), (LEAD + SPAN, wb), (LEAD + SPAN, wx), (LEAD + SPAN, wb)],
        scalars=2,
    )
    peers = lax.axis_size("tp")
    across = [(i, peers - 1 - i) for i in range(peers)]
    arrived = lax.ppermute(give, "tp", across)
    packed = packed + swap_cores(packed)
    steps = (mirror(2), lambda i: i ^ 2, mirror(RING))
    packed = fold(packed, "chip", steps[0])
    arrived, packed = lax.optimization_barrier((arrived, packed))
    mine = keep + arrived
    arrived = lax.ppermute(mine, "tp", [(i, i ^ 1) for i in range(peers)])
    packed = fold(packed, "chip", steps[1])
    arrived, packed = lax.optimization_barrier((arrived, packed))
    mine = mine + arrived
    heads = jnp.concatenate([xheads, mine[:, 2 * SPAN :].reshape(32, TILE)], axis=0)
    heads = lax.ppermute(heads, CTX, [(i + 1, i) for i in range(size - 1)])
    packed = fold(packed, "chip", steps[2])
    heads, packed = lax.optimization_barrier((heads, packed))
    packed = sum_four(packed, "chip", RING)
    grad_x_raw, half = call(
        settle_kernel,
        "settle",
        [((SPAN, wx), jnp.bfloat16), ((2, 2 * SPAN, TILE), jnp.bfloat16)],
        (xown, mine, heads),
    )
    other = lax.ppermute(half, "tp", across)
    bc_taps = sum_four(packed[:32], "tp")
    half_bc, each = ((SPAN, wb), jnp.bfloat16), ((1, LOCAL), F32)
    grad_b_raw, grad_c_raw, conv_x_total, conv_b_total, conv_c_total, gain_total, *small = call(
        finish_kernel,
        "finish",
        [half_bc, half_bc, ((CONV, wx), F32), ((CONV, wb), F32), ((CONV, wb), F32), ((1, wx), F32)] + [each] * 3,
        (sides, half, other, bc_taps, packed),
        scalars=1,
    )
    return (
        grad_x_raw,
        grad_b_raw,
        grad_c_raw,
        grad_z,
        by_head(ddt).T,
        conv_x_total,
        conv_b_total,
        conv_c_total,
        *(v.reshape(-1) for v in small),
        gain_total.reshape(-1),
    )


def solution(mesh):
    rows, cols, some = P(CTX, "tp"), P(None, "tp"), P("tp")
    chips, tp = mesh.shape["ctx"] // 2, mesh.shape["tp"]
    mesh = Mesh(mesh.devices.reshape(chips, 2, tp), (*CTX, "tp"))
    return jax.shard_map(
        body,
        mesh=mesh,
        in_specs=(rows, P(CTX, None), P(CTX, None), rows, rows, cols, P(), P(), some, some, some, some, rows),
        out_specs=(rows, P(CTX, None), P(CTX, None), rows, rows, cols, P(), P(), some, some, some, some),
        check_vma=False,
    )
```

```python
import functools

import jax
import jax.numpy as jnp
from jax import lax
from jax.experimental import pallas as pl
from jax.experimental.pallas import tpu as pltpu
from jax.sharding import Mesh, PartitionSpec as P

HEAD_DIM = 32
STATE = 128
GROUPS = 4
CONV = 4
SPAN = 128
TILE = 128
PER = 8
LOCAL = PER * GROUPS
ROWS = PER * HEAD_DIM
ALL = LOCAL * HEAD_DIM
HALF = ALL // 2
CHUNK = 2048
LEAD = 16
GROUP_WIDTH = 1024
EPSILON = 1e-05
F32 = jnp.float32
CTX = ("chip", "core")
RING = 8
PARAMS = pltpu.CompilerParams(vmem_limit_bytes=16 << 20)


def dot(a, b, ca=1, cb=0):
    return lax.dot_general(
        a, b, (((ca,), (cb,)), ((), ())), precision=lax.Precision.HIGHEST, preferred_element_type=F32
    )


def group(g):
    return slice(g * ROWS, (g + 1) * ROWS)


def lanes(r):
    return slice(r * TILE, (r + 1) * TILE)


def spot(g, r):
    return slice(g * ROWS + r * HEAD_DIM, g * ROWS + (r + 1) * HEAD_DIM)


def put(dst, r, tile):
    turned = tile.T
    for g in range(GROUPS):
        dst[spot(g, r), :] = turned[g * HEAD_DIM : (g + 1) * HEAD_DIM]


def take(values, r):
    rows = slice(r * HEAD_DIM, (r + 1) * HEAD_DIM)
    return jnp.concatenate([v[rows] for v in values], axis=0).T


def heads_out(v, g):
    return jnp.concatenate(
        [jnp.broadcast_to(v[g * PER + r : g * PER + r + 1], (HEAD_DIM, v.shape[1])) for r in range(PER)], axis=0
    )


def heads_in(v):
    return jnp.concatenate(
        [jnp.sum(v[r * HEAD_DIM : (r + 1) * HEAD_DIM], axis=0, keepdims=True) for r in range(PER)], axis=0
    )


def sigmoid(v):
    return 1.0 / (1.0 + jnp.exp(-v))


def silu_slope(v):
    s = sigmoid(v)
    return s * (1.0 + v * (1.0 - s))


def extend(ext, raw, before, at):
    ext[0:LEAD, :] = before[:, at : at + ext.shape[1]].astype(F32)
    ext[LEAD : LEAD + SPAN, :] = raw[...].astype(F32)


def group_order():
    to = lax.broadcasted_iota(jnp.int32, (LOCAL, LOCAL), 0)
    at = lax.broadcasted_iota(jnp.int32, (LOCAL, LOCAL), 1)
    return jnp.where(at == to % PER * GROUPS + to // PER, 1.0, 0.0)


def conv_tile(ext, w, cols):
    total = w[0:1, cols] * ext[LEAD - 3 : LEAD - 3 + SPAN, cols]
    for k in range(1, CONV):
        total = total + w[k : k + 1, cols] * ext[LEAD - 3 + k : LEAD - 3 + k + SPAN, cols]
    return total


def conv_back_tile(ext, pad, w, cols, grad):
    dpre = grad * silu_slope(conv_tile(ext, w, cols))
    pad[8 : 8 + SPAN, cols] = dpre
    taps = [
        jnp.sum(dpre * ext[LEAD - 3 + k : LEAD - 3 + k + SPAN, cols], axis=0, keepdims=True) for k in range(CONV)
    ]
    mine = w[0:1, cols] * pad[11 : 11 + SPAN, cols]
    ahead = w[0:1, cols] * pad[3:11, cols]
    for k in range(1, CONV):
        mine = mine + w[k : k + 1, cols] * pad[11 - k : 11 - k + SPAN, cols]
        ahead = ahead + w[k : k + 1, cols] * pad[3 - k : 11 - k, cols]
    return mine, ahead, taps


def clear_pad(pad):
    pad[0:8, :] = jnp.zeros((8, pad.shape[1]), F32)
    pad[8 + SPAN : 16 + SPAN, :] = jnp.zeros((8, pad.shape[1]), F32)


def halves(core, full, keep, give):
    keep[...] = full[pl.ds(pl.multiple_of(core * HALF, HALF), HALF), :]
    give[0:HALF, :] = full[pl.ds(pl.multiple_of((1 - core) * HALF, HALF), HALF), :]


def unite(core, full, own, got):
    full[pl.ds(pl.multiple_of(core * HALF, HALF), HALF), :] = own[...]
    full[pl.ds(pl.multiple_of((1 - core) * HALF, HALF), HALF), :] = got[...]


def triangle(upper):
    rows = lax.broadcasted_iota(jnp.int32, (SPAN, SPAN), 0)
    cols = lax.broadcasted_iota(jnp.int32, (SPAN, SPAN), 1)
    return rows <= cols if upper else rows >= cols


def steps_kernel(raw, bias, alog, d_skip, dt, heads, step, cum, ends, skip):
    order = group_order()
    dt[...] = dot(order, raw[...])
    rows = jnp.concatenate([bias[...], alog[...], d_skip[...], jnp.zeros((5, LOCAL), F32)], axis=0)
    heads[...] = dot(order, rows, 1, 1)
    v = dt[...] + heads[:, 0:1]
    skip[...] = jnp.broadcast_to(heads[:, 2:3], skip.shape)
    step[...] = jnp.maximum(v, 0.0) + jnp.log1p(jnp.exp(-jnp.abs(v)))
    rates = -jnp.exp(heads[:, 1:2]) * step[...]
    cum[...] = dot(rates, jnp.where(triangle(True), 1.0, 0.0))
    ends[...] = jnp.broadcast_to(jnp.exp(jnp.sum(rates, axis=1, keepdims=True)), ends.shape)


def turn_kernel(z, og, gain, zt, ogt, sgt):
    for r in range(PER):
        put(zt, r, z[:, lanes(r)].astype(F32))
        tile = og[:, lanes(r)].astype(F32)
        put(ogt, r, tile)
        put(sgt, r, tile * gain[:, lanes(r)])


def state_kernel(core, x, b, before, wx, wb, step, cum, ends, xt, zs, bc, keep, give, ext, extb, full):
    extend(ext, x, before, 0)
    extend(extb, b, before, x.shape[1])
    for g in range(GROUPS):
        pre = conv_tile(extb, wb, lanes(g))
        bc[:, lanes(g)] = pre * sigmoid(pre)
    for r in range(PER):
        pre = conv_tile(ext, wx, lanes(r))
        put(xt, r, pre * sigmoid(pre))
    scale = jnp.exp(-cum[...]) * step[...]
    for g in range(GROUPS):
        zg = xt[group(g), :] * heads_out(scale, g)
        zs[group(g), :] = zg
        full[group(g), :] = heads_out(ends[...], g) * dot(zg, bc[:, lanes(g)])
    halves(core[0], full, keep, give)
    give[HALF : HALF + LOCAL, :] = ends[...]


def local_kernel(c, before, wc, bc, xt, zs, cum, skip, cc, mt, y, extc):
    extend(extc, c, before, before.shape[1] - c.shape[1])
    alpha = jnp.exp(cum[...])
    causal = triangle(True)
    for g in range(GROUPS):
        pre = conv_tile(extc, wc, lanes(g))
        cg = pre * sigmoid(pre)
        cc[:, lanes(g)] = cg
        m = jnp.where(causal, dot(bc[:, lanes(g)], cg, 1, 1), 0.0)
        mt[lanes(g), :] = m
        y[group(g), :] = heads_out(alpha, g) * dot(zs[group(g), :], m) + heads_out(skip[...], g) * xt[group(g), :]


def output_kernel(core, own, got, cc, y1, cum, zt, sgt, full, y, sums):
    unite(core[0], full, own, got)
    alpha = jnp.exp(cum[...])
    for g in range(GROUPS):
        yg = y1[group(g), :] + heads_out(alpha, g) * dot(full[group(g), :], cc[:, lanes(g)], 1, 1)
        y[group(g), :] = yg
        z = zt[group(g), :]
        gated = yg * z * sigmoid(z)
        sums[g : g + 1, :] = jnp.sum(gated * gated, axis=0, keepdims=True)
        sums[GROUPS + g : GROUPS + g + 1, :] = jnp.sum(sgt[group(g), :] * gated, axis=0, keepdims=True)


def gate_kernel(core, sums, y, zt, sgt, cum, cc, keep, give, dy, dg, full):
    alpha = jnp.exp(cum[...])
    for g in range(GROUPS):
        inv = lax.rsqrt(sums[g : g + 1, :] / GROUP_WIDTH + EPSILON)
        fix = inv * inv * inv * sums[GROUPS + g : GROUPS + g + 1, :] / GROUP_WIDTH
        z = zt[group(g), :]
        act = z * sigmoid(z)
        dgated = inv * sgt[group(g), :] - y[group(g), :] * act * fix
        dg[group(g), :] = dgated
        dyg = dgated * act
        dy[group(g), :] = dyg
        full[group(g), :] = dot(heads_out(alpha, g) * dyg, cc[:, lanes(g)])
    halves(core[0], full, keep, give)


def middle_kernel(
    sums, y, zt, ogt, dy, dg, full, mt, zs, xt, bc, cc, cum, skip, c, before, wc,
    dz, db, dcum, dskip, gz, early, cpart, extc, padc, dc,
):
    alpha = jnp.exp(cum[...])
    causal = triangle(True)
    slope, shares = [], []
    for g in range(GROUPS):
        z, yg, dyg = zt[group(g), :], y[group(g), :], dy[group(g), :]
        inv = lax.rsqrt(sums[g : g + 1, :] / GROUP_WIDTH + EPSILON)
        slope.append(dg[group(g), :] * yg * silu_slope(z))
        shares.append(ogt[group(g), :] * yg * z * sigmoid(z) * inv)
        heads = slice(g * PER, (g + 1) * PER)
        x = xt[group(g), :]
        passed = heads_in(dyg * x)
        dskip[heads, :] = passed
        dcum[heads, :] = heads_in(dyg * (yg - heads_out(skip[...], g) * x))
        u = heads_out(alpha, g) * dyg
        dz[group(g), :] = dot(u, mt[lanes(g), :], 1, 1)
        dm = jnp.where(causal, dot(zs[group(g), :], u, 0, 0), 0.0)
        dc[:, lanes(g)] = dot(dm, bc[:, lanes(g)], 0, 0) + dot(u, full[group(g), :], 0, 0)
        db[:, lanes(g)] = dot(dm, cc[:, lanes(g)])
    for r in range(PER):
        gz[:, lanes(r)] = take(slope, r).astype(jnp.bfloat16)
        early[16 + r : 17 + r, :] = jnp.sum(take(shares, r), axis=0, keepdims=True)
    extend(extc, c, before, before.shape[1] - c.shape[1])
    clear_pad(padc)
    for g in range(GROUPS):
        mine, ahead, taps = conv_back_tile(extc, padc, wc, lanes(g), dc[:, lanes(g)])
        cpart[g, 0:SPAN, :] = mine
        cpart[g, SPAN : SPAN + 8, :] = ahead
        for k in range(CONV):
            early[k * GROUPS + g : k * GROUPS + g + 1, :] = taps[k]


def last_kernel(
    core, which, own, got, full, ends, dz1, db1, dcum1, dskip, early, cpart, dy, zs, xt, bc, cum, step, skip, dt, per_head,
    x, wx, b, wb, before,
    xown, heads, keep, give, packed, ddt, parts, later, ext, extb, pad, padb,
):
    unite(core[0], later, own, got)
    gamma = jnp.exp(-cum[...])
    scale = gamma * step[...]
    clear_pad(pad)
    clear_pad(padb)
    extend(ext, x, before, 0)
    extend(extb, b, before, x.shape[1])
    dxs, turned, straight = [], [], []
    at_end = lax.broadcasted_iota(jnp.int32, (PER, SPAN), 1) == SPAN - 1
    for g in range(GROUPS):
        here = slice(g * PER, (g + 1) * PER)
        zg, xg = zs[group(g), :], xt[group(g), :]
        d = heads_out(ends[...], g) * later[group(g), :]
        second = dot(d, bc[:, lanes(g)], 1, 1)
        dzg = dz1[group(g), :] + second
        dxs.append(heads_out(scale, g) * dzg + heads_out(skip[...], g) * dy[group(g), :])
        edge = heads_in(zg * second + d * full[group(g), :])
        edge = jnp.sum(edge, axis=1, keepdims=True)
        turned.append(dcum1[here, :] - heads_in(dzg * zg) + jnp.where(at_end, edge, 0.0))
        straight.append(heads_in(dzg * xg))
        dbg = db1[:, lanes(g)] + dot(zg, d, 0, 0)
        mine, ahead, taps = conv_back_tile(extb, padb, wb, lanes(g), dbg)
        parts[g, 0:SPAN, :] = mine
        parts[g, SPAN : 2 * SPAN, :] = cpart[g, 0:SPAN, :]
        parts[g, 2 * SPAN : 2 * SPAN + 8, :] = ahead
        parts[g, 2 * SPAN + 8 : 2 * SPAN + 16, :] = cpart[g, SPAN : SPAN + 8, :]
        for k in range(CONV):
            packed[k * GROUPS + g : k * GROUPS + g + 1, :] = taps[k]
    dlog = dot(jnp.concatenate(turned, axis=0), jnp.where(triangle(False), 1.0, 0.0))
    rate = -jnp.exp(per_head[:, 1:2])
    dstep = jnp.concatenate(straight, axis=0) * gamma + dlog * rate
    draw = dstep * sigmoid(dt[...] + per_head[:, 0:1])
    ddt[...] = dot(group_order(), draw, 0, 0)
    each = jnp.concatenate([draw, dlog * rate * step[...], dskip[...], jnp.zeros((LOCAL, SPAN), F32)], axis=0)
    at = lax.broadcasted_iota(jnp.int32, (SPAN, SPAN), 0)
    to = lax.broadcasted_iota(jnp.int32, (SPAN, SPAN), 1)
    source = to // LOCAL * LOCAL + to % GROUPS * PER + to % LOCAL // GROUPS
    packed[72:80, :] = dot(dot(jnp.ones((8, SPAN), F32), each, 1, 1), jnp.where(at == source, 1.0, 0.0))
    packed[16:32, :] = early[0:16, :]
    packed[64:72, :] = early[16:24, :]
    side = which[0]
    keep[...] = parts[pl.ds(side * 2, 2)]
    give[...] = parts[pl.ds((1 - side) * 2, 2)]
    for r in range(PER):
        mine, ahead, taps = conv_back_tile(ext, pad, wx, lanes(r), take(dxs, r))
        xown[:, lanes(r)] = mine
        heads[8 * r : 8 * r + 8, :] = ahead
        for k in range(CONV):
            packed[32 + k * PER + r : 33 + k * PER + r, :] = taps[k]


def pair_decays(core, pair, lead):
    mine, theirs = pair[0 : LOCAL // 2, :], pair[LOCAL // 2 : LOCAL, :]
    leads = core == lead
    return jnp.where(leads, mine, theirs), jnp.where(leads, theirs, mine), leads


def join_first_kernel(core, keep, got, ends, joint, pair):
    half = LOCAL // 2
    pair[0:half, :] = ends[pl.ds(pl.multiple_of(core[0] * half, half), half), :]
    pair[half:LOCAL, :] = got[pl.ds(pl.multiple_of(HALF + core[0] * half, half), half), :]
    first, second, leads = pair_decays(core[0], pair, 0)
    for h in range(half):
        rows = slice(h * HEAD_DIM, (h + 1) * HEAD_DIM)
        mine, theirs = keep[rows, :], got[rows, :]
        both = second[h : h + 1] * jnp.where(leads, mine, theirs) + jnp.where(leads, theirs, mine)
        for i in range(HEAD_DIM):
            joint[2 * h + i // 16, :, lanes(i % 16)] = both[i : i + 1]
        for i in range(2):
            joint[2 * h + i, :, CHUNK:] = first[h : h + 1] * second[h : h + 1]


def join_again_kernel(core, keep, got, pair, joint):
    _, second, leads = pair_decays(core[0], pair, 1)
    for h in range(LOCAL // 2):
        rows = slice(h * HEAD_DIM, (h + 1) * HEAD_DIM)
        mine, theirs = keep[rows, :], got[rows, :]
        joint[rows, :] = second[h : h + 1] * jnp.where(leads, mine, theirs) + jnp.where(leads, theirs, mine)


def split_kernel(lead, core, ahead, keep, got, pair, own, give):
    first, _, leads = pair_decays(core[0], pair, lead)
    for h in range(LOCAL // 2):
        rows = slice(h * HEAD_DIM, (h + 1) * HEAD_DIM)
        far = ahead[rows, :]
        near = first[h : h + 1] * far + jnp.where(leads, keep[rows, :], got[rows, :])
        own[rows, :] = jnp.where(leads, far, near)
        give[rows, :] = jnp.where(leads, near, far)


def settle_kernel(xown, mine, heads, gx, half):
    last = slice(SPAN - LEAD, SPAN)
    none = jnp.zeros((LEAD - 8, TILE), F32)
    for r in range(PER):
        gx[0 : SPAN - LEAD, lanes(r)] = xown[0 : SPAN - LEAD, lanes(r)].astype(jnp.bfloat16)
        more = jnp.concatenate([none, heads[8 * r : 8 * r + 8, :]], axis=0)
        gx[last, lanes(r)] = (xown[last, lanes(r)] + more).astype(jnp.bfloat16)
    for g in range(2):
        for i in range(2):
            at = 64 + 16 * g + 8 * i
            more = jnp.concatenate([none, heads[at : at + 8, :]], axis=0)
            start, stop = i * SPAN, (i + 1) * SPAN
            half[g, start : stop - LEAD, :] = mine[g, start : stop - LEAD, :].astype(jnp.bfloat16)
            half[g, stop - LEAD : stop, :] = (mine[g, stop - LEAD : stop, :] + more).astype(jnp.bfloat16)


def finish_kernel(which, half, other, bc_taps, packed, gb, gc, tx, tb, tc, tgain, bias, rate, skip):
    left = which[0] == 0
    for g in range(GROUPS):
        first, second = (half, other) if g < 2 else (other, half)
        both = jnp.where(left, first[g % 2].astype(F32), second[g % 2].astype(F32)).astype(jnp.bfloat16)
        gb[:, lanes(g)] = both[0:SPAN]
        gc[:, lanes(g)] = both[SPAN : 2 * SPAN]
    for k in range(CONV):
        for g in range(GROUPS):
            tb[k : k + 1, lanes(g)] = bc_taps[k * GROUPS + g : k * GROUPS + g + 1, :]
            tc[k : k + 1, lanes(g)] = bc_taps[16 + k * GROUPS + g : 17 + k * GROUPS + g, :]
        for r in range(PER):
            tx[k : k + 1, lanes(r)] = packed[32 + k * PER + r : 33 + k * PER + r, :]
    for r in range(PER):
        tgain[:, lanes(r)] = packed[64 + r : 65 + r, :]
    bias[...] = packed[72:73, 0:LOCAL]
    rate[...] = packed[72:73, LOCAL : 2 * LOCAL]
    skip[...] = packed[72:73, 2 * LOCAL : 3 * LOCAL]


def scan_kernel(backward, s, d, o):
    count = s.shape[0]
    at = d.shape[2] - TILE
    carry = [jnp.zeros((1, TILE), F32)] * (CHUNK // TILE)
    for j in range(count):
        j = count - 1 - j if backward else j
        decay = d[j, :, at:]
        for k in range(CHUNK // TILE):
            o[j, :, lanes(k)] = carry[k]
            carry[k] = decay * carry[k] + s[j, :, lanes(k)]


def call(kernel, name, outs, args, scratch=(), scalars=0, flops=20_000_000):
    smem = pl.BlockSpec(memory_space=pltpu.SMEM)
    vmem = pl.BlockSpec(memory_space=pltpu.VMEM)
    return pl.pallas_call(
        kernel,
        out_shape=[jax.ShapeDtypeStruct(s, d) for s, d in outs],
        in_specs=[smem if i < scalars else vmem for i in range(len(args))],
        out_specs=[vmem] * len(outs),
        scratch_shapes=[pltpu.VMEM(s, F32) for s in scratch],
        compiler_params=PARAMS,
        cost_estimate=pl.CostEstimate(flops=flops, bytes_accessed=4 << 20, transcendentals=1 << 18),
        name=name,
    )(*args)


def swap_cores(v):
    return lax.ppermute(v, "core", [(0, 1), (1, 0)])


def alike(size, by):
    return [(i, i ^ by) for i in range(size)]


def over_chips(v):
    return lax.all_to_all(v, "chip", 0, 0)


def fold(x, axis, partner):
    return x + lax.ppermute(x, axis, [(i, partner(i)) for i in range(lax.axis_size(axis))])


def sum_four(x, axis, block=1):
    near, far, last = (
        lax.ppermute(x, axis, [(i, (i // block ^ k) * block + i % block) for i in range(lax.axis_size(axis))])
        for k in range(1, 4)
    )
    return (x + near) + (far + last)


def mirror(within):
    return lambda i: i // within * within + within - 1 - i % within


def body(
    x_raw, b_raw, c_raw, z_gate, dt_raw, conv_x, conv_b, conv_c, dt_bias, a_log, d_skip, gain, grad_out
):
    size = lax.axis_size(CTX)
    core = lax.axis_index("core")
    side = lax.axis_index("tp") // (lax.axis_size("tp") // 2)
    cores, sides = lax.optimization_barrier((core.reshape(1), side.reshape(1)))
    is_even = core == 0
    t_shape = ((ALL, SPAN), F32)
    bc_shape = ((SPAN, GROUPS * STATE), F32)
    h_shape = ((LOCAL, SPAN), F32)
    tails = jnp.concatenate([v[SPAN - LEAD :] for v in (x_raw, b_raw, c_raw)], axis=1)
    before = lax.ppermute(tails, CTX, [(i, i + 1) for i in range(size - 1)])
    wx, wb = x_raw.shape[1], b_raw.shape[1]

    dt, per_head, step, cum, ends, skip = call(
        steps_kernel,
        "steps",
        [h_shape, ((LOCAL, 8), F32)] + [h_shape] * 4,
        (dt_raw.T, dt_bias[None], a_log[None], d_skip[None]),
    )
    zt, ogt, sgt = call(turn_kernel, "turn", [t_shape] * 3, (z_gate, grad_out, gain[None]))
    xt, zs, bc, keep, give = call(
        state_kernel,
        "state",
        [t_shape, t_shape, bc_shape, ((HALF, STATE), F32), ((HALF + LOCAL, STATE), F32)],
        (cores, x_raw, b_raw, before, conv_x, conv_b, step, cum, ends),
        [(LEAD + SPAN, wx), (LEAD + SPAN, wb), (ALL, STATE)],
        scalars=1,
    )
    got = swap_cores(give)
    half_shape = ((HALF, STATE), F32)
    chips = lax.axis_size("chip")
    joint, pair = call(
        join_first_kernel,
        "join",
        [((chips, 1, CHUNK + TILE), F32), h_shape],
        (cores, keep, got, ends),
        scalars=1,
    )
    firsts = over_chips(joint)
    (entering,) = call(
        functools.partial(scan_kernel, False), "block_scan", [((chips, 1, CHUNK), F32)], (firsts, firsts)
    )
    ahead = over_chips(entering).reshape(HALF, STATE)
    enter_own, enter_give = call(
        functools.partial(split_kernel, 0), "split", [half_shape] * 2, (cores, ahead, keep, got, pair), scalars=1
    )
    enter_got = swap_cores(enter_give)

    cc, mt, y1 = call(
        local_kernel,
        "local",
        [bc_shape, ((GROUPS * SPAN, SPAN), F32), t_shape],
        (c_raw, before, conv_c, bc, xt, zs, cum, skip),
        [(LEAD + SPAN, wb)],
    )
    enter, y, sums = call(
        output_kernel,
        "output",
        [t_shape, t_shape, ((2 * GROUPS, SPAN), F32)],
        (cores, enter_own, enter_got, cc, y1, cum, zt, sgt),
        scalars=1,
    )
    sums = sum_four(sums, "tp")
    keep, give, dy, dg = call(
        gate_kernel,
        "gate",
        [((HALF, STATE), F32)] * 2 + [t_shape, t_shape],
        (cores, sums, y, zt, sgt, cum, cc),
        [(ALL, STATE)],
        scalars=1,
    )
    got = swap_cores(give)
    (joint,) = call(join_again_kernel, "join", [half_shape], (cores, keep, got, pair), scalars=1)
    pieces = over_chips(joint.reshape(chips, 1, CHUNK))
    (leaving,) = call(
        functools.partial(scan_kernel, True), "block_scan", [((chips, 1, CHUNK), F32)], (pieces, firsts)
    )
    ahead = over_chips(leaving).reshape(HALF, STATE)
    later_own, later_give = call(
        functools.partial(split_kernel, 1), "split", [half_shape] * 2, (cores, ahead, keep, got, pair), scalars=1
    )
    later_got = swap_cores(later_give)
    dz, db, dcum, dskip, grad_z, early, cpart = call(
        middle_kernel,
        "middle",
        [t_shape, bc_shape, h_shape, h_shape, ((SPAN, wx), jnp.bfloat16), ((24, TILE), F32)]
        + [((GROUPS, SPAN + 8, TILE), F32)],
        (sums, y, zt, ogt, dy, dg, enter, mt, zs, xt, bc, cc, cum, skip, c_raw, before, conv_c),
        [(LEAD + SPAN, wb), (LEAD + SPAN, wb), (SPAN, wb)],
    )
    half_parts = ((2, 2 * SPAN + 16, TILE), F32)
    xown, xheads, keep, give, packed, ddt = call(
        last_kernel,
        "last",
        [((SPAN, wx), F32), ((64, TILE), F32), half_parts, half_parts, ((80, TILE), F32), h_shape],
        (cores, sides, later_own, later_got, enter, ends, dz, db, dcum, dskip, early, cpart)
        + (dy, zs, xt, bc, cum, step, skip, dt, per_head, x_raw, conv_x, b_raw, conv_b, before),
        [(GROUPS, 2 * SPAN + 16, TILE), (ALL, STATE)]
        + [(LEAD + SPAN, wx), (LEAD + SPAN, wb), (LEAD + SPAN, wx), (LEAD + SPAN, wb)],
        scalars=2,
    )
    peers = lax.axis_size("tp")
    across = [(i, peers - 1 - i) for i in range(peers)]
    arrived = lax.ppermute(give, "tp", across)
    packed = packed + swap_cores(packed)
    packed = fold(packed, "chip", mirror(2))
    packed = fold(packed, "chip", lambda i: i ^ 2)
    arrived, packed = lax.optimization_barrier((arrived, packed))
    mine = keep + arrived
    arrived = lax.ppermute(mine, "tp", [(i, i ^ 1) for i in range(peers)])
    packed = fold(packed, "chip", mirror(RING))
    arrived, packed = lax.optimization_barrier((arrived, packed))
    mine = mine + arrived
    heads = jnp.concatenate([xheads, mine[:, 2 * SPAN :].reshape(32, TILE)], axis=0)
    heads = lax.ppermute(heads, CTX, [(i + 1, i) for i in range(size - 1)])
    packed = sum_four(packed, "chip", RING)
    heads, packed = lax.optimization_barrier((heads, packed))
    grad_x_raw, half = call(
        settle_kernel,
        "settle",
        [((SPAN, wx), jnp.bfloat16), ((2, 2 * SPAN, TILE), jnp.bfloat16)],
        (xown, mine, heads),
    )
    half, packed = lax.optimization_barrier((half, packed))
    other = lax.ppermute(half, "tp", across)
    bc_taps = sum_four(packed[:32], "tp")
    half_bc, each = ((SPAN, wb), jnp.bfloat16), ((1, LOCAL), F32)
    grad_b_raw, grad_c_raw, conv_x_total, conv_b_total, conv_c_total, gain_total, *small = call(
        finish_kernel,
        "finish",
        [half_bc, half_bc, ((CONV, wx), F32), ((CONV, wb), F32), ((CONV, wb), F32), ((1, wx), F32)] + [each] * 3,
        (sides, half, other, bc_taps, packed),
        scalars=1,
    )
    return (
        grad_x_raw,
        grad_b_raw,
        grad_c_raw,
        grad_z,
        ddt.T,
        conv_x_total,
        conv_b_total,
        conv_c_total,
        *(v.reshape(-1) for v in small),
        gain_total.reshape(-1),
    )


def solution(mesh):
    rows, cols, some = P(CTX, "tp"), P(None, "tp"), P("tp")
    chips, tp = mesh.shape["ctx"] // 2, mesh.shape["tp"]
    mesh = Mesh(mesh.devices.reshape(chips, 2, tp), (*CTX, "tp"))
    return jax.shard_map(
        body,
        mesh=mesh,
        in_specs=(rows, P(CTX, None), P(CTX, None), rows, rows, cols, P(), P(), some, some, some, some, rows),
        out_specs=(rows, P(CTX, None), P(CTX, None), rows, rows, cols, P(), P(), some, some, some, some),
        check_vma=False,
    )
```

```python
import functools

import jax
import jax.numpy as jnp
from jax import lax
from jax.experimental import pallas as pl
from jax.experimental.pallas import tpu as pltpu
from jax.sharding import Mesh, PartitionSpec as P

HEAD_DIM = 32
STATE = 128
GROUPS = 4
CONV = 4
SPAN = 128
TILE = 128
PER = 8
LOCAL = PER * GROUPS
ROWS = PER * HEAD_DIM
ALL = LOCAL * HEAD_DIM
HALF = ALL // 2
CHUNK = 2048
LEAD = 16
GROUP_WIDTH = 1024
EPSILON = 1e-05
F32 = jnp.float32
CTX = ("chip", "core")
RING = 8
PARAMS = pltpu.CompilerParams(vmem_limit_bytes=16 << 20)


def dot(a, b, ca=1, cb=0):
    return lax.dot_general(
        a, b, (((ca,), (cb,)), ((), ())), precision=lax.Precision.HIGHEST, preferred_element_type=F32
    )


def group(g):
    return slice(g * ROWS, (g + 1) * ROWS)


def lanes(r):
    return slice(r * TILE, (r + 1) * TILE)


def spot(g, r):
    return slice(g * ROWS + r * HEAD_DIM, g * ROWS + (r + 1) * HEAD_DIM)


def put(dst, r, tile):
    turned = tile.T
    for g in range(GROUPS):
        dst[spot(g, r), :] = turned[g * HEAD_DIM : (g + 1) * HEAD_DIM]


def take(values, r):
    rows = slice(r * HEAD_DIM, (r + 1) * HEAD_DIM)
    return jnp.concatenate([v[rows] for v in values], axis=0).T


def heads_out(v, g):
    return jnp.concatenate(
        [jnp.broadcast_to(v[g * PER + r : g * PER + r + 1], (HEAD_DIM, v.shape[1])) for r in range(PER)], axis=0
    )


def heads_in(v):
    return jnp.concatenate(
        [jnp.sum(v[r * HEAD_DIM : (r + 1) * HEAD_DIM], axis=0, keepdims=True) for r in range(PER)], axis=0
    )


def sigmoid(v):
    return 1.0 / (1.0 + jnp.exp(-v))


def silu_slope(v):
    s = sigmoid(v)
    return s * (1.0 + v * (1.0 - s))


def extend(ext, raw, before, at):
    ext[0:LEAD, :] = before[:, at : at + ext.shape[1]].astype(F32)
    ext[LEAD : LEAD + SPAN, :] = raw[...].astype(F32)


def group_order():
    to = lax.broadcasted_iota(jnp.int32, (LOCAL, LOCAL), 0)
    at = lax.broadcasted_iota(jnp.int32, (LOCAL, LOCAL), 1)
    return jnp.where(at == to % PER * GROUPS + to // PER, 1.0, 0.0)


def conv_tile(ext, w, cols):
    total = w[0:1, cols] * ext[LEAD - 3 : LEAD - 3 + SPAN, cols]
    for k in range(1, CONV):
        total = total + w[k : k + 1, cols] * ext[LEAD - 3 + k : LEAD - 3 + k + SPAN, cols]
    return total


def conv_back_tile(ext, pad, w, cols, grad):
    dpre = grad * silu_slope(conv_tile(ext, w, cols))
    pad[8 : 8 + SPAN, cols] = dpre
    taps = [
        jnp.sum(dpre * ext[LEAD - 3 + k : LEAD - 3 + k + SPAN, cols], axis=0, keepdims=True) for k in range(CONV)
    ]
    mine = w[0:1, cols] * pad[11 : 11 + SPAN, cols]
    ahead = w[0:1, cols] * pad[3:11, cols]
    for k in range(1, CONV):
        mine = mine + w[k : k + 1, cols] * pad[11 - k : 11 - k + SPAN, cols]
        ahead = ahead + w[k : k + 1, cols] * pad[3 - k : 11 - k, cols]
    return mine, ahead, taps


def clear_pad(pad):
    pad[0:8, :] = jnp.zeros((8, pad.shape[1]), F32)
    pad[8 + SPAN : 16 + SPAN, :] = jnp.zeros((8, pad.shape[1]), F32)


def halves(core, full, keep, give):
    keep[...] = full[pl.ds(pl.multiple_of(core * HALF, HALF), HALF), :]
    give[0:HALF, :] = full[pl.ds(pl.multiple_of((1 - core) * HALF, HALF), HALF), :]


def unite(core, full, own, got):
    full[pl.ds(pl.multiple_of(core * HALF, HALF), HALF), :] = own[...]
    full[pl.ds(pl.multiple_of((1 - core) * HALF, HALF), HALF), :] = got[...]


def triangle(upper):
    rows = lax.broadcasted_iota(jnp.int32, (SPAN, SPAN), 0)
    cols = lax.broadcasted_iota(jnp.int32, (SPAN, SPAN), 1)
    return rows <= cols if upper else rows >= cols


def steps_kernel(raw, bias, alog, d_skip, dt, heads, step, cum, ends, skip):
    order = group_order()
    dt[...] = dot(order, raw[...])
    rows = jnp.concatenate([bias[...], alog[...], d_skip[...], jnp.zeros((5, LOCAL), F32)], axis=0)
    heads[...] = dot(order, rows, 1, 1)
    v = dt[...] + heads[:, 0:1]
    skip[...] = jnp.broadcast_to(heads[:, 2:3], skip.shape)
    step[...] = jnp.maximum(v, 0.0) + jnp.log1p(jnp.exp(-jnp.abs(v)))
    rates = -jnp.exp(heads[:, 1:2]) * step[...]
    cum[...] = dot(rates, jnp.where(triangle(True), 1.0, 0.0))
    ends[...] = jnp.broadcast_to(jnp.exp(jnp.sum(rates, axis=1, keepdims=True)), ends.shape)


def turn_kernel(z, og, gain, zt, ogt, sgt):
    for r in range(PER):
        put(zt, r, z[:, lanes(r)].astype(F32))
        tile = og[:, lanes(r)].astype(F32)
        put(ogt, r, tile)
        put(sgt, r, tile * gain[:, lanes(r)])


def state_kernel(core, x, b, before, wx, wb, step, cum, ends, xt, zs, bc, keep, give, ext, extb, full):
    extend(ext, x, before, 0)
    extend(extb, b, before, x.shape[1])
    for g in range(GROUPS):
        pre = conv_tile(extb, wb, lanes(g))
        bc[:, lanes(g)] = pre * sigmoid(pre)
    for r in range(PER):
        pre = conv_tile(ext, wx, lanes(r))
        put(xt, r, pre * sigmoid(pre))
    scale = jnp.exp(-cum[...]) * step[...]
    for g in range(GROUPS):
        zg = xt[group(g), :] * heads_out(scale, g)
        zs[group(g), :] = zg
        full[group(g), :] = heads_out(ends[...], g) * dot(zg, bc[:, lanes(g)])
    halves(core[0], full, keep, give)
    give[HALF : HALF + LOCAL, :] = ends[...]


def local_kernel(c, before, wc, bc, xt, zs, cum, skip, cc, mt, y, extc):
    extend(extc, c, before, before.shape[1] - c.shape[1])
    alpha = jnp.exp(cum[...])
    causal = triangle(True)
    for g in range(GROUPS):
        pre = conv_tile(extc, wc, lanes(g))
        cg = pre * sigmoid(pre)
        cc[:, lanes(g)] = cg
        m = jnp.where(causal, dot(bc[:, lanes(g)], cg, 1, 1), 0.0)
        mt[lanes(g), :] = m
        y[group(g), :] = heads_out(alpha, g) * dot(zs[group(g), :], m) + heads_out(skip[...], g) * xt[group(g), :]


def output_kernel(core, own, got, cc, y1, cum, zt, sgt, full, y, sums):
    unite(core[0], full, own, got)
    alpha = jnp.exp(cum[...])
    for g in range(GROUPS):
        yg = y1[group(g), :] + heads_out(alpha, g) * dot(full[group(g), :], cc[:, lanes(g)], 1, 1)
        y[group(g), :] = yg
        z = zt[group(g), :]
        gated = yg * z * sigmoid(z)
        sums[g : g + 1, :] = jnp.sum(gated * gated, axis=0, keepdims=True)
        sums[GROUPS + g : GROUPS + g + 1, :] = jnp.sum(sgt[group(g), :] * gated, axis=0, keepdims=True)


def gate_kernel(core, sums, y, zt, sgt, cum, cc, keep, give, dy, dg, full):
    alpha = jnp.exp(cum[...])
    for g in range(GROUPS):
        inv = lax.rsqrt(sums[g : g + 1, :] / GROUP_WIDTH + EPSILON)
        fix = inv * inv * inv * sums[GROUPS + g : GROUPS + g + 1, :] / GROUP_WIDTH
        z = zt[group(g), :]
        act = z * sigmoid(z)
        dgated = inv * sgt[group(g), :] - y[group(g), :] * act * fix
        dg[group(g), :] = dgated
        dyg = dgated * act
        dy[group(g), :] = dyg
        full[group(g), :] = dot(heads_out(alpha, g) * dyg, cc[:, lanes(g)])
    halves(core[0], full, keep, give)


def middle_kernel(
    sums, y, zt, ogt, dy, dg, full, mt, zs, xt, bc, cc, cum, skip, c, before, wc,
    dz, db, dcum, dskip, gz, early, cpart, extc, padc, dc,
):
    alpha = jnp.exp(cum[...])
    causal = triangle(True)
    slope, shares = [], []
    for g in range(GROUPS):
        z, yg, dyg = zt[group(g), :], y[group(g), :], dy[group(g), :]
        inv = lax.rsqrt(sums[g : g + 1, :] / GROUP_WIDTH + EPSILON)
        slope.append(dg[group(g), :] * yg * silu_slope(z))
        shares.append(ogt[group(g), :] * yg * z * sigmoid(z) * inv)
        heads = slice(g * PER, (g + 1) * PER)
        x = xt[group(g), :]
        passed = heads_in(dyg * x)
        dskip[heads, :] = passed
        dcum[heads, :] = heads_in(dyg * (yg - heads_out(skip[...], g) * x))
        u = heads_out(alpha, g) * dyg
        dz[group(g), :] = dot(u, mt[lanes(g), :], 1, 1)
        dm = jnp.where(causal, dot(zs[group(g), :], u, 0, 0), 0.0)
        dc[:, lanes(g)] = dot(dm, bc[:, lanes(g)], 0, 0) + dot(u, full[group(g), :], 0, 0)
        db[:, lanes(g)] = dot(dm, cc[:, lanes(g)])
    for r in range(PER):
        gz[:, lanes(r)] = take(slope, r).astype(jnp.bfloat16)
        early[16 + r : 17 + r, :] = jnp.sum(take(shares, r), axis=0, keepdims=True)
    extend(extc, c, before, before.shape[1] - c.shape[1])
    clear_pad(padc)
    for g in range(GROUPS):
        mine, ahead, taps = conv_back_tile(extc, padc, wc, lanes(g), dc[:, lanes(g)])
        cpart[g, 0:SPAN, :] = mine
        cpart[g, SPAN : SPAN + 8, :] = ahead
        for k in range(CONV):
            early[k * GROUPS + g : k * GROUPS + g + 1, :] = taps[k]


def last_kernel(
    core, which, own, got, full, ends, dz1, db1, dcum1, dskip, early, cpart, dy, zs, xt, bc, cum, step, skip, dt, per_head,
    x, wx, b, wb, before,
    xown, heads, keep, give_one, give_two, give_three, packed, ddt, parts, later, ext, extb, pad, padb,
):
    unite(core[0], later, own, got)
    gamma = jnp.exp(-cum[...])
    scale = gamma * step[...]
    clear_pad(pad)
    clear_pad(padb)
    extend(ext, x, before, 0)
    extend(extb, b, before, x.shape[1])
    dxs, turned, straight = [], [], []
    at_end = lax.broadcasted_iota(jnp.int32, (PER, SPAN), 1) == SPAN - 1
    for g in range(GROUPS):
        here = slice(g * PER, (g + 1) * PER)
        zg, xg = zs[group(g), :], xt[group(g), :]
        d = heads_out(ends[...], g) * later[group(g), :]
        second = dot(d, bc[:, lanes(g)], 1, 1)
        dzg = dz1[group(g), :] + second
        dxs.append(heads_out(scale, g) * dzg + heads_out(skip[...], g) * dy[group(g), :])
        edge = heads_in(zg * second + d * full[group(g), :])
        edge = jnp.sum(edge, axis=1, keepdims=True)
        turned.append(dcum1[here, :] - heads_in(dzg * zg) + jnp.where(at_end, edge, 0.0))
        straight.append(heads_in(dzg * xg))
        dbg = db1[:, lanes(g)] + dot(zg, d, 0, 0)
        mine, ahead, taps = conv_back_tile(extb, padb, wb, lanes(g), dbg)
        parts[g, 0:SPAN, :] = mine
        parts[g, SPAN : 2 * SPAN, :] = cpart[g, 0:SPAN, :]
        parts[g, 2 * SPAN : 2 * SPAN + 8, :] = ahead
        parts[g, 2 * SPAN + 8 : 2 * SPAN + 16, :] = cpart[g, SPAN : SPAN + 8, :]
        for k in range(CONV):
            packed[k * GROUPS + g : k * GROUPS + g + 1, :] = taps[k]
    dlog = dot(jnp.concatenate(turned, axis=0), jnp.where(triangle(False), 1.0, 0.0))
    rate = -jnp.exp(per_head[:, 1:2])
    dstep = jnp.concatenate(straight, axis=0) * gamma + dlog * rate
    draw = dstep * sigmoid(dt[...] + per_head[:, 0:1])
    ddt[...] = dot(group_order(), draw, 0, 0)
    each = jnp.concatenate([draw, dlog * rate * step[...], dskip[...], jnp.zeros((LOCAL, SPAN), F32)], axis=0)
    at = lax.broadcasted_iota(jnp.int32, (SPAN, SPAN), 0)
    to = lax.broadcasted_iota(jnp.int32, (SPAN, SPAN), 1)
    source = to // LOCAL * LOCAL + to % GROUPS * PER + to % LOCAL // GROUPS
    packed[72:80, :] = dot(dot(jnp.ones((8, SPAN), F32), each, 1, 1), jnp.where(at == source, 1.0, 0.0))
    packed[16:32, :] = early[0:16, :]
    packed[64:72, :] = early[16:24, :]
    for k, quarter in enumerate((keep, give_one, give_two, give_three)):
        quarter[...] = parts[lax.rem(which[0] + k, GROUPS)]
    for r in range(PER):
        mine, ahead, taps = conv_back_tile(ext, pad, wx, lanes(r), take(dxs, r))
        xown[:, lanes(r)] = mine
        heads[8 * r : 8 * r + 8, :] = ahead
        for k in range(CONV):
            packed[32 + k * PER + r : 33 + k * PER + r, :] = taps[k]


def pair_decays(core, pair, lead):
    mine, theirs = pair[0 : LOCAL // 2, :], pair[LOCAL // 2 : LOCAL, :]
    leads = core == lead
    return jnp.where(leads, mine, theirs), jnp.where(leads, theirs, mine), leads


def join_first_kernel(core, keep, got, ends, joint, pair):
    half = LOCAL // 2
    pair[0:half, :] = ends[pl.ds(pl.multiple_of(core[0] * half, half), half), :]
    pair[half:LOCAL, :] = got[pl.ds(pl.multiple_of(HALF + core[0] * half, half), half), :]
    first, second, leads = pair_decays(core[0], pair, 0)
    for h in range(half):
        rows = slice(h * HEAD_DIM, (h + 1) * HEAD_DIM)
        mine, theirs = keep[rows, :], got[rows, :]
        both = second[h : h + 1] * jnp.where(leads, mine, theirs) + jnp.where(leads, theirs, mine)
        for i in range(HEAD_DIM):
            joint[2 * h + i // 16, :, lanes(i % 16)] = both[i : i + 1]
        for i in range(2):
            joint[2 * h + i, :, CHUNK:] = first[h : h + 1] * second[h : h + 1]


def join_again_kernel(core, keep, got, pair, joint):
    _, second, leads = pair_decays(core[0], pair, 1)
    for h in range(LOCAL // 2):
        rows = slice(h * HEAD_DIM, (h + 1) * HEAD_DIM)
        mine, theirs = keep[rows, :], got[rows, :]
        joint[rows, :] = second[h : h + 1] * jnp.where(leads, mine, theirs) + jnp.where(leads, theirs, mine)


def split_kernel(lead, core, ahead, keep, got, pair, own, give):
    first, _, leads = pair_decays(core[0], pair, lead)
    for h in range(LOCAL // 2):
        rows = slice(h * HEAD_DIM, (h + 1) * HEAD_DIM)
        far = ahead[rows, :]
        near = first[h : h + 1] * far + jnp.where(leads, keep[rows, :], got[rows, :])
        own[rows, :] = jnp.where(leads, far, near)
        give[rows, :] = jnp.where(leads, near, far)


def settle_kernel(xown, mine, heads, gx, quarter):
    last = slice(SPAN - LEAD, SPAN)
    none = jnp.zeros((LEAD - 8, TILE), F32)
    for r in range(PER):
        gx[0 : SPAN - LEAD, lanes(r)] = xown[0 : SPAN - LEAD, lanes(r)].astype(jnp.bfloat16)
        more = jnp.concatenate([none, heads[8 * r : 8 * r + 8, :]], axis=0)
        gx[last, lanes(r)] = (xown[last, lanes(r)] + more).astype(jnp.bfloat16)
    for i in range(2):
        more = jnp.concatenate([none, heads[64 + 8 * i : 72 + 8 * i, :]], axis=0)
        start, stop = i * SPAN, (i + 1) * SPAN
        quarter[start : stop - LEAD, :] = mine[start : stop - LEAD, :].astype(jnp.bfloat16)
        quarter[stop - LEAD : stop, :] = (mine[stop - LEAD : stop, :] + more).astype(jnp.bfloat16)


def finish_kernel(which, own, one, two, three, bc_taps, packed, gb, gc, tx, tb, tc, tgain, bias, rate, skip):
    for k, quarter in enumerate((own, one, two, three)):
        at = lax.rem(which[0] + GROUPS - k, GROUPS)
        cols = pl.ds(pl.multiple_of(at * TILE, TILE), TILE)
        gb[:, cols] = quarter[0:SPAN, :]
        gc[:, cols] = quarter[SPAN : 2 * SPAN, :]
    for k in range(CONV):
        for g in range(GROUPS):
            tb[k : k + 1, lanes(g)] = bc_taps[k * GROUPS + g : k * GROUPS + g + 1, :]
            tc[k : k + 1, lanes(g)] = bc_taps[16 + k * GROUPS + g : 17 + k * GROUPS + g, :]
        for r in range(PER):
            tx[k : k + 1, lanes(r)] = packed[32 + k * PER + r : 33 + k * PER + r, :]
    for r in range(PER):
        tgain[:, lanes(r)] = packed[64 + r : 65 + r, :]
    bias[...] = packed[72:73, 0:LOCAL]
    rate[...] = packed[72:73, LOCAL : 2 * LOCAL]
    skip[...] = packed[72:73, 2 * LOCAL : 3 * LOCAL]


def scan_kernel(backward, s, d, o):
    count = s.shape[0]
    at = d.shape[2] - TILE
    carry = [jnp.zeros((1, TILE), F32)] * (CHUNK // TILE)
    for j in range(count):
        j = count - 1 - j if backward else j
        decay = d[j, :, at:]
        for k in range(CHUNK // TILE):
            o[j, :, lanes(k)] = carry[k]
            carry[k] = decay * carry[k] + s[j, :, lanes(k)]


def call(kernel, name, outs, args, scratch=(), scalars=0, flops=20_000_000):
    smem = pl.BlockSpec(memory_space=pltpu.SMEM)
    vmem = pl.BlockSpec(memory_space=pltpu.VMEM)
    return pl.pallas_call(
        kernel,
        out_shape=[jax.ShapeDtypeStruct(s, d) for s, d in outs],
        in_specs=[smem if i < scalars else vmem for i in range(len(args))],
        out_specs=[vmem] * len(outs),
        scratch_shapes=[pltpu.VMEM(s, F32) for s in scratch],
        compiler_params=PARAMS,
        cost_estimate=pl.CostEstimate(flops=flops, bytes_accessed=4 << 20, transcendentals=1 << 18),
        name=name,
    )(*args)


def swap_cores(v):
    return lax.ppermute(v, "core", [(0, 1), (1, 0)])


def alike(size, by):
    return [(i, i ^ by) for i in range(size)]


def over_chips(v):
    return lax.all_to_all(v, "chip", 0, 0)


def fold(x, axis, partner):
    return x + lax.ppermute(x, axis, [(i, partner(i)) for i in range(lax.axis_size(axis))])


def sum_four(x, axis, one, two):
    near, far, last = (
        lax.ppermute(x, axis, [(i, partner(i)) for i in range(lax.axis_size(axis))])
        for partner in (one, two, lambda i: one(two(i)))
    )
    return (x + near) + (far + last)


def flip(bits):
    return lambda i: i ^ bits


def mirror(within):
    return lambda i: i // within * within + within - 1 - i % within


def body(
    x_raw, b_raw, c_raw, z_gate, dt_raw, conv_x, conv_b, conv_c, dt_bias, a_log, d_skip, gain, grad_out
):
    size = lax.axis_size(CTX)
    core = lax.axis_index("core")
    place = lax.axis_index("tp")
    cores, places = lax.optimization_barrier((core.reshape(1), place.reshape(1)))
    is_even = core == 0
    t_shape = ((ALL, SPAN), F32)
    bc_shape = ((SPAN, GROUPS * STATE), F32)
    h_shape = ((LOCAL, SPAN), F32)
    tails = jnp.concatenate([v[SPAN - LEAD :] for v in (x_raw, b_raw, c_raw)], axis=1)
    before = lax.ppermute(tails, CTX, [(i, i + 1) for i in range(size - 1)])
    wx, wb = x_raw.shape[1], b_raw.shape[1]

    dt, per_head, step, cum, ends, skip = call(
        steps_kernel,
        "steps",
        [h_shape, ((LOCAL, 8), F32)] + [h_shape] * 4,
        (dt_raw.T, dt_bias[None], a_log[None], d_skip[None]),
    )
    zt, ogt, sgt = call(turn_kernel, "turn", [t_shape] * 3, (z_gate, grad_out, gain[None]))
    xt, zs, bc, keep, give = call(
        state_kernel,
        "state",
        [t_shape, t_shape, bc_shape, ((HALF, STATE), F32), ((HALF + LOCAL, STATE), F32)],
        (cores, x_raw, b_raw, before, conv_x, conv_b, step, cum, ends),
        [(LEAD + SPAN, wx), (LEAD + SPAN, wb), (ALL, STATE)],
        scalars=1,
    )
    got = swap_cores(give)
    half_shape = ((HALF, STATE), F32)
    chips = lax.axis_size("chip")
    joint, pair = call(
        join_first_kernel,
        "join",
        [((chips, 1, CHUNK + TILE), F32), h_shape],
        (cores, keep, got, ends),
        scalars=1,
    )
    firsts = over_chips(joint)
    (entering,) = call(
        functools.partial(scan_kernel, False), "block_scan", [((chips, 1, CHUNK), F32)], (firsts, firsts)
    )
    ahead = over_chips(entering).reshape(HALF, STATE)
    enter_own, enter_give = call(
        functools.partial(split_kernel, 0), "split", [half_shape] * 2, (cores, ahead, keep, got, pair), scalars=1
    )
    enter_got = swap_cores(enter_give)

    cc, mt, y1 = call(
        local_kernel,
        "local",
        [bc_shape, ((GROUPS * SPAN, SPAN), F32), t_shape],
        (c_raw, before, conv_c, bc, xt, zs, cum, skip),
        [(LEAD + SPAN, wb)],
    )
    enter, y, sums = call(
        output_kernel,
        "output",
        [t_shape, t_shape, ((2 * GROUPS, SPAN), F32)],
        (cores, enter_own, enter_got, cc, y1, cum, zt, sgt),
        scalars=1,
    )
    sums = sum_four(sums, "tp", flip(1), flip(2))
    keep, give, dy, dg = call(
        gate_kernel,
        "gate",
        [((HALF, STATE), F32)] * 2 + [t_shape, t_shape],
        (cores, sums, y, zt, sgt, cum, cc),
        [(ALL, STATE)],
        scalars=1,
    )
    got = swap_cores(give)
    (joint,) = call(join_again_kernel, "join", [half_shape], (cores, keep, got, pair), scalars=1)
    pieces = over_chips(joint.reshape(chips, 1, CHUNK))
    (leaving,) = call(
        functools.partial(scan_kernel, True), "block_scan", [((chips, 1, CHUNK), F32)], (pieces, firsts)
    )
    ahead = over_chips(leaving).reshape(HALF, STATE)
    later_own, later_give = call(
        functools.partial(split_kernel, 1), "split", [half_shape] * 2, (cores, ahead, keep, got, pair), scalars=1
    )
    later_got = swap_cores(later_give)
    dz, db, dcum, dskip, grad_z, early, cpart = call(
        middle_kernel,
        "middle",
        [t_shape, bc_shape, h_shape, h_shape, ((SPAN, wx), jnp.bfloat16), ((24, TILE), F32)]
        + [((GROUPS, SPAN + 8, TILE), F32)],
        (sums, y, zt, ogt, dy, dg, enter, mt, zs, xt, bc, cc, cum, skip, c_raw, before, conv_c),
        [(LEAD + SPAN, wb), (LEAD + SPAN, wb), (SPAN, wb)],
    )
    quarter = ((2 * SPAN + 16, TILE), F32)
    xown, xheads, mine, *gives, packed, ddt = call(
        last_kernel,
        "last",
        [((SPAN, wx), F32), ((64, TILE), F32)] + [quarter] * GROUPS + [((80, TILE), F32), h_shape],
        (cores, places, later_own, later_got, enter, ends, dz, db, dcum, dskip, early, cpart)
        + (dy, zs, xt, bc, cum, step, skip, dt, per_head, x_raw, conv_x, b_raw, conv_b, before),
        [(GROUPS, 2 * SPAN + 16, TILE), (ALL, STATE)]
        + [(LEAD + SPAN, wx), (LEAD + SPAN, wb), (LEAD + SPAN, wx), (LEAD + SPAN, wb)],
        scalars=2,
    )
    peers = lax.axis_size("tp")

    def ahead_by(v, k):
        return lax.ppermute(v, "tp", [(i, (i + k) % peers) for i in range(peers)])

    arrived = [ahead_by(v, k + 1) for k, v in enumerate(gives)]
    packed = packed + swap_cores(packed)
    packed = fold(packed, "chip", flip(1))
    arrived, packed = lax.optimization_barrier((arrived, packed))
    mine = (mine + arrived[0]) + (arrived[1] + arrived[2])
    heads = jnp.concatenate([xheads, mine[2 * SPAN :]], axis=0)
    heads = lax.ppermute(heads, CTX, [(i + 1, i) for i in range(size - 1)])
    packed = sum_four(packed, "chip", flip(2), mirror(RING))
    heads, packed = lax.optimization_barrier((heads, packed))
    grad_x_raw, quarter = call(
        settle_kernel,
        "settle",
        [((SPAN, wx), jnp.bfloat16), ((2 * SPAN, TILE), jnp.bfloat16)],
        (xown, mine, heads),
    )
    quarter, packed = lax.optimization_barrier((quarter, packed))
    others = [ahead_by(quarter, k) for k in range(1, peers)]
    packed = sum_four(packed, "chip", flip(RING), flip(2 * RING))
    others, packed = lax.optimization_barrier((others, packed))
    bc_taps = sum_four(packed[:32], "tp", flip(1), flip(2))
    half_bc, each = ((SPAN, wb), jnp.bfloat16), ((1, LOCAL), F32)
    grad_b_raw, grad_c_raw, conv_x_total, conv_b_total, conv_c_total, gain_total, *small = call(
        finish_kernel,
        "finish",
        [half_bc, half_bc, ((CONV, wx), F32), ((CONV, wb), F32), ((CONV, wb), F32), ((1, wx), F32)] + [each] * 3,
        (places, quarter, *others, bc_taps, packed),
        scalars=1,
    )
    return (
        grad_x_raw,
        grad_b_raw,
        grad_c_raw,
        grad_z,
        ddt.T,
        conv_x_total,
        conv_b_total,
        conv_c_total,
        *(v.reshape(-1) for v in small),
        gain_total.reshape(-1),
    )


def solution(mesh):
    rows, cols, some = P(CTX, "tp"), P(None, "tp"), P("tp")
    chips, tp = mesh.shape["ctx"] // 2, mesh.shape["tp"]
    mesh = Mesh(mesh.devices.reshape(chips, 2, tp), (*CTX, "tp"))
    return jax.shard_map(
        body,
        mesh=mesh,
        in_specs=(rows, P(CTX, None), P(CTX, None), rows, rows, cols, P(), P(), some, some, some, some, rows),
        out_specs=(rows, P(CTX, None), P(CTX, None), rows, rows, cols, P(), P(), some, some, some, some),
        check_vma=False,
    )
```

```python
import functools

import jax
import jax.numpy as jnp
from jax import lax
from jax.experimental import pallas as pl
from jax.experimental.pallas import tpu as pltpu
from jax.sharding import Mesh, PartitionSpec as P

HEAD_DIM = 32
STATE = 128
GROUPS = 4
CONV = 4
SPAN = 128
TILE = 128
PER = 8
LOCAL = PER * GROUPS
ROWS = PER * HEAD_DIM
ALL = LOCAL * HEAD_DIM
HALF = ALL // 2
CHUNK = 2048
LEAD = 16
GROUP_WIDTH = 1024
EPSILON = 1e-05
F32 = jnp.float32
CTX = ("chip", "core")
RING = 8
PARAMS = pltpu.CompilerParams(vmem_limit_bytes=16 << 20)


def dot(a, b, ca=1, cb=0):
    return lax.dot_general(
        a, b, (((ca,), (cb,)), ((), ())), precision=lax.Precision.HIGHEST, preferred_element_type=F32
    )


def group(g):
    return slice(g * ROWS, (g + 1) * ROWS)


def lanes(r):
    return slice(r * TILE, (r + 1) * TILE)


def spot(g, r):
    return slice(g * ROWS + r * HEAD_DIM, g * ROWS + (r + 1) * HEAD_DIM)


def put(dst, r, tile):
    turned = tile.T
    for g in range(GROUPS):
        dst[spot(g, r), :] = turned[g * HEAD_DIM : (g + 1) * HEAD_DIM]


def take(values, r):
    rows = slice(r * HEAD_DIM, (r + 1) * HEAD_DIM)
    return jnp.concatenate([v[rows] for v in values], axis=0).T


def heads_out(v, g):
    return jnp.concatenate(
        [jnp.broadcast_to(v[g * PER + r : g * PER + r + 1], (HEAD_DIM, v.shape[1])) for r in range(PER)], axis=0
    )


def heads_in(v):
    return jnp.concatenate(
        [jnp.sum(v[r * HEAD_DIM : (r + 1) * HEAD_DIM], axis=0, keepdims=True) for r in range(PER)], axis=0
    )


def sigmoid(v):
    return 1.0 / (1.0 + jnp.exp(-v))


def silu_slope(v):
    s = sigmoid(v)
    return s * (1.0 + v * (1.0 - s))


def extend(ext, raw, before, at):
    ext[0:LEAD, :] = before[:, at : at + ext.shape[1]].astype(F32)
    ext[LEAD : LEAD + SPAN, :] = raw[...].astype(F32)


def group_order():
    to = lax.broadcasted_iota(jnp.int32, (LOCAL, LOCAL), 0)
    at = lax.broadcasted_iota(jnp.int32, (LOCAL, LOCAL), 1)
    return jnp.where(at == to % PER * GROUPS + to // PER, 1.0, 0.0)


def conv_tile(ext, w, cols):
    total = w[0:1, cols] * ext[LEAD - 3 : LEAD - 3 + SPAN, cols]
    for k in range(1, CONV):
        total = total + w[k : k + 1, cols] * ext[LEAD - 3 + k : LEAD - 3 + k + SPAN, cols]
    return total


def conv_back_tile(ext, pad, w, cols, grad):
    dpre = grad * silu_slope(conv_tile(ext, w, cols))
    pad[8 : 8 + SPAN, cols] = dpre
    taps = [
        jnp.sum(dpre * ext[LEAD - 3 + k : LEAD - 3 + k + SPAN, cols], axis=0, keepdims=True) for k in range(CONV)
    ]
    mine = w[0:1, cols] * pad[11 : 11 + SPAN, cols]
    ahead = w[0:1, cols] * pad[3:11, cols]
    for k in range(1, CONV):
        mine = mine + w[k : k + 1, cols] * pad[11 - k : 11 - k + SPAN, cols]
        ahead = ahead + w[k : k + 1, cols] * pad[3 - k : 11 - k, cols]
    return mine, ahead, taps


def clear_pad(pad):
    pad[0:8, :] = jnp.zeros((8, pad.shape[1]), F32)
    pad[8 + SPAN : 16 + SPAN, :] = jnp.zeros((8, pad.shape[1]), F32)


def halves(core, full, keep, give):
    keep[...] = full[pl.ds(pl.multiple_of(core * HALF, HALF), HALF), :]
    give[0:HALF, :] = full[pl.ds(pl.multiple_of((1 - core) * HALF, HALF), HALF), :]


def unite(core, full, own, got):
    full[pl.ds(pl.multiple_of(core * HALF, HALF), HALF), :] = own[...]
    full[pl.ds(pl.multiple_of((1 - core) * HALF, HALF), HALF), :] = got[...]


def triangle(upper):
    rows = lax.broadcasted_iota(jnp.int32, (SPAN, SPAN), 0)
    cols = lax.broadcasted_iota(jnp.int32, (SPAN, SPAN), 1)
    return rows <= cols if upper else rows >= cols


def steps_kernel(raw, bias, alog, d_skip, dt, heads, step, cum, ends, skip):
    order = group_order()
    dt[...] = dot(order, raw[...])
    rows = jnp.concatenate([bias[...], alog[...], d_skip[...], jnp.zeros((5, LOCAL), F32)], axis=0)
    heads[...] = dot(order, rows, 1, 1)
    v = dt[...] + heads[:, 0:1]
    skip[...] = jnp.broadcast_to(heads[:, 2:3], skip.shape)
    step[...] = jnp.maximum(v, 0.0) + jnp.log1p(jnp.exp(-jnp.abs(v)))
    rates = -jnp.exp(heads[:, 1:2]) * step[...]
    cum[...] = dot(rates, jnp.where(triangle(True), 1.0, 0.0))
    ends[...] = jnp.broadcast_to(jnp.exp(jnp.sum(rates, axis=1, keepdims=True)), ends.shape)


def turn_kernel(z, og, gain, zt, ogt, sgt):
    for r in range(PER):
        put(zt, r, z[:, lanes(r)].astype(F32))
        tile = og[:, lanes(r)].astype(F32)
        put(ogt, r, tile)
        put(sgt, r, tile * gain[:, lanes(r)])


def state_kernel(core, x, b, before, wx, wb, step, cum, ends, xt, zs, bc, keep, give, ext, extb, full):
    extend(ext, x, before, 0)
    extend(extb, b, before, x.shape[1])
    for g in range(GROUPS):
        pre = conv_tile(extb, wb, lanes(g))
        bc[:, lanes(g)] = pre * sigmoid(pre)
    for r in range(PER):
        pre = conv_tile(ext, wx, lanes(r))
        put(xt, r, pre * sigmoid(pre))
    scale = jnp.exp(-cum[...]) * step[...]
    for g in range(GROUPS):
        zg = xt[group(g), :] * heads_out(scale, g)
        zs[group(g), :] = zg
        full[group(g), :] = heads_out(ends[...], g) * dot(zg, bc[:, lanes(g)])
    halves(core[0], full, keep, give)
    give[HALF : HALF + LOCAL, :] = ends[...]


def local_kernel(c, before, wc, bc, xt, zs, cum, skip, cc, mt, y, extc):
    extend(extc, c, before, before.shape[1] - c.shape[1])
    alpha = jnp.exp(cum[...])
    causal = triangle(True)
    for g in range(GROUPS):
        pre = conv_tile(extc, wc, lanes(g))
        cg = pre * sigmoid(pre)
        cc[:, lanes(g)] = cg
        m = jnp.where(causal, dot(bc[:, lanes(g)], cg, 1, 1), 0.0)
        mt[lanes(g), :] = m
        y[group(g), :] = heads_out(alpha, g) * dot(zs[group(g), :], m) + heads_out(skip[...], g) * xt[group(g), :]


def output_kernel(core, own, got, cc, y1, cum, zt, sgt, full, y, sums):
    unite(core[0], full, own, got)
    alpha = jnp.exp(cum[...])
    for g in range(GROUPS):
        yg = y1[group(g), :] + heads_out(alpha, g) * dot(full[group(g), :], cc[:, lanes(g)], 1, 1)
        y[group(g), :] = yg
        z = zt[group(g), :]
        gated = yg * z * sigmoid(z)
        sums[g : g + 1, :] = jnp.sum(gated * gated, axis=0, keepdims=True)
        sums[GROUPS + g : GROUPS + g + 1, :] = jnp.sum(sgt[group(g), :] * gated, axis=0, keepdims=True)


def gate_kernel(core, sums, y, zt, sgt, cum, cc, keep, give, dy, dg, full):
    alpha = jnp.exp(cum[...])
    for g in range(GROUPS):
        inv = lax.rsqrt(sums[g : g + 1, :] / GROUP_WIDTH + EPSILON)
        fix = inv * inv * inv * sums[GROUPS + g : GROUPS + g + 1, :] / GROUP_WIDTH
        z = zt[group(g), :]
        act = z * sigmoid(z)
        dgated = inv * sgt[group(g), :] - y[group(g), :] * act * fix
        dg[group(g), :] = dgated
        dyg = dgated * act
        dy[group(g), :] = dyg
        full[group(g), :] = dot(heads_out(alpha, g) * dyg, cc[:, lanes(g)])
    halves(core[0], full, keep, give)


def middle_kernel(
    sums, y, zt, ogt, dy, dg, full, mt, zs, xt, bc, cc, cum, skip, c, before, wc,
    dz, db, dcum, dskip, gz, early, cpart, extc, padc, dc,
):
    alpha = jnp.exp(cum[...])
    causal = triangle(True)
    slope, shares = [], []
    for g in range(GROUPS):
        z, yg, dyg = zt[group(g), :], y[group(g), :], dy[group(g), :]
        inv = lax.rsqrt(sums[g : g + 1, :] / GROUP_WIDTH + EPSILON)
        slope.append(dg[group(g), :] * yg * silu_slope(z))
        shares.append(ogt[group(g), :] * yg * z * sigmoid(z) * inv)
        heads = slice(g * PER, (g + 1) * PER)
        x = xt[group(g), :]
        passed = heads_in(dyg * x)
        dskip[heads, :] = passed
        dcum[heads, :] = heads_in(dyg * (yg - heads_out(skip[...], g) * x))
        u = heads_out(alpha, g) * dyg
        dz[group(g), :] = dot(u, mt[lanes(g), :], 1, 1)
        dm = jnp.where(causal, dot(zs[group(g), :], u, 0, 0), 0.0)
        dc[:, lanes(g)] = dot(dm, bc[:, lanes(g)], 0, 0) + dot(u, full[group(g), :], 0, 0)
        db[:, lanes(g)] = dot(dm, cc[:, lanes(g)])
    for r in range(PER):
        gz[:, lanes(r)] = take(slope, r).astype(jnp.bfloat16)
        early[16 + r : 17 + r, :] = jnp.sum(take(shares, r), axis=0, keepdims=True)
    extend(extc, c, before, before.shape[1] - c.shape[1])
    clear_pad(padc)
    for g in range(GROUPS):
        mine, ahead, taps = conv_back_tile(extc, padc, wc, lanes(g), dc[:, lanes(g)])
        cpart[g, 0:SPAN, :] = mine
        cpart[g, SPAN : SPAN + 8, :] = ahead
        for k in range(CONV):
            early[k * GROUPS + g : k * GROUPS + g + 1, :] = taps[k]


def last_kernel(
    core, which, own, got, full, ends, dz1, db1, dcum1, dskip, early, cpart, dy, zs, xt, bc, cum, step, skip, dt, per_head,
    x, wx, b, wb, before,
    xown, heads, keep, give, packed, ddt, parts, later, ext, extb, pad, padb,
):
    unite(core[0], later, own, got)
    gamma = jnp.exp(-cum[...])
    scale = gamma * step[...]
    clear_pad(pad)
    clear_pad(padb)
    extend(ext, x, before, 0)
    extend(extb, b, before, x.shape[1])
    dxs, turned, straight = [], [], []
    at_end = lax.broadcasted_iota(jnp.int32, (PER, SPAN), 1) == SPAN - 1
    for g in range(GROUPS):
        here = slice(g * PER, (g + 1) * PER)
        zg, xg = zs[group(g), :], xt[group(g), :]
        d = heads_out(ends[...], g) * later[group(g), :]
        second = dot(d, bc[:, lanes(g)], 1, 1)
        dzg = dz1[group(g), :] + second
        dxs.append(heads_out(scale, g) * dzg + heads_out(skip[...], g) * dy[group(g), :])
        edge = heads_in(zg * second + d * full[group(g), :])
        edge = jnp.sum(edge, axis=1, keepdims=True)
        turned.append(dcum1[here, :] - heads_in(dzg * zg) + jnp.where(at_end, edge, 0.0))
        straight.append(heads_in(dzg * xg))
        dbg = db1[:, lanes(g)] + dot(zg, d, 0, 0)
        mine, ahead, taps = conv_back_tile(extb, padb, wb, lanes(g), dbg)
        parts[g, 0:SPAN, :] = mine
        parts[g, SPAN : 2 * SPAN, :] = cpart[g, 0:SPAN, :]
        parts[g, 2 * SPAN : 2 * SPAN + 8, :] = ahead
        parts[g, 2 * SPAN + 8 : 2 * SPAN + 16, :] = cpart[g, SPAN : SPAN + 8, :]
        for k in range(CONV):
            packed[k * GROUPS + g : k * GROUPS + g + 1, :] = taps[k]
    dlog = dot(jnp.concatenate(turned, axis=0), jnp.where(triangle(False), 1.0, 0.0))
    rate = -jnp.exp(per_head[:, 1:2])
    dstep = jnp.concatenate(straight, axis=0) * gamma + dlog * rate
    draw = dstep * sigmoid(dt[...] + per_head[:, 0:1])
    ddt[...] = dot(group_order(), draw, 0, 0)
    each = jnp.concatenate([draw, dlog * rate * step[...], dskip[...], jnp.zeros((LOCAL, SPAN), F32)], axis=0)
    at = lax.broadcasted_iota(jnp.int32, (SPAN, SPAN), 0)
    to = lax.broadcasted_iota(jnp.int32, (SPAN, SPAN), 1)
    source = to // LOCAL * LOCAL + to % GROUPS * PER + to % LOCAL // GROUPS
    packed[72:80, :] = dot(dot(jnp.ones((8, SPAN), F32), each, 1, 1), jnp.where(at == source, 1.0, 0.0))
    packed[16:32, :] = early[0:16, :]
    packed[64:72, :] = early[16:24, :]
    side = which[0]
    keep[...] = parts[pl.ds(side * 2, 2)]
    give[...] = parts[pl.ds((1 - side) * 2, 2)]
    for r in range(PER):
        mine, ahead, taps = conv_back_tile(ext, pad, wx, lanes(r), take(dxs, r))
        xown[:, lanes(r)] = mine
        heads[8 * r : 8 * r + 8, :] = ahead
        for k in range(CONV):
            packed[32 + k * PER + r : 33 + k * PER + r, :] = taps[k]


def pair_decays(core, pair, lead):
    mine, theirs = pair[0 : LOCAL // 2, :], pair[LOCAL // 2 : LOCAL, :]
    leads = core == lead
    return jnp.where(leads, mine, theirs), jnp.where(leads, theirs, mine), leads


def join_first_kernel(core, keep, got, ends, joint, pair):
    half = LOCAL // 2
    pair[0:half, :] = ends[pl.ds(pl.multiple_of(core[0] * half, half), half), :]
    pair[half:LOCAL, :] = got[pl.ds(pl.multiple_of(HALF + core[0] * half, half), half), :]
    first, second, leads = pair_decays(core[0], pair, 0)
    for h in range(half):
        rows = slice(h * HEAD_DIM, (h + 1) * HEAD_DIM)
        mine, theirs = keep[rows, :], got[rows, :]
        both = second[h : h + 1] * jnp.where(leads, mine, theirs) + jnp.where(leads, theirs, mine)
        for i in range(HEAD_DIM):
            joint[2 * h + i // 16, :, lanes(i % 16)] = both[i : i + 1]
        for i in range(2):
            joint[2 * h + i, :, CHUNK:] = first[h : h + 1] * second[h : h + 1]


def join_again_kernel(core, keep, got, pair, joint):
    _, second, leads = pair_decays(core[0], pair, 1)
    for h in range(LOCAL // 2):
        rows = slice(h * HEAD_DIM, (h + 1) * HEAD_DIM)
        mine, theirs = keep[rows, :], got[rows, :]
        joint[rows, :] = second[h : h + 1] * jnp.where(leads, mine, theirs) + jnp.where(leads, theirs, mine)


def split_kernel(lead, core, ahead, keep, got, pair, own, give):
    first, _, leads = pair_decays(core[0], pair, lead)
    for h in range(LOCAL // 2):
        rows = slice(h * HEAD_DIM, (h + 1) * HEAD_DIM)
        far = ahead[rows, :]
        near = first[h : h + 1] * far + jnp.where(leads, keep[rows, :], got[rows, :])
        own[rows, :] = jnp.where(leads, far, near)
        give[rows, :] = jnp.where(leads, near, far)


def settle_kernel(xown, mine, heads, gx, half):
    last = slice(SPAN - LEAD, SPAN)
    none = jnp.zeros((LEAD - 8, TILE), F32)
    for r in range(PER):
        gx[0 : SPAN - LEAD, lanes(r)] = xown[0 : SPAN - LEAD, lanes(r)].astype(jnp.bfloat16)
        more = jnp.concatenate([none, heads[8 * r : 8 * r + 8, :]], axis=0)
        gx[last, lanes(r)] = (xown[last, lanes(r)] + more).astype(jnp.bfloat16)
    for g in range(2):
        for i in range(2):
            at = 64 + 16 * g + 8 * i
            more = jnp.concatenate([none, heads[at : at + 8, :]], axis=0)
            start, stop = i * SPAN, (i + 1) * SPAN
            half[g, start : stop - LEAD, :] = mine[g, start : stop - LEAD, :].astype(jnp.bfloat16)
            half[g, stop - LEAD : stop, :] = (mine[g, stop - LEAD : stop, :] + more).astype(jnp.bfloat16)


def finish_kernel(which, half, other, bc_taps, packed, gb, gc, tx, tb, tc, tgain, bias, rate, skip):
    left = which[0] == 0
    for g in range(GROUPS):
        first, second = (half, other) if g < 2 else (other, half)
        both = jnp.where(left, first[g % 2].astype(F32), second[g % 2].astype(F32)).astype(jnp.bfloat16)
        gb[:, lanes(g)] = both[0:SPAN]
        gc[:, lanes(g)] = both[SPAN : 2 * SPAN]
    for k in range(CONV):
        for g in range(GROUPS):
            tb[k : k + 1, lanes(g)] = bc_taps[k * GROUPS + g : k * GROUPS + g + 1, :]
            tc[k : k + 1, lanes(g)] = bc_taps[16 + k * GROUPS + g : 17 + k * GROUPS + g, :]
        for r in range(PER):
            tx[k : k + 1, lanes(r)] = packed[32 + k * PER + r : 33 + k * PER + r, :]
    for r in range(PER):
        tgain[:, lanes(r)] = packed[64 + r : 65 + r, :]
    bias[...] = packed[72:73, 0:LOCAL]
    rate[...] = packed[72:73, LOCAL : 2 * LOCAL]
    skip[...] = packed[72:73, 2 * LOCAL : 3 * LOCAL]


def scan_kernel(backward, s, d, o):
    count = s.shape[0]
    at = d.shape[2] - TILE
    carry = [jnp.zeros((1, TILE), F32)] * (CHUNK // TILE)
    for j in range(count):
        j = count - 1 - j if backward else j
        decay = d[j, :, at:]
        for k in range(CHUNK // TILE):
            o[j, :, lanes(k)] = carry[k]
            carry[k] = decay * carry[k] + s[j, :, lanes(k)]


def call(kernel, name, outs, args, scratch=(), scalars=0, flops=20_000_000):
    smem = pl.BlockSpec(memory_space=pltpu.SMEM)
    vmem = pl.BlockSpec(memory_space=pltpu.VMEM)
    return pl.pallas_call(
        kernel,
        out_shape=[jax.ShapeDtypeStruct(s, d) for s, d in outs],
        in_specs=[smem if i < scalars else vmem for i in range(len(args))],
        out_specs=[vmem] * len(outs),
        scratch_shapes=[pltpu.VMEM(s, F32) for s in scratch],
        compiler_params=PARAMS,
        cost_estimate=pl.CostEstimate(flops=flops, bytes_accessed=4 << 20, transcendentals=1 << 18),
        name=name,
    )(*args)


def swap_cores(v):
    return lax.ppermute(v, "core", [(0, 1), (1, 0)])


def alike(size, by):
    return [(i, i ^ by) for i in range(size)]


def over_chips(v):
    return lax.all_to_all(v, "chip", 0, 0)


def fold(x, axis, partner):
    return x + lax.ppermute(x, axis, [(i, partner(i)) for i in range(lax.axis_size(axis))])


def sum_four(x, axis, block=1):
    near, far, last = (
        lax.ppermute(x, axis, [(i, (i // block ^ k) * block + i % block) for i in range(lax.axis_size(axis))])
        for k in range(1, 4)
    )
    return (x + near) + (far + last)


def mirror(within):
    return lambda i: i // within * within + within - 1 - i % within


def body(
    x_raw, b_raw, c_raw, z_gate, dt_raw, conv_x, conv_b, conv_c, dt_bias, a_log, d_skip, gain, grad_out
):
    size = lax.axis_size(CTX)
    core = lax.axis_index("core")
    side = lax.axis_index("tp") // (lax.axis_size("tp") // 2)
    cores, sides = lax.optimization_barrier((core.reshape(1), side.reshape(1)))
    is_even = core == 0
    t_shape = ((ALL, SPAN), F32)
    bc_shape = ((SPAN, GROUPS * STATE), F32)
    h_shape = ((LOCAL, SPAN), F32)
    tails = jnp.concatenate([v[SPAN - LEAD :] for v in (x_raw, b_raw, c_raw)], axis=1)
    before = lax.ppermute(tails, CTX, [(i, i + 1) for i in range(size - 1)])
    wx, wb = x_raw.shape[1], b_raw.shape[1]

    dt, per_head, step, cum, ends, skip = call(
        steps_kernel,
        "steps",
        [h_shape, ((LOCAL, 8), F32)] + [h_shape] * 4,
        (dt_raw.T, dt_bias[None], a_log[None], d_skip[None]),
    )
    zt, ogt, sgt = call(turn_kernel, "turn", [t_shape] * 3, (z_gate, grad_out, gain[None]))
    before, zt, ogt, sgt = lax.optimization_barrier((before, zt, ogt, sgt))
    xt, zs, bc, keep, give = call(
        state_kernel,
        "state",
        [t_shape, t_shape, bc_shape, ((HALF, STATE), F32), ((HALF + LOCAL, STATE), F32)],
        (cores, x_raw, b_raw, before, conv_x, conv_b, step, cum, ends),
        [(LEAD + SPAN, wx), (LEAD + SPAN, wb), (ALL, STATE)],
        scalars=1,
    )
    got = swap_cores(give)
    half_shape = ((HALF, STATE), F32)
    chips = lax.axis_size("chip")
    joint, pair = call(
        join_first_kernel,
        "join",
        [((chips, 1, CHUNK + TILE), F32), h_shape],
        (cores, keep, got, ends),
        scalars=1,
    )
    firsts = over_chips(joint)
    (entering,) = call(
        functools.partial(scan_kernel, False), "block_scan", [((chips, 1, CHUNK), F32)], (firsts, firsts)
    )
    ahead = over_chips(entering).reshape(HALF, STATE)
    enter_own, enter_give = call(
        functools.partial(split_kernel, 0), "split", [half_shape] * 2, (cores, ahead, keep, got, pair), scalars=1
    )
    enter_got = swap_cores(enter_give)

    cc, mt, y1 = call(
        local_kernel,
        "local",
        [bc_shape, ((GROUPS * SPAN, SPAN), F32), t_shape],
        (c_raw, before, conv_c, bc, xt, zs, cum, skip),
        [(LEAD + SPAN, wb)],
    )
    enter, y, sums = call(
        output_kernel,
        "output",
        [t_shape, t_shape, ((2 * GROUPS, SPAN), F32)],
        (cores, enter_own, enter_got, cc, y1, cum, zt, sgt),
        scalars=1,
    )
    sums = sum_four(sums, "tp")
    keep, give, dy, dg = call(
        gate_kernel,
        "gate",
        [((HALF, STATE), F32)] * 2 + [t_shape, t_shape],
        (cores, sums, y, zt, sgt, cum, cc),
        [(ALL, STATE)],
        scalars=1,
    )
    got = swap_cores(give)
    (joint,) = call(join_again_kernel, "join", [half_shape], (cores, keep, got, pair), scalars=1)
    pieces = over_chips(joint.reshape(chips, 1, CHUNK))
    (leaving,) = call(
        functools.partial(scan_kernel, True), "block_scan", [((chips, 1, CHUNK), F32)], (pieces, firsts)
    )
    ahead = over_chips(leaving).reshape(HALF, STATE)
    later_own, later_give = call(
        functools.partial(split_kernel, 1), "split", [half_shape] * 2, (cores, ahead, keep, got, pair), scalars=1
    )
    later_got = swap_cores(later_give)
    dz, db, dcum, dskip, grad_z, early, cpart = call(
        middle_kernel,
        "middle",
        [t_shape, bc_shape, h_shape, h_shape, ((SPAN, wx), jnp.bfloat16), ((24, TILE), F32)]
        + [((GROUPS, SPAN + 8, TILE), F32)],
        (sums, y, zt, ogt, dy, dg, enter, mt, zs, xt, bc, cc, cum, skip, c_raw, before, conv_c),
        [(LEAD + SPAN, wb), (LEAD + SPAN, wb), (SPAN, wb)],
    )
    half_parts = ((2, 2 * SPAN + 16, TILE), F32)
    xown, xheads, keep, give, packed, ddt = call(
        last_kernel,
        "last",
        [((SPAN, wx), F32), ((64, TILE), F32), half_parts, half_parts, ((80, TILE), F32), h_shape],
        (cores, sides, later_own, later_got, enter, ends, dz, db, dcum, dskip, early, cpart)
        + (dy, zs, xt, bc, cum, step, skip, dt, per_head, x_raw, conv_x, b_raw, conv_b, before),
        [(GROUPS, 2 * SPAN + 16, TILE), (ALL, STATE)]
        + [(LEAD + SPAN, wx), (LEAD + SPAN, wb), (LEAD + SPAN, wx), (LEAD + SPAN, wb)],
        scalars=2,
    )
    peers = lax.axis_size("tp")
    across = [(i, peers - 1 - i) for i in range(peers)]
    arrived = lax.ppermute(give, "tp", across)
    packed = packed + swap_cores(packed)
    packed = fold(packed, "chip", mirror(2))
    packed = fold(packed, "chip", lambda i: i ^ 2)
    arrived, packed = lax.optimization_barrier((arrived, packed))
    mine = keep + arrived
    arrived = lax.ppermute(mine, "tp", [(i, i ^ 1) for i in range(peers)])
    packed = fold(packed, "chip", mirror(RING))
    mine = mine + arrived
    heads = jnp.concatenate([xheads, mine[:, 2 * SPAN :].reshape(32, TILE)], axis=0)
    mine, heads, packed = lax.optimization_barrier((mine, heads, packed))
    heads = lax.ppermute(heads, CTX, [(i + 1, i) for i in range(size - 1)])
    grad_x_raw, half = call(
        settle_kernel,
        "settle",
        [((SPAN, wx), jnp.bfloat16), ((2, 2 * SPAN, TILE), jnp.bfloat16)],
        (xown, mine, heads),
    )
    half, packed = lax.optimization_barrier((half, packed))
    other = lax.ppermute(half, "tp", across)
    packed = sum_four(packed, "chip", RING)
    other, packed = lax.optimization_barrier((other, packed))
    bc_taps = sum_four(packed[:32], "tp")
    half_bc, each = ((SPAN, wb), jnp.bfloat16), ((1, LOCAL), F32)
    grad_b_raw, grad_c_raw, conv_x_total, conv_b_total, conv_c_total, gain_total, *small = call(
        finish_kernel,
        "finish",
        [half_bc, half_bc, ((CONV, wx), F32), ((CONV, wb), F32), ((CONV, wb), F32), ((1, wx), F32)] + [each] * 3,
        (sides, half, other, bc_taps, packed),
        scalars=1,
    )
    return (
        grad_x_raw,
        grad_b_raw,
        grad_c_raw,
        grad_z,
        ddt.T,
        conv_x_total,
        conv_b_total,
        conv_c_total,
        *(v.reshape(-1) for v in small),
        gain_total.reshape(-1),
    )


def solution(mesh):
    rows, cols, some = P(CTX, "tp"), P(None, "tp"), P("tp")
    chips, tp = mesh.shape["ctx"] // 2, mesh.shape["tp"]
    mesh = Mesh(mesh.devices.reshape(chips, 2, tp), (*CTX, "tp"))
    return jax.shard_map(
        body,
        mesh=mesh,
        in_specs=(rows, P(CTX, None), P(CTX, None), rows, rows, cols, P(), P(), some, some, some, some, rows),
        out_specs=(rows, P(CTX, None), P(CTX, None), rows, rows, cols, P(), P(), some, some, some, some),
        check_vma=False,
    )
```

```python
import functools

import jax
import jax.numpy as jnp
from jax import lax
from jax.experimental import pallas as pl
from jax.experimental.pallas import tpu as pltpu
from jax.sharding import Mesh, PartitionSpec as P

HEAD_DIM = 32
STATE = 128
GROUPS = 4
CONV = 4
SPAN = 128
TILE = 128
PER = 8
LOCAL = PER * GROUPS
ROWS = PER * HEAD_DIM
ALL = LOCAL * HEAD_DIM
HALF = ALL // 2
CHUNK = 2048
LEAD = 16
GROUP_WIDTH = 1024
EPSILON = 1e-05
F32 = jnp.float32
CTX = ("chip", "core")
RING = 8
PARAMS = pltpu.CompilerParams(vmem_limit_bytes=16 << 20)


def exact(a, b, ca=1, cb=0):
    return lax.dot_general(
        a, b, (((ca,), (cb,)), ((), ())), precision=lax.Precision.HIGHEST, preferred_element_type=F32
    )


def dot(a, b, ca=1, cb=0):
    high_a, high_b = a.astype(jnp.bfloat16), b.astype(jnp.bfloat16)
    low_a = (a - high_a.astype(F32)).astype(jnp.bfloat16)
    low_b = (b - high_b.astype(F32)).astype(jnp.bfloat16)

    def part(x, y):
        return lax.dot_general(x, y, (((ca,), (cb,)), ((), ())), preferred_element_type=F32)

    return part(high_a, high_b) + (part(high_a, low_b) + part(low_a, high_b))


def group(g):
    return slice(g * ROWS, (g + 1) * ROWS)


def lanes(r):
    return slice(r * TILE, (r + 1) * TILE)


def spot(g, r):
    return slice(g * ROWS + r * HEAD_DIM, g * ROWS + (r + 1) * HEAD_DIM)


def put(dst, r, tile):
    turned = tile.T
    for g in range(GROUPS):
        dst[spot(g, r), :] = turned[g * HEAD_DIM : (g + 1) * HEAD_DIM]


def take(values, r):
    rows = slice(r * HEAD_DIM, (r + 1) * HEAD_DIM)
    return jnp.concatenate([v[rows] for v in values], axis=0).T


def heads_out(v, g):
    return jnp.concatenate(
        [jnp.broadcast_to(v[g * PER + r : g * PER + r + 1], (HEAD_DIM, v.shape[1])) for r in range(PER)], axis=0
    )


def heads_in(v):
    return jnp.concatenate(
        [jnp.sum(v[r * HEAD_DIM : (r + 1) * HEAD_DIM], axis=0, keepdims=True) for r in range(PER)], axis=0
    )


def sigmoid(v):
    return 1.0 / (1.0 + jnp.exp(-v))


def silu_slope(v):
    s = sigmoid(v)
    return s * (1.0 + v * (1.0 - s))


def extend(ext, raw, before, at):
    ext[0:LEAD, :] = before[:, at : at + ext.shape[1]].astype(F32)
    ext[LEAD : LEAD + SPAN, :] = raw[...].astype(F32)


def group_order():
    to = lax.broadcasted_iota(jnp.int32, (LOCAL, LOCAL), 0)
    at = lax.broadcasted_iota(jnp.int32, (LOCAL, LOCAL), 1)
    return jnp.where(at == to % PER * GROUPS + to // PER, 1.0, 0.0)


def conv_tile(ext, w, cols):
    total = w[0:1, cols] * ext[LEAD - 3 : LEAD - 3 + SPAN, cols]
    for k in range(1, CONV):
        total = total + w[k : k + 1, cols] * ext[LEAD - 3 + k : LEAD - 3 + k + SPAN, cols]
    return total


def conv_back_tile(ext, pad, w, cols, grad):
    dpre = grad * silu_slope(conv_tile(ext, w, cols))
    pad[8 : 8 + SPAN, cols] = dpre
    taps = [
        jnp.sum(dpre * ext[LEAD - 3 + k : LEAD - 3 + k + SPAN, cols], axis=0, keepdims=True) for k in range(CONV)
    ]
    mine = w[0:1, cols] * pad[11 : 11 + SPAN, cols]
    ahead = w[0:1, cols] * pad[3:11, cols]
    for k in range(1, CONV):
        mine = mine + w[k : k + 1, cols] * pad[11 - k : 11 - k + SPAN, cols]
        ahead = ahead + w[k : k + 1, cols] * pad[3 - k : 11 - k, cols]
    return mine, ahead, taps


def clear_pad(pad):
    pad[0:8, :] = jnp.zeros((8, pad.shape[1]), F32)
    pad[8 + SPAN : 16 + SPAN, :] = jnp.zeros((8, pad.shape[1]), F32)


def halves(core, full, keep, give):
    keep[...] = full[pl.ds(pl.multiple_of(core * HALF, HALF), HALF), :]
    give[0:HALF, :] = full[pl.ds(pl.multiple_of((1 - core) * HALF, HALF), HALF), :]


def unite(core, full, own, got):
    full[pl.ds(pl.multiple_of(core * HALF, HALF), HALF), :] = own[...]
    full[pl.ds(pl.multiple_of((1 - core) * HALF, HALF), HALF), :] = got[...]


def triangle(upper):
    rows = lax.broadcasted_iota(jnp.int32, (SPAN, SPAN), 0)
    cols = lax.broadcasted_iota(jnp.int32, (SPAN, SPAN), 1)
    return rows <= cols if upper else rows >= cols


def steps_kernel(raw, bias, alog, d_skip, dt, heads, step, cum, ends, skip):
    order = group_order()
    dt[...] = exact(order, raw[...])
    rows = jnp.concatenate([bias[...], alog[...], d_skip[...], jnp.zeros((5, LOCAL), F32)], axis=0)
    heads[...] = exact(order, rows, 1, 1)
    v = dt[...] + heads[:, 0:1]
    skip[...] = jnp.broadcast_to(heads[:, 2:3], skip.shape)
    step[...] = jnp.maximum(v, 0.0) + jnp.log1p(jnp.exp(-jnp.abs(v)))
    rates = -jnp.exp(heads[:, 1:2]) * step[...]
    cum[...] = exact(rates, jnp.where(triangle(True), 1.0, 0.0))
    ends[...] = jnp.broadcast_to(jnp.exp(jnp.sum(rates, axis=1, keepdims=True)), ends.shape)


def turn_kernel(z, og, gain, zt, ogt, sgt):
    for r in range(PER):
        put(zt, r, z[:, lanes(r)].astype(F32))
        tile = og[:, lanes(r)].astype(F32)
        put(ogt, r, tile)
        put(sgt, r, tile * gain[:, lanes(r)])


def state_kernel(core, x, b, before, wx, wb, step, cum, ends, xt, zs, bc, keep, give, ext, extb, full):
    extend(ext, x, before, 0)
    extend(extb, b, before, x.shape[1])
    for g in range(GROUPS):
        pre = conv_tile(extb, wb, lanes(g))
        bc[:, lanes(g)] = pre * sigmoid(pre)
    for r in range(PER):
        pre = conv_tile(ext, wx, lanes(r))
        put(xt, r, pre * sigmoid(pre))
    scale = jnp.exp(-cum[...]) * step[...]
    for g in range(GROUPS):
        zg = xt[group(g), :] * heads_out(scale, g)
        zs[group(g), :] = zg
        full[group(g), :] = heads_out(ends[...], g) * dot(zg, bc[:, lanes(g)])
    halves(core[0], full, keep, give)
    give[HALF : HALF + LOCAL, :] = ends[...]


def local_kernel(c, before, wc, bc, xt, zs, cum, skip, cc, mt, y, extc):
    extend(extc, c, before, before.shape[1] - c.shape[1])
    alpha = jnp.exp(cum[...])
    causal = triangle(True)
    for g in range(GROUPS):
        pre = conv_tile(extc, wc, lanes(g))
        cg = pre * sigmoid(pre)
        cc[:, lanes(g)] = cg
        m = jnp.where(causal, dot(bc[:, lanes(g)], cg, 1, 1), 0.0)
        mt[lanes(g), :] = m
        y[group(g), :] = heads_out(alpha, g) * dot(zs[group(g), :], m) + heads_out(skip[...], g) * xt[group(g), :]


def output_kernel(core, own, got, cc, y1, cum, zt, sgt, full, y, sums):
    unite(core[0], full, own, got)
    alpha = jnp.exp(cum[...])
    for g in range(GROUPS):
        yg = y1[group(g), :] + heads_out(alpha, g) * dot(full[group(g), :], cc[:, lanes(g)], 1, 1)
        y[group(g), :] = yg
        z = zt[group(g), :]
        gated = yg * z * sigmoid(z)
        sums[g : g + 1, :] = jnp.sum(gated * gated, axis=0, keepdims=True)
        sums[GROUPS + g : GROUPS + g + 1, :] = jnp.sum(sgt[group(g), :] * gated, axis=0, keepdims=True)


def gate_kernel(core, sums, y, zt, sgt, cum, cc, keep, give, dy, dg, full):
    alpha = jnp.exp(cum[...])
    for g in range(GROUPS):
        inv = lax.rsqrt(sums[g : g + 1, :] / GROUP_WIDTH + EPSILON)
        fix = inv * inv * inv * sums[GROUPS + g : GROUPS + g + 1, :] / GROUP_WIDTH
        z = zt[group(g), :]
        act = z * sigmoid(z)
        dgated = inv * sgt[group(g), :] - y[group(g), :] * act * fix
        dg[group(g), :] = dgated
        dyg = dgated * act
        dy[group(g), :] = dyg
        full[group(g), :] = dot(heads_out(alpha, g) * dyg, cc[:, lanes(g)])
    halves(core[0], full, keep, give)


def middle_kernel(
    sums, y, zt, ogt, dy, dg, full, mt, zs, xt, bc, cc, cum, skip, c, before, wc,
    dz, db, dcum, dskip, gz, early, cpart, extc, padc, dc,
):
    alpha = jnp.exp(cum[...])
    causal = triangle(True)
    slope, shares = [], []
    for g in range(GROUPS):
        z, yg, dyg = zt[group(g), :], y[group(g), :], dy[group(g), :]
        inv = lax.rsqrt(sums[g : g + 1, :] / GROUP_WIDTH + EPSILON)
        slope.append(dg[group(g), :] * yg * silu_slope(z))
        shares.append(ogt[group(g), :] * yg * z * sigmoid(z) * inv)
        heads = slice(g * PER, (g + 1) * PER)
        x = xt[group(g), :]
        passed = heads_in(dyg * x)
        dskip[heads, :] = passed
        dcum[heads, :] = heads_in(dyg * (yg - heads_out(skip[...], g) * x))
        u = heads_out(alpha, g) * dyg
        dz[group(g), :] = dot(u, mt[lanes(g), :], 1, 1)
        dm = jnp.where(causal, dot(zs[group(g), :], u, 0, 0), 0.0)
        dc[:, lanes(g)] = dot(dm, bc[:, lanes(g)], 0, 0) + dot(u, full[group(g), :], 0, 0)
        db[:, lanes(g)] = dot(dm, cc[:, lanes(g)])
    for r in range(PER):
        gz[:, lanes(r)] = take(slope, r).astype(jnp.bfloat16)
        early[16 + r : 17 + r, :] = jnp.sum(take(shares, r), axis=0, keepdims=True)
    extend(extc, c, before, before.shape[1] - c.shape[1])
    clear_pad(padc)
    for g in range(GROUPS):
        mine, ahead, taps = conv_back_tile(extc, padc, wc, lanes(g), dc[:, lanes(g)])
        cpart[g, 0:SPAN, :] = mine
        cpart[g, SPAN : SPAN + 8, :] = ahead
        for k in range(CONV):
            early[k * GROUPS + g : k * GROUPS + g + 1, :] = taps[k]


def last_kernel(
    core, which, own, got, full, ends, dz1, db1, dcum1, dskip, early, cpart, dy, zs, xt, bc, cum, step, skip, dt, per_head,
    x, wx, b, wb, before,
    xown, heads, keep, give, packed, ddt, parts, later, ext, extb, pad, padb,
):
    unite(core[0], later, own, got)
    gamma = jnp.exp(-cum[...])
    scale = gamma * step[...]
    clear_pad(pad)
    clear_pad(padb)
    extend(ext, x, before, 0)
    extend(extb, b, before, x.shape[1])
    dxs, turned, straight = [], [], []
    at_end = lax.broadcasted_iota(jnp.int32, (PER, SPAN), 1) == SPAN - 1
    for g in range(GROUPS):
        here = slice(g * PER, (g + 1) * PER)
        zg, xg = zs[group(g), :], xt[group(g), :]
        d = heads_out(ends[...], g) * later[group(g), :]
        second = dot(d, bc[:, lanes(g)], 1, 1)
        dzg = dz1[group(g), :] + second
        dxs.append(heads_out(scale, g) * dzg + heads_out(skip[...], g) * dy[group(g), :])
        edge = heads_in(zg * second + d * full[group(g), :])
        edge = jnp.sum(edge, axis=1, keepdims=True)
        turned.append(dcum1[here, :] - heads_in(dzg * zg) + jnp.where(at_end, edge, 0.0))
        straight.append(heads_in(dzg * xg))
        dbg = db1[:, lanes(g)] + dot(zg, d, 0, 0)
        mine, ahead, taps = conv_back_tile(extb, padb, wb, lanes(g), dbg)
        parts[g, 0:SPAN, :] = mine
        parts[g, SPAN : 2 * SPAN, :] = cpart[g, 0:SPAN, :]
        parts[g, 2 * SPAN : 2 * SPAN + 8, :] = ahead
        parts[g, 2 * SPAN + 8 : 2 * SPAN + 16, :] = cpart[g, SPAN : SPAN + 8, :]
        for k in range(CONV):
            packed[k * GROUPS + g : k * GROUPS + g + 1, :] = taps[k]
    dlog = exact(jnp.concatenate(turned, axis=0), jnp.where(triangle(False), 1.0, 0.0))
    rate = -jnp.exp(per_head[:, 1:2])
    dstep = jnp.concatenate(straight, axis=0) * gamma + dlog * rate
    draw = dstep * sigmoid(dt[...] + per_head[:, 0:1])
    ddt[...] = exact(group_order(), draw, 0, 0)
    each = jnp.concatenate([draw, dlog * rate * step[...], dskip[...], jnp.zeros((LOCAL, SPAN), F32)], axis=0)
    at = lax.broadcasted_iota(jnp.int32, (SPAN, SPAN), 0)
    to = lax.broadcasted_iota(jnp.int32, (SPAN, SPAN), 1)
    source = to // LOCAL * LOCAL + to % GROUPS * PER + to % LOCAL // GROUPS
    packed[72:80, :] = exact(exact(jnp.ones((8, SPAN), F32), each, 1, 1), jnp.where(at == source, 1.0, 0.0))
    packed[16:32, :] = early[0:16, :]
    packed[64:72, :] = early[16:24, :]
    side = which[0]
    keep[...] = parts[pl.ds(side * 2, 2)]
    give[...] = parts[pl.ds((1 - side) * 2, 2)]
    for r in range(PER):
        mine, ahead, taps = conv_back_tile(ext, pad, wx, lanes(r), take(dxs, r))
        xown[:, lanes(r)] = mine
        heads[8 * r : 8 * r + 8, :] = ahead
        for k in range(CONV):
            packed[32 + k * PER + r : 33 + k * PER + r, :] = taps[k]


def pair_decays(core, pair, lead):
    mine, theirs = pair[0 : LOCAL // 2, :], pair[LOCAL // 2 : LOCAL, :]
    leads = core == lead
    return jnp.where(leads, mine, theirs), jnp.where(leads, theirs, mine), leads


def join_first_kernel(core, keep, got, ends, joint, pair):
    half = LOCAL // 2
    pair[0:half, :] = ends[pl.ds(pl.multiple_of(core[0] * half, half), half), :]
    pair[half:LOCAL, :] = got[pl.ds(pl.multiple_of(HALF + core[0] * half, half), half), :]
    first, second, leads = pair_decays(core[0], pair, 0)
    for h in range(half):
        rows = slice(h * HEAD_DIM, (h + 1) * HEAD_DIM)
        mine, theirs = keep[rows, :], got[rows, :]
        both = second[h : h + 1] * jnp.where(leads, mine, theirs) + jnp.where(leads, theirs, mine)
        for i in range(HEAD_DIM):
            joint[2 * h + i // 16, :, lanes(i % 16)] = both[i : i + 1]
        for i in range(2):
            joint[2 * h + i, :, CHUNK:] = first[h : h + 1] * second[h : h + 1]


def join_again_kernel(core, keep, got, pair, joint):
    _, second, leads = pair_decays(core[0], pair, 1)
    for h in range(LOCAL // 2):
        rows = slice(h * HEAD_DIM, (h + 1) * HEAD_DIM)
        mine, theirs = keep[rows, :], got[rows, :]
        joint[rows, :] = second[h : h + 1] * jnp.where(leads, mine, theirs) + jnp.where(leads, theirs, mine)


def split_kernel(lead, core, ahead, keep, got, pair, own, give):
    first, _, leads = pair_decays(core[0], pair, lead)
    for h in range(LOCAL // 2):
        rows = slice(h * HEAD_DIM, (h + 1) * HEAD_DIM)
        far = ahead[rows, :]
        near = first[h : h + 1] * far + jnp.where(leads, keep[rows, :], got[rows, :])
        own[rows, :] = jnp.where(leads, far, near)
        give[rows, :] = jnp.where(leads, near, far)


def settle_kernel(xown, mine, heads, gx, half):
    last = slice(SPAN - LEAD, SPAN)
    none = jnp.zeros((LEAD - 8, TILE), F32)
    for r in range(PER):
        gx[0 : SPAN - LEAD, lanes(r)] = xown[0 : SPAN - LEAD, lanes(r)].astype(jnp.bfloat16)
        more = jnp.concatenate([none, heads[8 * r : 8 * r + 8, :]], axis=0)
        gx[last, lanes(r)] = (xown[last, lanes(r)] + more).astype(jnp.bfloat16)
    for g in range(2):
        for i in range(2):
            at = 64 + 16 * g + 8 * i
            more = jnp.concatenate([none, heads[at : at + 8, :]], axis=0)
            start, stop = i * SPAN, (i + 1) * SPAN
            half[g, start : stop - LEAD, :] = mine[g, start : stop - LEAD, :].astype(jnp.bfloat16)
            half[g, stop - LEAD : stop, :] = (mine[g, stop - LEAD : stop, :] + more).astype(jnp.bfloat16)


def finish_kernel(which, half, other, bc_taps, packed, gb, gc, tx, tb, tc, tgain, bias, rate, skip):
    left = which[0] == 0
    for g in range(GROUPS):
        first, second = (half, other) if g < 2 else (other, half)
        both = jnp.where(left, first[g % 2].astype(F32), second[g % 2].astype(F32)).astype(jnp.bfloat16)
        gb[:, lanes(g)] = both[0:SPAN]
        gc[:, lanes(g)] = both[SPAN : 2 * SPAN]
    for k in range(CONV):
        for g in range(GROUPS):
            tb[k : k + 1, lanes(g)] = bc_taps[k * GROUPS + g : k * GROUPS + g + 1, :]
            tc[k : k + 1, lanes(g)] = bc_taps[16 + k * GROUPS + g : 17 + k * GROUPS + g, :]
        for r in range(PER):
            tx[k : k + 1, lanes(r)] = packed[32 + k * PER + r : 33 + k * PER + r, :]
    for r in range(PER):
        tgain[:, lanes(r)] = packed[64 + r : 65 + r, :]
    bias[...] = packed[72:73, 0:LOCAL]
    rate[...] = packed[72:73, LOCAL : 2 * LOCAL]
    skip[...] = packed[72:73, 2 * LOCAL : 3 * LOCAL]


def scan_kernel(backward, s, d, o):
    count = s.shape[0]
    at = d.shape[2] - TILE
    carry = [jnp.zeros((1, TILE), F32)] * (CHUNK // TILE)
    for j in range(count):
        j = count - 1 - j if backward else j
        decay = d[j, :, at:]
        for k in range(CHUNK // TILE):
            o[j, :, lanes(k)] = carry[k]
            carry[k] = decay * carry[k] + s[j, :, lanes(k)]


def call(kernel, name, outs, args, scratch=(), scalars=0, flops=20_000_000):
    smem = pl.BlockSpec(memory_space=pltpu.SMEM)
    vmem = pl.BlockSpec(memory_space=pltpu.VMEM)
    return pl.pallas_call(
        kernel,
        out_shape=[jax.ShapeDtypeStruct(s, d) for s, d in outs],
        in_specs=[smem if i < scalars else vmem for i in range(len(args))],
        out_specs=[vmem] * len(outs),
        scratch_shapes=[pltpu.VMEM(s, F32) for s in scratch],
        compiler_params=PARAMS,
        cost_estimate=pl.CostEstimate(flops=flops, bytes_accessed=4 << 20, transcendentals=1 << 18),
        name=name,
    )(*args)


def swap_cores(v):
    return lax.ppermute(v, "core", [(0, 1), (1, 0)])


def alike(size, by):
    return [(i, i ^ by) for i in range(size)]


def over_chips(v):
    return lax.all_to_all(v, "chip", 0, 0)


def fold(x, axis, partner):
    return x + lax.ppermute(x, axis, [(i, partner(i)) for i in range(lax.axis_size(axis))])


def sum_four(x, axis, block=1):
    near, far, last = (
        lax.ppermute(x, axis, [(i, (i // block ^ k) * block + i % block) for i in range(lax.axis_size(axis))])
        for k in range(1, 4)
    )
    return (x + near) + (far + last)


def mirror(within):
    return lambda i: i // within * within + within - 1 - i % within


def body(
    x_raw, b_raw, c_raw, z_gate, dt_raw, conv_x, conv_b, conv_c, dt_bias, a_log, d_skip, gain, grad_out
):
    size = lax.axis_size(CTX)
    core = lax.axis_index("core")
    side = lax.axis_index("tp") // (lax.axis_size("tp") // 2)
    cores, sides = lax.optimization_barrier((core.reshape(1), side.reshape(1)))
    is_even = core == 0
    t_shape = ((ALL, SPAN), F32)
    bc_shape = ((SPAN, GROUPS * STATE), F32)
    h_shape = ((LOCAL, SPAN), F32)
    tails = jnp.concatenate([v[SPAN - LEAD :] for v in (x_raw, b_raw, c_raw)], axis=1)
    before = lax.ppermute(tails, CTX, [(i, i + 1) for i in range(size - 1)])
    wx, wb = x_raw.shape[1], b_raw.shape[1]

    dt, per_head, step, cum, ends, skip = call(
        steps_kernel,
        "steps",
        [h_shape, ((LOCAL, 8), F32)] + [h_shape] * 4,
        (dt_raw.T, dt_bias[None], a_log[None], d_skip[None]),
    )
    zt, ogt, sgt = call(turn_kernel, "turn", [t_shape] * 3, (z_gate, grad_out, gain[None]))
    before, zt, ogt, sgt = lax.optimization_barrier((before, zt, ogt, sgt))
    xt, zs, bc, keep, give = call(
        state_kernel,
        "state",
        [t_shape, t_shape, bc_shape, ((HALF, STATE), F32), ((HALF + LOCAL, STATE), F32)],
        (cores, x_raw, b_raw, before, conv_x, conv_b, step, cum, ends),
        [(LEAD + SPAN, wx), (LEAD + SPAN, wb), (ALL, STATE)],
        scalars=1,
    )
    got = swap_cores(give)
    half_shape = ((HALF, STATE), F32)
    chips = lax.axis_size("chip")
    joint, pair = call(
        join_first_kernel,
        "join",
        [((chips, 1, CHUNK + TILE), F32), h_shape],
        (cores, keep, got, ends),
        scalars=1,
    )
    firsts = over_chips(joint)
    (entering,) = call(
        functools.partial(scan_kernel, False), "block_scan", [((chips, 1, CHUNK), F32)], (firsts, firsts)
    )
    ahead = over_chips(entering).reshape(HALF, STATE)
    enter_own, enter_give = call(
        functools.partial(split_kernel, 0), "split", [half_shape] * 2, (cores, ahead, keep, got, pair), scalars=1
    )
    enter_got = swap_cores(enter_give)

    cc, mt, y1 = call(
        local_kernel,
        "local",
        [bc_shape, ((GROUPS * SPAN, SPAN), F32), t_shape],
        (c_raw, before, conv_c, bc, xt, zs, cum, skip),
        [(LEAD + SPAN, wb)],
    )
    enter, y, sums = call(
        output_kernel,
        "output",
        [t_shape, t_shape, ((2 * GROUPS, SPAN), F32)],
        (cores, enter_own, enter_got, cc, y1, cum, zt, sgt),
        scalars=1,
    )
    sums = sum_four(sums, "tp")
    keep, give, dy, dg = call(
        gate_kernel,
        "gate",
        [((HALF, STATE), F32)] * 2 + [t_shape, t_shape],
        (cores, sums, y, zt, sgt, cum, cc),
        [(ALL, STATE)],
        scalars=1,
    )
    got = swap_cores(give)
    (joint,) = call(join_again_kernel, "join", [half_shape], (cores, keep, got, pair), scalars=1)
    pieces = over_chips(joint.reshape(chips, 1, CHUNK))
    (leaving,) = call(
        functools.partial(scan_kernel, True), "block_scan", [((chips, 1, CHUNK), F32)], (pieces, firsts)
    )
    ahead = over_chips(leaving).reshape(HALF, STATE)
    later_own, later_give = call(
        functools.partial(split_kernel, 1), "split", [half_shape] * 2, (cores, ahead, keep, got, pair), scalars=1
    )
    later_got = swap_cores(later_give)
    dz, db, dcum, dskip, grad_z, early, cpart = call(
        middle_kernel,
        "middle",
        [t_shape, bc_shape, h_shape, h_shape, ((SPAN, wx), jnp.bfloat16), ((24, TILE), F32)]
        + [((GROUPS, SPAN + 8, TILE), F32)],
        (sums, y, zt, ogt, dy, dg, enter, mt, zs, xt, bc, cc, cum, skip, c_raw, before, conv_c),
        [(LEAD + SPAN, wb), (LEAD + SPAN, wb), (SPAN, wb)],
    )
    half_parts = ((2, 2 * SPAN + 16, TILE), F32)
    xown, xheads, keep, give, packed, ddt = call(
        last_kernel,
        "last",
        [((SPAN, wx), F32), ((64, TILE), F32), half_parts, half_parts, ((80, TILE), F32), h_shape],
        (cores, sides, later_own, later_got, enter, ends, dz, db, dcum, dskip, early, cpart)
        + (dy, zs, xt, bc, cum, step, skip, dt, per_head, x_raw, conv_x, b_raw, conv_b, before),
        [(GROUPS, 2 * SPAN + 16, TILE), (ALL, STATE)]
        + [(LEAD + SPAN, wx), (LEAD + SPAN, wb), (LEAD + SPAN, wx), (LEAD + SPAN, wb)],
        scalars=2,
    )
    peers = lax.axis_size("tp")
    across = [(i, peers - 1 - i) for i in range(peers)]
    arrived = lax.ppermute(give, "tp", across)
    packed = packed + swap_cores(packed)
    packed = fold(packed, "chip", mirror(2))
    packed = fold(packed, "chip", lambda i: i ^ 2)
    arrived, packed = lax.optimization_barrier((arrived, packed))
    mine = keep + arrived
    arrived = lax.ppermute(mine, "tp", [(i, i ^ 1) for i in range(peers)])
    packed = fold(packed, "chip", mirror(RING))
    mine = mine + arrived
    heads = jnp.concatenate([xheads, mine[:, 2 * SPAN :].reshape(32, TILE)], axis=0)
    mine, heads, packed = lax.optimization_barrier((mine, heads, packed))
    heads = lax.ppermute(heads, CTX, [(i + 1, i) for i in range(size - 1)])
    grad_x_raw, half = call(
        settle_kernel,
        "settle",
        [((SPAN, wx), jnp.bfloat16), ((2, 2 * SPAN, TILE), jnp.bfloat16)],
        (xown, mine, heads),
    )
    half, packed = lax.optimization_barrier((half, packed))
    other = lax.ppermute(half, "tp", across)
    packed = sum_four(packed, "chip", RING)
    bc_taps = sum_four(packed[:32], "tp")
    half_bc, each = ((SPAN, wb), jnp.bfloat16), ((1, LOCAL), F32)
    grad_b_raw, grad_c_raw, conv_x_total, conv_b_total, conv_c_total, gain_total, *small = call(
        finish_kernel,
        "finish",
        [half_bc, half_bc, ((CONV, wx), F32), ((CONV, wb), F32), ((CONV, wb), F32), ((1, wx), F32)] + [each] * 3,
        (sides, half, other, bc_taps, packed),
        scalars=1,
    )
    return (
        grad_x_raw,
        grad_b_raw,
        grad_c_raw,
        grad_z,
        ddt.T,
        conv_x_total,
        conv_b_total,
        conv_c_total,
        *(v.reshape(-1) for v in small),
        gain_total.reshape(-1),
    )


def solution(mesh):
    rows, cols, some = P(CTX, "tp"), P(None, "tp"), P("tp")
    chips, tp = mesh.shape["ctx"] // 2, mesh.shape["tp"]
    mesh = Mesh(mesh.devices.reshape(chips, 2, tp), (*CTX, "tp"))
    return jax.shard_map(
        body,
        mesh=mesh,
        in_specs=(rows, P(CTX, None), P(CTX, None), rows, rows, cols, P(), P(), some, some, some, some, rows),
        out_specs=(rows, P(CTX, None), P(CTX, None), rows, rows, cols, P(), P(), some, some, some, some),
        check_vma=False,
    )
```

```python
import functools

import jax
import jax.numpy as jnp
from jax import lax
from jax.experimental import pallas as pl
from jax.experimental.pallas import tpu as pltpu
from jax.sharding import Mesh, PartitionSpec as P

HEAD_DIM = 32
STATE = 128
GROUPS = 4
CONV = 4
SPAN = 128
TILE = 128
PER = 8
LOCAL = PER * GROUPS
ROWS = PER * HEAD_DIM
ALL = LOCAL * HEAD_DIM
HALF = ALL // 2
CHUNK = 2048
LEAD = 16
GROUP_WIDTH = 1024
EPSILON = 1e-05
F32 = jnp.float32
CTX = ("chip", "core")
RING = 8
PARAMS = pltpu.CompilerParams(vmem_limit_bytes=16 << 20)


def exact(a, b, ca=1, cb=0):
    return lax.dot_general(
        a, b, (((ca,), (cb,)), ((), ())), precision=lax.Precision.HIGHEST, preferred_element_type=F32
    )


def dot(a, b, ca=1, cb=0):
    high_a, high_b = a.astype(jnp.bfloat16), b.astype(jnp.bfloat16)
    low_a = (a - high_a.astype(F32)).astype(jnp.bfloat16)
    low_b = (b - high_b.astype(F32)).astype(jnp.bfloat16)

    def part(x, y):
        return lax.dot_general(x, y, (((ca,), (cb,)), ((), ())), preferred_element_type=F32)

    return part(high_a, high_b) + (part(high_a, low_b) + part(low_a, high_b))


def group(g):
    return slice(g * ROWS, (g + 1) * ROWS)


def lanes(r):
    return slice(r * TILE, (r + 1) * TILE)


def spot(g, r):
    return slice(g * ROWS + r * HEAD_DIM, g * ROWS + (r + 1) * HEAD_DIM)


def put(dst, r, tile):
    turned = tile.T
    for g in range(GROUPS):
        dst[spot(g, r), :] = turned[g * HEAD_DIM : (g + 1) * HEAD_DIM]


def take(values, r):
    rows = slice(r * HEAD_DIM, (r + 1) * HEAD_DIM)
    return jnp.concatenate([v[rows] for v in values], axis=0).T


def heads_out(v, g):
    return jnp.concatenate(
        [jnp.broadcast_to(v[g * PER + r : g * PER + r + 1], (HEAD_DIM, v.shape[1])) for r in range(PER)], axis=0
    )


def heads_in(v):
    return jnp.concatenate(
        [jnp.sum(v[r * HEAD_DIM : (r + 1) * HEAD_DIM], axis=0, keepdims=True) for r in range(PER)], axis=0
    )


def sigmoid(v):
    return 1.0 / (1.0 + jnp.exp(-v))


def silu_slope(v):
    s = sigmoid(v)
    return s * (1.0 + v * (1.0 - s))


def extend(ext, raw, before, at):
    ext[0:LEAD, :] = before[:, at : at + ext.shape[1]].astype(F32)
    ext[LEAD : LEAD + SPAN, :] = raw[...].astype(F32)


def group_order():
    to = lax.broadcasted_iota(jnp.int32, (LOCAL, LOCAL), 0)
    at = lax.broadcasted_iota(jnp.int32, (LOCAL, LOCAL), 1)
    return jnp.where(at == to % PER * GROUPS + to // PER, 1.0, 0.0)


def conv_tile(ext, w, cols):
    total = w[0:1, cols] * ext[LEAD - 3 : LEAD - 3 + SPAN, cols]
    for k in range(1, CONV):
        total = total + w[k : k + 1, cols] * ext[LEAD - 3 + k : LEAD - 3 + k + SPAN, cols]
    return total


def conv_back_tile(ext, pad, w, cols, grad):
    dpre = grad * silu_slope(conv_tile(ext, w, cols))
    pad[8 : 8 + SPAN, cols] = dpre
    taps = [
        jnp.sum(dpre * ext[LEAD - 3 + k : LEAD - 3 + k + SPAN, cols], axis=0, keepdims=True) for k in range(CONV)
    ]
    mine = w[0:1, cols] * pad[11 : 11 + SPAN, cols]
    ahead = w[0:1, cols] * pad[3:11, cols]
    for k in range(1, CONV):
        mine = mine + w[k : k + 1, cols] * pad[11 - k : 11 - k + SPAN, cols]
        ahead = ahead + w[k : k + 1, cols] * pad[3 - k : 11 - k, cols]
    return mine, ahead, taps


def clear_pad(pad):
    pad[0:8, :] = jnp.zeros((8, pad.shape[1]), F32)
    pad[8 + SPAN : 16 + SPAN, :] = jnp.zeros((8, pad.shape[1]), F32)


def halves(core, full, keep, give):
    keep[...] = full[pl.ds(pl.multiple_of(core * HALF, HALF), HALF), :]
    give[0:HALF, :] = full[pl.ds(pl.multiple_of((1 - core) * HALF, HALF), HALF), :]


def unite(core, full, own, got):
    full[pl.ds(pl.multiple_of(core * HALF, HALF), HALF), :] = own[...]
    full[pl.ds(pl.multiple_of((1 - core) * HALF, HALF), HALF), :] = got[...]


def triangle(upper):
    rows = lax.broadcasted_iota(jnp.int32, (SPAN, SPAN), 0)
    cols = lax.broadcasted_iota(jnp.int32, (SPAN, SPAN), 1)
    return rows <= cols if upper else rows >= cols


def steps_kernel(raw, bias, alog, d_skip, dt, heads, step, cum, ends, skip):
    order = group_order()
    dt[...] = exact(order, raw[...])
    rows = jnp.concatenate([bias[...], alog[...], d_skip[...], jnp.zeros((5, LOCAL), F32)], axis=0)
    heads[...] = exact(order, rows, 1, 1)
    v = dt[...] + heads[:, 0:1]
    skip[...] = jnp.broadcast_to(heads[:, 2:3], skip.shape)
    step[...] = jnp.maximum(v, 0.0) + jnp.log1p(jnp.exp(-jnp.abs(v)))
    rates = -jnp.exp(heads[:, 1:2]) * step[...]
    cum[...] = exact(rates, jnp.where(triangle(True), 1.0, 0.0))
    ends[...] = jnp.broadcast_to(jnp.exp(jnp.sum(rates, axis=1, keepdims=True)), ends.shape)


def turn_kernel(z, og, gain, zt, ogt, sgt):
    for r in range(PER):
        put(zt, r, z[:, lanes(r)].astype(F32))
        tile = og[:, lanes(r)].astype(F32)
        put(ogt, r, tile)
        put(sgt, r, tile * gain[:, lanes(r)])


def state_kernel(core, x, b, before, wx, wb, step, cum, ends, xt, zs, bc, keep, give, ext, extb, full):
    extend(ext, x, before, 0)
    extend(extb, b, before, x.shape[1])
    for g in range(GROUPS):
        pre = conv_tile(extb, wb, lanes(g))
        bc[:, lanes(g)] = pre * sigmoid(pre)
    for r in range(PER):
        pre = conv_tile(ext, wx, lanes(r))
        put(xt, r, pre * sigmoid(pre))
    scale = jnp.exp(-cum[...]) * step[...]
    for g in range(GROUPS):
        zg = xt[group(g), :] * heads_out(scale, g)
        zs[group(g), :] = zg
        full[group(g), :] = heads_out(ends[...], g) * dot(zg, bc[:, lanes(g)])
    halves(core[0], full, keep, give)
    give[HALF : HALF + LOCAL, :] = ends[...]


def local_kernel(c, before, wc, bc, xt, zs, cum, skip, cc, mt, y, extc):
    extend(extc, c, before, before.shape[1] - c.shape[1])
    alpha = jnp.exp(cum[...])
    causal = triangle(True)
    for g in range(GROUPS):
        pre = conv_tile(extc, wc, lanes(g))
        cg = pre * sigmoid(pre)
        cc[:, lanes(g)] = cg
        m = jnp.where(causal, dot(bc[:, lanes(g)], cg, 1, 1), 0.0)
        mt[lanes(g), :] = m
        y[group(g), :] = heads_out(alpha, g) * dot(zs[group(g), :], m) + heads_out(skip[...], g) * xt[group(g), :]


def output_kernel(core, own, got, cc, y1, cum, zt, sgt, full, y, sums):
    unite(core[0], full, own, got)
    alpha = jnp.exp(cum[...])
    for g in range(GROUPS):
        yg = y1[group(g), :] + heads_out(alpha, g) * dot(full[group(g), :], cc[:, lanes(g)], 1, 1)
        y[group(g), :] = yg
        z = zt[group(g), :]
        gated = yg * z * sigmoid(z)
        sums[g : g + 1, :] = jnp.sum(gated * gated, axis=0, keepdims=True)
        sums[GROUPS + g : GROUPS + g + 1, :] = jnp.sum(sgt[group(g), :] * gated, axis=0, keepdims=True)


def gate_kernel(core, sums, y, zt, sgt, cum, cc, keep, give, dy, dg, full):
    alpha = jnp.exp(cum[...])
    for g in range(GROUPS):
        inv = lax.rsqrt(sums[g : g + 1, :] / GROUP_WIDTH + EPSILON)
        fix = inv * inv * inv * sums[GROUPS + g : GROUPS + g + 1, :] / GROUP_WIDTH
        z = zt[group(g), :]
        act = z * sigmoid(z)
        dgated = inv * sgt[group(g), :] - y[group(g), :] * act * fix
        dg[group(g), :] = dgated
        dyg = dgated * act
        dy[group(g), :] = dyg
        full[group(g), :] = dot(heads_out(alpha, g) * dyg, cc[:, lanes(g)])
    halves(core[0], full, keep, give)


def middle_kernel(
    sums, y, zt, ogt, dy, dg, full, mt, zs, xt, bc, cc, cum, skip, c, before, wc,
    dz, db, dcum, dskip, gz, early, cpart, extc, padc, dc,
):
    alpha = jnp.exp(cum[...])
    causal = triangle(True)
    slope, shares = [], []
    for g in range(GROUPS):
        z, yg, dyg = zt[group(g), :], y[group(g), :], dy[group(g), :]
        inv = lax.rsqrt(sums[g : g + 1, :] / GROUP_WIDTH + EPSILON)
        slope.append(dg[group(g), :] * yg * silu_slope(z))
        shares.append(ogt[group(g), :] * yg * z * sigmoid(z) * inv)
        heads = slice(g * PER, (g + 1) * PER)
        x = xt[group(g), :]
        passed = heads_in(dyg * x)
        dskip[heads, :] = passed
        dcum[heads, :] = heads_in(dyg * (yg - heads_out(skip[...], g) * x))
        u = heads_out(alpha, g) * dyg
        dz[group(g), :] = dot(u, mt[lanes(g), :], 1, 1)
        dm = jnp.where(causal, dot(zs[group(g), :], u, 0, 0), 0.0)
        dc[:, lanes(g)] = dot(dm, bc[:, lanes(g)], 0, 0) + dot(u, full[group(g), :], 0, 0)
        db[:, lanes(g)] = dot(dm, cc[:, lanes(g)])
    for r in range(PER):
        gz[:, lanes(r)] = take(slope, r).astype(jnp.bfloat16)
        early[16 + r : 17 + r, :] = jnp.sum(take(shares, r), axis=0, keepdims=True)
    extend(extc, c, before, before.shape[1] - c.shape[1])
    clear_pad(padc)
    for g in range(GROUPS):
        mine, ahead, taps = conv_back_tile(extc, padc, wc, lanes(g), dc[:, lanes(g)])
        cpart[g, 0:SPAN, :] = mine
        cpart[g, SPAN : SPAN + 8, :] = ahead
        for k in range(CONV):
            early[k * GROUPS + g : k * GROUPS + g + 1, :] = taps[k]


def last_kernel(
    core, which, own, got, full, ends, dz1, db1, dcum1, dskip, early, cpart, dy, zs, xt, bc, cum, step, skip, dt, per_head,
    x, wx, b, wb, before,
    xown, heads, keep, give, packed, ddt, parts, later, ext, extb, pad, padb,
):
    unite(core[0], later, own, got)
    gamma = jnp.exp(-cum[...])
    scale = gamma * step[...]
    clear_pad(pad)
    clear_pad(padb)
    extend(ext, x, before, 0)
    extend(extb, b, before, x.shape[1])
    dxs, turned, straight = [], [], []
    at_end = lax.broadcasted_iota(jnp.int32, (PER, SPAN), 1) == SPAN - 1
    for g in range(GROUPS):
        here = slice(g * PER, (g + 1) * PER)
        zg, xg = zs[group(g), :], xt[group(g), :]
        d = heads_out(ends[...], g) * later[group(g), :]
        second = dot(d, bc[:, lanes(g)], 1, 1)
        dzg = dz1[group(g), :] + second
        dxs.append(heads_out(scale, g) * dzg + heads_out(skip[...], g) * dy[group(g), :])
        edge = heads_in(zg * second + d * full[group(g), :])
        edge = jnp.sum(edge, axis=1, keepdims=True)
        turned.append(dcum1[here, :] - heads_in(dzg * zg) + jnp.where(at_end, edge, 0.0))
        straight.append(heads_in(dzg * xg))
        dbg = db1[:, lanes(g)] + dot(zg, d, 0, 0)
        mine, ahead, taps = conv_back_tile(extb, padb, wb, lanes(g), dbg)
        parts[g, 0:SPAN, :] = mine
        parts[g, SPAN : 2 * SPAN, :] = cpart[g, 0:SPAN, :]
        parts[g, 2 * SPAN : 2 * SPAN + 8, :] = ahead
        parts[g, 2 * SPAN + 8 : 2 * SPAN + 16, :] = cpart[g, SPAN : SPAN + 8, :]
        for k in range(CONV):
            packed[k * GROUPS + g : k * GROUPS + g + 1, :] = taps[k]
    dlog = exact(jnp.concatenate(turned, axis=0), jnp.where(triangle(False), 1.0, 0.0))
    rate = -jnp.exp(per_head[:, 1:2])
    dstep = jnp.concatenate(straight, axis=0) * gamma + dlog * rate
    draw = dstep * sigmoid(dt[...] + per_head[:, 0:1])
    ddt[...] = exact(group_order(), draw, 0, 0)
    each = jnp.concatenate([draw, dlog * rate * step[...], dskip[...], jnp.zeros((LOCAL, SPAN), F32)], axis=0)
    at = lax.broadcasted_iota(jnp.int32, (SPAN, SPAN), 0)
    to = lax.broadcasted_iota(jnp.int32, (SPAN, SPAN), 1)
    source = to // LOCAL * LOCAL + to % GROUPS * PER + to % LOCAL // GROUPS
    packed[72:80, :] = exact(exact(jnp.ones((8, SPAN), F32), each, 1, 1), jnp.where(at == source, 1.0, 0.0))
    packed[16:32, :] = early[0:16, :]
    packed[64:72, :] = early[16:24, :]
    side = which[0]
    keep[...] = parts[pl.ds(side * 2, 2)]
    give[...] = parts[pl.ds((1 - side) * 2, 2)]
    for r in range(PER):
        mine, ahead, taps = conv_back_tile(ext, pad, wx, lanes(r), take(dxs, r))
        xown[:, lanes(r)] = mine
        heads[8 * r : 8 * r + 8, :] = ahead
        for k in range(CONV):
            packed[32 + k * PER + r : 33 + k * PER + r, :] = taps[k]


def pair_decays(core, pair, lead):
    mine, theirs = pair[0 : LOCAL // 2, :], pair[LOCAL // 2 : LOCAL, :]
    leads = core == lead
    return jnp.where(leads, mine, theirs), jnp.where(leads, theirs, mine), leads


def join_first_kernel(core, keep, got, ends, joint, pair):
    half = LOCAL // 2
    pair[0:half, :] = ends[pl.ds(pl.multiple_of(core[0] * half, half), half), :]
    pair[half:LOCAL, :] = got[pl.ds(pl.multiple_of(HALF + core[0] * half, half), half), :]
    first, second, leads = pair_decays(core[0], pair, 0)
    for h in range(half):
        rows = slice(h * HEAD_DIM, (h + 1) * HEAD_DIM)
        mine, theirs = keep[rows, :], got[rows, :]
        both = second[h : h + 1] * jnp.where(leads, mine, theirs) + jnp.where(leads, theirs, mine)
        for i in range(HEAD_DIM):
            joint[2 * h + i // 16, :, lanes(i % 16)] = both[i : i + 1]
        for i in range(2):
            joint[2 * h + i, :, CHUNK:] = first[h : h + 1] * second[h : h + 1]


def join_again_kernel(core, keep, got, pair, joint):
    _, second, leads = pair_decays(core[0], pair, 1)
    for h in range(LOCAL // 2):
        rows = slice(h * HEAD_DIM, (h + 1) * HEAD_DIM)
        mine, theirs = keep[rows, :], got[rows, :]
        joint[rows, :] = second[h : h + 1] * jnp.where(leads, mine, theirs) + jnp.where(leads, theirs, mine)


def split_kernel(lead, core, ahead, keep, got, pair, own, give):
    first, _, leads = pair_decays(core[0], pair, lead)
    for h in range(LOCAL // 2):
        rows = slice(h * HEAD_DIM, (h + 1) * HEAD_DIM)
        far = ahead[rows, :]
        near = first[h : h + 1] * far + jnp.where(leads, keep[rows, :], got[rows, :])
        own[rows, :] = jnp.where(leads, far, near)
        give[rows, :] = jnp.where(leads, near, far)


def settle_kernel(xown, mine, heads, gx, half):
    last = slice(SPAN - LEAD, SPAN)
    none = jnp.zeros((LEAD - 8, TILE), F32)
    for r in range(PER):
        gx[0 : SPAN - LEAD, lanes(r)] = xown[0 : SPAN - LEAD, lanes(r)].astype(jnp.bfloat16)
        more = jnp.concatenate([none, heads[8 * r : 8 * r + 8, :]], axis=0)
        gx[last, lanes(r)] = (xown[last, lanes(r)] + more).astype(jnp.bfloat16)
    for g in range(2):
        for i in range(2):
            at = 64 + 16 * g + 8 * i
            more = jnp.concatenate([none, heads[at : at + 8, :]], axis=0)
            start, stop = i * SPAN, (i + 1) * SPAN
            half[g, start : stop - LEAD, :] = mine[g, start : stop - LEAD, :].astype(jnp.bfloat16)
            half[g, stop - LEAD : stop, :] = (mine[g, stop - LEAD : stop, :] + more).astype(jnp.bfloat16)


def place_kernel(which, half, other, gb, gc):
    left = which[0] == 0
    for g in range(GROUPS):
        first, second = (half, other) if g < 2 else (other, half)
        both = jnp.where(left, first[g % 2].astype(F32), second[g % 2].astype(F32)).astype(jnp.bfloat16)
        gb[:, lanes(g)] = both[0:SPAN]
        gc[:, lanes(g)] = both[SPAN : 2 * SPAN]


def finish_kernel(bc_taps, packed, tx, tb, tc, tgain, bias, rate, skip):
    for k in range(CONV):
        for g in range(GROUPS):
            tb[k : k + 1, lanes(g)] = bc_taps[k * GROUPS + g : k * GROUPS + g + 1, :]
            tc[k : k + 1, lanes(g)] = bc_taps[16 + k * GROUPS + g : 17 + k * GROUPS + g, :]
        for r in range(PER):
            tx[k : k + 1, lanes(r)] = packed[32 + k * PER + r : 33 + k * PER + r, :]
    for r in range(PER):
        tgain[:, lanes(r)] = packed[64 + r : 65 + r, :]
    bias[...] = packed[72:73, 0:LOCAL]
    rate[...] = packed[72:73, LOCAL : 2 * LOCAL]
    skip[...] = packed[72:73, 2 * LOCAL : 3 * LOCAL]


def scan_kernel(backward, s, d, o):
    count = s.shape[0]
    at = d.shape[2] - TILE
    carry = [jnp.zeros((1, TILE), F32)] * (CHUNK // TILE)
    for j in range(count):
        j = count - 1 - j if backward else j
        decay = d[j, :, at:]
        for k in range(CHUNK // TILE):
            o[j, :, lanes(k)] = carry[k]
            carry[k] = decay * carry[k] + s[j, :, lanes(k)]


def call(kernel, name, outs, args, scratch=(), scalars=0, flops=20_000_000):
    smem = pl.BlockSpec(memory_space=pltpu.SMEM)
    vmem = pl.BlockSpec(memory_space=pltpu.VMEM)
    return pl.pallas_call(
        kernel,
        out_shape=[jax.ShapeDtypeStruct(s, d) for s, d in outs],
        in_specs=[smem if i < scalars else vmem for i in range(len(args))],
        out_specs=[vmem] * len(outs),
        scratch_shapes=[pltpu.VMEM(s, F32) for s in scratch],
        compiler_params=PARAMS,
        cost_estimate=pl.CostEstimate(flops=flops, bytes_accessed=4 << 20, transcendentals=1 << 18),
        name=name,
    )(*args)


def swap_cores(v):
    return lax.ppermute(v, "core", [(0, 1), (1, 0)])


def alike(size, by):
    return [(i, i ^ by) for i in range(size)]


def over_chips(v):
    return lax.all_to_all(v, "chip", 0, 0)


def fold(x, axis, partner):
    return x + lax.ppermute(x, axis, [(i, partner(i)) for i in range(lax.axis_size(axis))])


def sum_four(x, axis, block=1, behind=None):
    sent = [
        lax.ppermute(x, axis, [(i, (i // block ^ k) * block + i % block) for i in range(lax.axis_size(axis))])
        for k in range(1, 4)
    ]
    if behind is not None:
        *sent, behind = lax.optimization_barrier((*sent, behind))
    near, far, last = sent
    total = (x + near) + (far + last)
    return total if behind is None else (total, behind)


def mirror(within):
    return lambda i: i // within * within + within - 1 - i % within


def body(
    x_raw, b_raw, c_raw, z_gate, dt_raw, conv_x, conv_b, conv_c, dt_bias, a_log, d_skip, gain, grad_out
):
    size = lax.axis_size(CTX)
    core = lax.axis_index("core")
    side = lax.axis_index("tp") // (lax.axis_size("tp") // 2)
    cores, sides = lax.optimization_barrier((core.reshape(1), side.reshape(1)))
    is_even = core == 0
    t_shape = ((ALL, SPAN), F32)
    bc_shape = ((SPAN, GROUPS * STATE), F32)
    h_shape = ((LOCAL, SPAN), F32)
    tails = jnp.concatenate([v[SPAN - LEAD :] for v in (x_raw, b_raw, c_raw)], axis=1)
    before = lax.ppermute(tails, CTX, [(i, i + 1) for i in range(size - 1)])
    wx, wb = x_raw.shape[1], b_raw.shape[1]

    dt, per_head, step, cum, ends, skip = call(
        steps_kernel,
        "steps",
        [h_shape, ((LOCAL, 8), F32)] + [h_shape] * 4,
        (dt_raw.T, dt_bias[None], a_log[None], d_skip[None]),
    )
    zt, ogt, sgt = call(turn_kernel, "turn", [t_shape] * 3, (z_gate, grad_out, gain[None]))
    before, zt, ogt, sgt = lax.optimization_barrier((before, zt, ogt, sgt))
    xt, zs, bc, keep, give = call(
        state_kernel,
        "state",
        [t_shape, t_shape, bc_shape, ((HALF, STATE), F32), ((HALF + LOCAL, STATE), F32)],
        (cores, x_raw, b_raw, before, conv_x, conv_b, step, cum, ends),
        [(LEAD + SPAN, wx), (LEAD + SPAN, wb), (ALL, STATE)],
        scalars=1,
    )
    got = swap_cores(give)
    half_shape = ((HALF, STATE), F32)
    chips = lax.axis_size("chip")
    joint, pair = call(
        join_first_kernel,
        "join",
        [((chips, 1, CHUNK + TILE), F32), h_shape],
        (cores, keep, got, ends),
        scalars=1,
    )
    firsts = over_chips(joint)
    (entering,) = call(
        functools.partial(scan_kernel, False), "block_scan", [((chips, 1, CHUNK), F32)], (firsts, firsts)
    )
    ahead = over_chips(entering).reshape(HALF, STATE)
    enter_own, enter_give = call(
        functools.partial(split_kernel, 0), "split", [half_shape] * 2, (cores, ahead, keep, got, pair), scalars=1
    )
    enter_got = swap_cores(enter_give)

    cc, mt, y1 = call(
        local_kernel,
        "local",
        [bc_shape, ((GROUPS * SPAN, SPAN), F32), t_shape],
        (c_raw, before, conv_c, bc, xt, zs, cum, skip),
        [(LEAD + SPAN, wb)],
    )
    enter, y, sums = call(
        output_kernel,
        "output",
        [t_shape, t_shape, ((2 * GROUPS, SPAN), F32)],
        (cores, enter_own, enter_got, cc, y1, cum, zt, sgt),
        scalars=1,
    )
    sums = sum_four(sums, "tp")
    keep, give, dy, dg = call(
        gate_kernel,
        "gate",
        [((HALF, STATE), F32)] * 2 + [t_shape, t_shape],
        (cores, sums, y, zt, sgt, cum, cc),
        [(ALL, STATE)],
        scalars=1,
    )
    got = swap_cores(give)
    (joint,) = call(join_again_kernel, "join", [half_shape], (cores, keep, got, pair), scalars=1)
    pieces = over_chips(joint.reshape(chips, 1, CHUNK))
    (leaving,) = call(
        functools.partial(scan_kernel, True), "block_scan", [((chips, 1, CHUNK), F32)], (pieces, firsts)
    )
    ahead = over_chips(leaving).reshape(HALF, STATE)
    later_own, later_give = call(
        functools.partial(split_kernel, 1), "split", [half_shape] * 2, (cores, ahead, keep, got, pair), scalars=1
    )
    later_got = swap_cores(later_give)
    dz, db, dcum, dskip, grad_z, early, cpart = call(
        middle_kernel,
        "middle",
        [t_shape, bc_shape, h_shape, h_shape, ((SPAN, wx), jnp.bfloat16), ((24, TILE), F32)]
        + [((GROUPS, SPAN + 8, TILE), F32)],
        (sums, y, zt, ogt, dy, dg, enter, mt, zs, xt, bc, cc, cum, skip, c_raw, before, conv_c),
        [(LEAD + SPAN, wb), (LEAD + SPAN, wb), (SPAN, wb)],
    )
    half_parts = ((2, 2 * SPAN + 16, TILE), F32)
    xown, xheads, keep, give, packed, ddt = call(
        last_kernel,
        "last",
        [((SPAN, wx), F32), ((64, TILE), F32), half_parts, half_parts, ((80, TILE), F32), h_shape],
        (cores, sides, later_own, later_got, enter, ends, dz, db, dcum, dskip, early, cpart)
        + (dy, zs, xt, bc, cum, step, skip, dt, per_head, x_raw, conv_x, b_raw, conv_b, before),
        [(GROUPS, 2 * SPAN + 16, TILE), (ALL, STATE)]
        + [(LEAD + SPAN, wx), (LEAD + SPAN, wb), (LEAD + SPAN, wx), (LEAD + SPAN, wb)],
        scalars=2,
    )
    peers = lax.axis_size("tp")
    across = [(i, peers - 1 - i) for i in range(peers)]
    arrived = lax.ppermute(give, "tp", across)
    packed = packed + swap_cores(packed)
    packed = fold(packed, "chip", mirror(2))
    packed = fold(packed, "chip", lambda i: i ^ 2)
    arrived, packed = lax.optimization_barrier((arrived, packed))
    mine = keep + arrived
    arrived = lax.ppermute(mine, "tp", [(i, i ^ 1) for i in range(peers)])
    packed = fold(packed, "chip", mirror(RING))
    mine = mine + arrived
    heads = jnp.concatenate([xheads, mine[:, 2 * SPAN :].reshape(32, TILE)], axis=0)
    mine, heads, packed = lax.optimization_barrier((mine, heads, packed))
    heads = lax.ppermute(heads, CTX, [(i + 1, i) for i in range(size - 1)])
    grad_x_raw, half = call(
        settle_kernel,
        "settle",
        [((SPAN, wx), jnp.bfloat16), ((2, 2 * SPAN, TILE), jnp.bfloat16)],
        (xown, mine, heads),
    )
    half, packed = lax.optimization_barrier((half, packed))
    other = lax.ppermute(half, "tp", across)
    half_bc, each = ((SPAN, wb), jnp.bfloat16), ((1, LOCAL), F32)
    grad_b_raw, grad_c_raw = call(
        place_kernel, "place", [half_bc, half_bc], (sides, half, other), scalars=1, flops=20_000_000_000
    )
    packed, grad_b_raw = sum_four(packed, "chip", RING, grad_b_raw)
    bc_taps = sum_four(packed[:32], "tp")
    conv_x_total, conv_b_total, conv_c_total, gain_total, *small = call(
        finish_kernel,
        "finish",
        [((CONV, wx), F32), ((CONV, wb), F32), ((CONV, wb), F32), ((1, wx), F32)] + [each] * 3,
        (bc_taps, packed),
    )
    return (
        grad_x_raw,
        grad_b_raw,
        grad_c_raw,
        grad_z,
        ddt.T,
        conv_x_total,
        conv_b_total,
        conv_c_total,
        *(v.reshape(-1) for v in small),
        gain_total.reshape(-1),
    )


def solution(mesh):
    rows, cols, some = P(CTX, "tp"), P(None, "tp"), P("tp")
    chips, tp = mesh.shape["ctx"] // 2, mesh.shape["tp"]
    mesh = Mesh(mesh.devices.reshape(chips, 2, tp), (*CTX, "tp"))
    return jax.shard_map(
        body,
        mesh=mesh,
        in_specs=(rows, P(CTX, None), P(CTX, None), rows, rows, cols, P(), P(), some, some, some, some, rows),
        out_specs=(rows, P(CTX, None), P(CTX, None), rows, rows, cols, P(), P(), some, some, some, some),
        check_vma=False,
    )
```

```python
import functools

import jax
import jax.numpy as jnp
from jax import lax
from jax.experimental import pallas as pl
from jax.experimental.pallas import tpu as pltpu
from jax.sharding import Mesh, PartitionSpec as P

HEAD_DIM = 32
STATE = 128
GROUPS = 4
CONV = 4
SPAN = 128
TILE = 128
PER = 8
LOCAL = PER * GROUPS
ROWS = PER * HEAD_DIM
ALL = LOCAL * HEAD_DIM
HALF = ALL // 2
CHUNK = 2048
LEAD = 16
GROUP_WIDTH = 1024
EPSILON = 1e-05
F32 = jnp.float32
CTX = ("chip", "core")
RING = 8
PARAMS = pltpu.CompilerParams(vmem_limit_bytes=16 << 20)


def exact(a, b, ca=1, cb=0):
    return lax.dot_general(
        a, b, (((ca,), (cb,)), ((), ())), precision=lax.Precision.HIGHEST, preferred_element_type=F32
    )


def dot(a, b, ca=1, cb=0):
    high_a, high_b = a.astype(jnp.bfloat16), b.astype(jnp.bfloat16)
    low_a = (a - high_a.astype(F32)).astype(jnp.bfloat16)
    low_b = (b - high_b.astype(F32)).astype(jnp.bfloat16)

    def part(x, y):
        return lax.dot_general(x, y, (((ca,), (cb,)), ((), ())), preferred_element_type=F32)

    return part(high_a, high_b) + (part(high_a, low_b) + part(low_a, high_b))


def group(g):
    return slice(g * ROWS, (g + 1) * ROWS)


def lanes(r):
    return slice(r * TILE, (r + 1) * TILE)


def spot(g, r):
    return slice(g * ROWS + r * HEAD_DIM, g * ROWS + (r + 1) * HEAD_DIM)


def put(dst, r, tile):
    turned = tile.T
    for g in range(GROUPS):
        dst[spot(g, r), :] = turned[g * HEAD_DIM : (g + 1) * HEAD_DIM]


def take(values, r):
    rows = slice(r * HEAD_DIM, (r + 1) * HEAD_DIM)
    return jnp.concatenate([v[rows] for v in values], axis=0).T


def heads_out(v, g):
    return jnp.concatenate(
        [jnp.broadcast_to(v[g * PER + r : g * PER + r + 1], (HEAD_DIM, v.shape[1])) for r in range(PER)], axis=0
    )


def heads_in(v):
    return jnp.concatenate(
        [jnp.sum(v[r * HEAD_DIM : (r + 1) * HEAD_DIM], axis=0, keepdims=True) for r in range(PER)], axis=0
    )


def sigmoid(v):
    return 1.0 / (1.0 + jnp.exp(-v))


def silu_slope(v):
    s = sigmoid(v)
    return s * (1.0 + v * (1.0 - s))


def extend(ext, raw, before, at):
    ext[0:LEAD, :] = before[:, at : at + ext.shape[1]].astype(F32)
    ext[LEAD : LEAD + SPAN, :] = raw[...].astype(F32)


def group_order():
    to = lax.broadcasted_iota(jnp.int32, (LOCAL, LOCAL), 0)
    at = lax.broadcasted_iota(jnp.int32, (LOCAL, LOCAL), 1)
    return jnp.where(at == to % PER * GROUPS + to // PER, 1.0, 0.0)


def conv_tile(ext, w, cols):
    total = w[0:1, cols] * ext[LEAD - 3 : LEAD - 3 + SPAN, cols]
    for k in range(1, CONV):
        total = total + w[k : k + 1, cols] * ext[LEAD - 3 + k : LEAD - 3 + k + SPAN, cols]
    return total


def conv_back_tile(ext, pad, w, cols, grad):
    dpre = grad * silu_slope(conv_tile(ext, w, cols))
    pad[8 : 8 + SPAN, cols] = dpre
    taps = [
        jnp.sum(dpre * ext[LEAD - 3 + k : LEAD - 3 + k + SPAN, cols], axis=0, keepdims=True) for k in range(CONV)
    ]
    mine = w[0:1, cols] * pad[11 : 11 + SPAN, cols]
    ahead = w[0:1, cols] * pad[3:11, cols]
    for k in range(1, CONV):
        mine = mine + w[k : k + 1, cols] * pad[11 - k : 11 - k + SPAN, cols]
        ahead = ahead + w[k : k + 1, cols] * pad[3 - k : 11 - k, cols]
    return mine, ahead, taps


def clear_pad(pad):
    pad[0:8, :] = jnp.zeros((8, pad.shape[1]), F32)
    pad[8 + SPAN : 16 + SPAN, :] = jnp.zeros((8, pad.shape[1]), F32)


def halves(core, full, keep, give):
    keep[...] = full[pl.ds(pl.multiple_of(core * HALF, HALF), HALF), :]
    give[0:HALF, :] = full[pl.ds(pl.multiple_of((1 - core) * HALF, HALF), HALF), :]


def unite(core, full, own, got):
    full[pl.ds(pl.multiple_of(core * HALF, HALF), HALF), :] = own[...]
    full[pl.ds(pl.multiple_of((1 - core) * HALF, HALF), HALF), :] = got[...]


def triangle(upper):
    rows = lax.broadcasted_iota(jnp.int32, (SPAN, SPAN), 0)
    cols = lax.broadcasted_iota(jnp.int32, (SPAN, SPAN), 1)
    return rows <= cols if upper else rows >= cols


def steps_kernel(raw, bias, alog, d_skip, dt, heads, step, cum, ends, skip):
    order = group_order()
    dt[...] = exact(order, raw[...])
    rows = jnp.concatenate([bias[...], alog[...], d_skip[...], jnp.zeros((5, LOCAL), F32)], axis=0)
    heads[...] = exact(order, rows, 1, 1)
    v = dt[...] + heads[:, 0:1]
    skip[...] = jnp.broadcast_to(heads[:, 2:3], skip.shape)
    step[...] = jnp.maximum(v, 0.0) + jnp.log1p(jnp.exp(-jnp.abs(v)))
    rates = -jnp.exp(heads[:, 1:2]) * step[...]
    cum[...] = exact(rates, jnp.where(triangle(True), 1.0, 0.0))
    ends[...] = jnp.broadcast_to(jnp.exp(jnp.sum(rates, axis=1, keepdims=True)), ends.shape)


def turn_kernel(z, og, gain, zt, ogt, sgt):
    for r in range(PER):
        put(zt, r, z[:, lanes(r)].astype(F32))
        tile = og[:, lanes(r)].astype(F32)
        put(ogt, r, tile)
        put(sgt, r, tile * gain[:, lanes(r)])


def state_kernel(core, x, b, before, wx, wb, step, cum, ends, xt, zs, bc, keep, give, ext, extb, full):
    extend(ext, x, before, 0)
    extend(extb, b, before, x.shape[1])
    for g in range(GROUPS):
        pre = conv_tile(extb, wb, lanes(g))
        bc[:, lanes(g)] = pre * sigmoid(pre)
    for r in range(PER):
        pre = conv_tile(ext, wx, lanes(r))
        put(xt, r, pre * sigmoid(pre))
    scale = jnp.exp(-cum[...]) * step[...]
    for g in range(GROUPS):
        zg = xt[group(g), :] * heads_out(scale, g)
        zs[group(g), :] = zg
        full[group(g), :] = heads_out(ends[...], g) * dot(zg, bc[:, lanes(g)])
    halves(core[0], full, keep, give)
    give[HALF : HALF + LOCAL, :] = ends[...]


def local_kernel(c, before, wc, bc, xt, zs, cum, skip, cc, mt, y, extc):
    extend(extc, c, before, before.shape[1] - c.shape[1])
    alpha = jnp.exp(cum[...])
    causal = triangle(True)
    for g in range(GROUPS):
        pre = conv_tile(extc, wc, lanes(g))
        cg = pre * sigmoid(pre)
        cc[:, lanes(g)] = cg
        m = jnp.where(causal, dot(bc[:, lanes(g)], cg, 1, 1), 0.0)
        mt[lanes(g), :] = m
        y[group(g), :] = heads_out(alpha, g) * dot(zs[group(g), :], m) + heads_out(skip[...], g) * xt[group(g), :]


def output_kernel(core, own, got, cc, y1, cum, zt, sgt, full, y, sums):
    unite(core[0], full, own, got)
    alpha = jnp.exp(cum[...])
    for g in range(GROUPS):
        yg = y1[group(g), :] + heads_out(alpha, g) * dot(full[group(g), :], cc[:, lanes(g)], 1, 1)
        y[group(g), :] = yg
        z = zt[group(g), :]
        gated = yg * z * sigmoid(z)
        sums[g : g + 1, :] = jnp.sum(gated * gated, axis=0, keepdims=True)
        sums[GROUPS + g : GROUPS + g + 1, :] = jnp.sum(sgt[group(g), :] * gated, axis=0, keepdims=True)


def gate_kernel(core, sums, y, zt, sgt, cum, cc, keep, give, dy, dg, full):
    alpha = jnp.exp(cum[...])
    for g in range(GROUPS):
        inv = lax.rsqrt(sums[g : g + 1, :] / GROUP_WIDTH + EPSILON)
        fix = inv * inv * inv * sums[GROUPS + g : GROUPS + g + 1, :] / GROUP_WIDTH
        z = zt[group(g), :]
        act = z * sigmoid(z)
        dgated = inv * sgt[group(g), :] - y[group(g), :] * act * fix
        dg[group(g), :] = dgated
        dyg = dgated * act
        dy[group(g), :] = dyg
        full[group(g), :] = dot(heads_out(alpha, g) * dyg, cc[:, lanes(g)])
    halves(core[0], full, keep, give)


def middle_kernel(
    sums, y, zt, ogt, dy, dg, full, mt, zs, xt, bc, cc, cum, skip, c, before, wc,
    dz, db, dcum, dskip, gz, early, cpart, extc, padc, dc,
):
    alpha = jnp.exp(cum[...])
    causal = triangle(True)
    slope, shares = [], []
    for g in range(GROUPS):
        z, yg, dyg = zt[group(g), :], y[group(g), :], dy[group(g), :]
        inv = lax.rsqrt(sums[g : g + 1, :] / GROUP_WIDTH + EPSILON)
        slope.append(dg[group(g), :] * yg * silu_slope(z))
        shares.append(ogt[group(g), :] * yg * z * sigmoid(z) * inv)
        heads = slice(g * PER, (g + 1) * PER)
        x = xt[group(g), :]
        passed = heads_in(dyg * x)
        dskip[heads, :] = passed
        dcum[heads, :] = heads_in(dyg * (yg - heads_out(skip[...], g) * x))
        u = heads_out(alpha, g) * dyg
        dz[group(g), :] = dot(u, mt[lanes(g), :], 1, 1)
        dm = jnp.where(causal, dot(zs[group(g), :], u, 0, 0), 0.0)
        dc[:, lanes(g)] = dot(dm, bc[:, lanes(g)], 0, 0) + dot(u, full[group(g), :], 0, 0)
        db[:, lanes(g)] = dot(dm, cc[:, lanes(g)])
    for r in range(PER):
        gz[:, lanes(r)] = take(slope, r).astype(jnp.bfloat16)
        early[16 + r : 17 + r, :] = jnp.sum(take(shares, r), axis=0, keepdims=True)
    extend(extc, c, before, before.shape[1] - c.shape[1])
    clear_pad(padc)
    for g in range(GROUPS):
        mine, ahead, taps = conv_back_tile(extc, padc, wc, lanes(g), dc[:, lanes(g)])
        cpart[g, 0:SPAN, :] = mine
        cpart[g, SPAN : SPAN + 8, :] = ahead
        for k in range(CONV):
            early[k * GROUPS + g : k * GROUPS + g + 1, :] = taps[k]


def last_kernel(
    core, which, own, got, full, ends, dz1, db1, dcum1, dskip, early, cpart, dy, zs, xt, bc, cum, step, skip, dt, per_head,
    x, wx, b, wb, before,
    xown, heads, keep, give, packed, ddt, parts, later, ext, extb, pad, padb,
):
    unite(core[0], later, own, got)
    gamma = jnp.exp(-cum[...])
    scale = gamma * step[...]
    clear_pad(pad)
    clear_pad(padb)
    extend(ext, x, before, 0)
    extend(extb, b, before, x.shape[1])
    dxs, turned, straight = [], [], []
    at_end = lax.broadcasted_iota(jnp.int32, (PER, SPAN), 1) == SPAN - 1
    for g in range(GROUPS):
        here = slice(g * PER, (g + 1) * PER)
        zg, xg = zs[group(g), :], xt[group(g), :]
        d = heads_out(ends[...], g) * later[group(g), :]
        second = dot(d, bc[:, lanes(g)], 1, 1)
        dzg = dz1[group(g), :] + second
        dxs.append(heads_out(scale, g) * dzg + heads_out(skip[...], g) * dy[group(g), :])
        edge = heads_in(zg * second + d * full[group(g), :])
        edge = jnp.sum(edge, axis=1, keepdims=True)
        turned.append(dcum1[here, :] - heads_in(dzg * zg) + jnp.where(at_end, edge, 0.0))
        straight.append(heads_in(dzg * xg))
        dbg = db1[:, lanes(g)] + dot(zg, d, 0, 0)
        mine, ahead, taps = conv_back_tile(extb, padb, wb, lanes(g), dbg)
        parts[g, 0:SPAN, :] = mine
        parts[g, SPAN : 2 * SPAN, :] = cpart[g, 0:SPAN, :]
        parts[g, 2 * SPAN : 2 * SPAN + 8, :] = ahead
        parts[g, 2 * SPAN + 8 : 2 * SPAN + 16, :] = cpart[g, SPAN : SPAN + 8, :]
        for k in range(CONV):
            packed[k * GROUPS + g : k * GROUPS + g + 1, :] = taps[k]
    dlog = exact(jnp.concatenate(turned, axis=0), jnp.where(triangle(False), 1.0, 0.0))
    rate = -jnp.exp(per_head[:, 1:2])
    dstep = jnp.concatenate(straight, axis=0) * gamma + dlog * rate
    draw = dstep * sigmoid(dt[...] + per_head[:, 0:1])
    ddt[...] = exact(group_order(), draw, 0, 0)
    each = jnp.concatenate([draw, dlog * rate * step[...], dskip[...], jnp.zeros((LOCAL, SPAN), F32)], axis=0)
    at = lax.broadcasted_iota(jnp.int32, (SPAN, SPAN), 0)
    to = lax.broadcasted_iota(jnp.int32, (SPAN, SPAN), 1)
    source = to // LOCAL * LOCAL + to % GROUPS * PER + to % LOCAL // GROUPS
    packed[72:80, :] = exact(exact(jnp.ones((8, SPAN), F32), each, 1, 1), jnp.where(at == source, 1.0, 0.0))
    packed[16:32, :] = early[0:16, :]
    packed[64:72, :] = early[16:24, :]
    side = which[0]
    keep[...] = parts[pl.ds(side * 2, 2)]
    give[...] = parts[pl.ds((1 - side) * 2, 2)]
    for r in range(PER):
        mine, ahead, taps = conv_back_tile(ext, pad, wx, lanes(r), take(dxs, r))
        xown[:, lanes(r)] = mine
        heads[8 * r : 8 * r + 8, :] = ahead
        for k in range(CONV):
            packed[32 + k * PER + r : 33 + k * PER + r, :] = taps[k]


def pair_decays(core, pair, lead):
    mine, theirs = pair[0 : LOCAL // 2, :], pair[LOCAL // 2 : LOCAL, :]
    leads = core == lead
    return jnp.where(leads, mine, theirs), jnp.where(leads, theirs, mine), leads


def join_first_kernel(core, keep, got, ends, joint, pair):
    half = LOCAL // 2
    pair[0:half, :] = ends[pl.ds(pl.multiple_of(core[0] * half, half), half), :]
    pair[half:LOCAL, :] = got[pl.ds(pl.multiple_of(HALF + core[0] * half, half), half), :]
    first, second, leads = pair_decays(core[0], pair, 0)
    for h in range(half):
        rows = slice(h * HEAD_DIM, (h + 1) * HEAD_DIM)
        mine, theirs = keep[rows, :], got[rows, :]
        both = second[h : h + 1] * jnp.where(leads, mine, theirs) + jnp.where(leads, theirs, mine)
        for i in range(HEAD_DIM):
            joint[2 * h + i // 16, :, lanes(i % 16)] = both[i : i + 1]
        for i in range(2):
            joint[2 * h + i, :, CHUNK:] = first[h : h + 1] * second[h : h + 1]


def join_again_kernel(core, keep, got, pair, joint):
    _, second, leads = pair_decays(core[0], pair, 1)
    for h in range(LOCAL // 2):
        rows = slice(h * HEAD_DIM, (h + 1) * HEAD_DIM)
        mine, theirs = keep[rows, :], got[rows, :]
        joint[rows, :] = second[h : h + 1] * jnp.where(leads, mine, theirs) + jnp.where(leads, theirs, mine)


def split_kernel(lead, core, ahead, keep, got, pair, own, give):
    first, _, leads = pair_decays(core[0], pair, lead)
    for h in range(LOCAL // 2):
        rows = slice(h * HEAD_DIM, (h + 1) * HEAD_DIM)
        far = ahead[rows, :]
        near = first[h : h + 1] * far + jnp.where(leads, keep[rows, :], got[rows, :])
        own[rows, :] = jnp.where(leads, far, near)
        give[rows, :] = jnp.where(leads, near, far)


def settle_kernel(xown, mine, heads, gx, half):
    last = slice(SPAN - LEAD, SPAN)
    none = jnp.zeros((LEAD - 8, TILE), F32)
    for r in range(PER):
        gx[0 : SPAN - LEAD, lanes(r)] = xown[0 : SPAN - LEAD, lanes(r)].astype(jnp.bfloat16)
        more = jnp.concatenate([none, heads[8 * r : 8 * r + 8, :]], axis=0)
        gx[last, lanes(r)] = (xown[last, lanes(r)] + more).astype(jnp.bfloat16)
    for g in range(2):
        for i in range(2):
            at = 64 + 16 * g + 8 * i
            more = jnp.concatenate([none, heads[at : at + 8, :]], axis=0)
            start, stop = i * SPAN, (i + 1) * SPAN
            half[g, start : stop - LEAD, :] = mine[g, start : stop - LEAD, :].astype(jnp.bfloat16)
            half[g, stop - LEAD : stop, :] = (mine[g, stop - LEAD : stop, :] + more).astype(jnp.bfloat16)


def place_kernel(which, half, other, gb, gc):
    left = which[0] == 0
    for g in range(GROUPS):
        first, second = (half, other) if g < 2 else (other, half)
        both = jnp.where(left, first[g % 2].astype(F32), second[g % 2].astype(F32)).astype(jnp.bfloat16)
        gb[:, lanes(g)] = both[0:SPAN]
        gc[:, lanes(g)] = both[SPAN : 2 * SPAN]


def finish_kernel(bc_taps, packed, tx, tb, tc, tgain, bias, rate, skip):
    for k in range(CONV):
        for g in range(GROUPS):
            tb[k : k + 1, lanes(g)] = bc_taps[k * GROUPS + g : k * GROUPS + g + 1, :]
            tc[k : k + 1, lanes(g)] = bc_taps[16 + k * GROUPS + g : 17 + k * GROUPS + g, :]
        for r in range(PER):
            tx[k : k + 1, lanes(r)] = packed[32 + k * PER + r : 33 + k * PER + r, :]
    for r in range(PER):
        tgain[:, lanes(r)] = packed[64 + r : 65 + r, :]
    bias[...] = packed[72:73, 0:LOCAL]
    rate[...] = packed[72:73, LOCAL : 2 * LOCAL]
    skip[...] = packed[72:73, 2 * LOCAL : 3 * LOCAL]


def scan_kernel(backward, s, d, o):
    count = s.shape[0]
    at = d.shape[2] - TILE
    carry = [jnp.zeros((1, TILE), F32)] * (CHUNK // TILE)
    for j in range(count):
        j = count - 1 - j if backward else j
        decay = d[j, :, at:]
        for k in range(CHUNK // TILE):
            o[j, :, lanes(k)] = carry[k]
            carry[k] = decay * carry[k] + s[j, :, lanes(k)]


def call(kernel, name, outs, args, scratch=(), scalars=0, flops=20_000_000):
    smem = pl.BlockSpec(memory_space=pltpu.SMEM)
    vmem = pl.BlockSpec(memory_space=pltpu.VMEM)
    return pl.pallas_call(
        kernel,
        out_shape=[jax.ShapeDtypeStruct(s, d) for s, d in outs],
        in_specs=[smem if i < scalars else vmem for i in range(len(args))],
        out_specs=[vmem] * len(outs),
        scratch_shapes=[pltpu.VMEM(s, F32) for s in scratch],
        compiler_params=PARAMS,
        cost_estimate=pl.CostEstimate(flops=flops, bytes_accessed=4 << 20, transcendentals=1 << 18),
        name=name,
    )(*args)


def swap_cores(v):
    return lax.ppermute(v, "core", [(0, 1), (1, 0)])


def alike(size, by):
    return [(i, i ^ by) for i in range(size)]


def over_chips(v):
    return lax.all_to_all(v, "chip", 0, 0)


def fold(x, axis, partner):
    return x + lax.ppermute(x, axis, [(i, partner(i)) for i in range(lax.axis_size(axis))])


def sum_four(x, axis, block=1, behind=None):
    sent = [
        lax.ppermute(x, axis, [(i, (i // block ^ k) * block + i % block) for i in range(lax.axis_size(axis))])
        for k in range(1, 4)
    ]
    if behind is not None:
        *sent, behind = lax.optimization_barrier((*sent, behind))
    near, far, last = sent
    total = (x + near) + (far + last)
    return total if behind is None else (total, behind)


def mirror(within):
    return lambda i: i // within * within + within - 1 - i % within


def body(
    x_raw, b_raw, c_raw, z_gate, dt_raw, conv_x, conv_b, conv_c, dt_bias, a_log, d_skip, gain, grad_out
):
    size = lax.axis_size(CTX)
    core = lax.axis_index("core")
    side = lax.axis_index("tp") // (lax.axis_size("tp") // 2)
    cores, sides = lax.optimization_barrier((core.reshape(1), side.reshape(1)))
    is_even = core == 0
    t_shape = ((ALL, SPAN), F32)
    bc_shape = ((SPAN, GROUPS * STATE), F32)
    h_shape = ((LOCAL, SPAN), F32)
    tails = jnp.concatenate([v[SPAN - LEAD :] for v in (x_raw, b_raw, c_raw)], axis=1)
    before = lax.ppermute(tails, CTX, [(i, i + 1) for i in range(size - 1)])
    wx, wb = x_raw.shape[1], b_raw.shape[1]

    dt, per_head, step, cum, ends, skip = call(
        steps_kernel,
        "steps",
        [h_shape, ((LOCAL, 8), F32)] + [h_shape] * 4,
        (dt_raw.T, dt_bias[None], a_log[None], d_skip[None]),
    )
    zt, ogt, sgt = call(turn_kernel, "turn", [t_shape] * 3, (z_gate, grad_out, gain[None]))
    before, zt, ogt, sgt = lax.optimization_barrier((before, zt, ogt, sgt))
    xt, zs, bc, keep, give = call(
        state_kernel,
        "state",
        [t_shape, t_shape, bc_shape, ((HALF, STATE), F32), ((HALF + LOCAL, STATE), F32)],
        (cores, x_raw, b_raw, before, conv_x, conv_b, step, cum, ends),
        [(LEAD + SPAN, wx), (LEAD + SPAN, wb), (ALL, STATE)],
        scalars=1,
    )
    got = swap_cores(give)
    half_shape = ((HALF, STATE), F32)
    chips = lax.axis_size("chip")
    joint, pair = call(
        join_first_kernel,
        "join",
        [((chips, 1, CHUNK + TILE), F32), h_shape],
        (cores, keep, got, ends),
        scalars=1,
    )
    firsts = over_chips(joint)
    (entering,) = call(
        functools.partial(scan_kernel, False), "block_scan", [((chips, 1, CHUNK), F32)], (firsts, firsts)
    )
    ahead = over_chips(entering).reshape(HALF, STATE)
    enter_own, enter_give = call(
        functools.partial(split_kernel, 0), "split", [half_shape] * 2, (cores, ahead, keep, got, pair), scalars=1
    )
    enter_got = swap_cores(enter_give)

    cc, mt, y1 = call(
        local_kernel,
        "local",
        [bc_shape, ((GROUPS * SPAN, SPAN), F32), t_shape],
        (c_raw, before, conv_c, bc, xt, zs, cum, skip),
        [(LEAD + SPAN, wb)],
    )
    enter, y, sums = call(
        output_kernel,
        "output",
        [t_shape, t_shape, ((2 * GROUPS, SPAN), F32)],
        (cores, enter_own, enter_got, cc, y1, cum, zt, sgt),
        scalars=1,
    )
    sums = sum_four(sums, "tp")
    keep, give, dy, dg = call(
        gate_kernel,
        "gate",
        [((HALF, STATE), F32)] * 2 + [t_shape, t_shape],
        (cores, sums, y, zt, sgt, cum, cc),
        [(ALL, STATE)],
        scalars=1,
    )
    got = swap_cores(give)
    (joint,) = call(join_again_kernel, "join", [half_shape], (cores, keep, got, pair), scalars=1)
    pieces = over_chips(joint.reshape(chips, 1, CHUNK))
    (leaving,) = call(
        functools.partial(scan_kernel, True), "block_scan", [((chips, 1, CHUNK), F32)], (pieces, firsts)
    )
    ahead = over_chips(leaving).reshape(HALF, STATE)
    later_own, later_give = call(
        functools.partial(split_kernel, 1), "split", [half_shape] * 2, (cores, ahead, keep, got, pair), scalars=1
    )
    later_got = swap_cores(later_give)
    dz, db, dcum, dskip, grad_z, early, cpart = call(
        middle_kernel,
        "middle",
        [t_shape, bc_shape, h_shape, h_shape, ((SPAN, wx), jnp.bfloat16), ((24, TILE), F32)]
        + [((GROUPS, SPAN + 8, TILE), F32)],
        (sums, y, zt, ogt, dy, dg, enter, mt, zs, xt, bc, cc, cum, skip, c_raw, before, conv_c),
        [(LEAD + SPAN, wb), (LEAD + SPAN, wb), (SPAN, wb)],
    )
    half_parts = ((2, 2 * SPAN + 16, TILE), F32)
    xown, xheads, keep, give, packed, ddt = call(
        last_kernel,
        "last",
        [((SPAN, wx), F32), ((64, TILE), F32), half_parts, half_parts, ((80, TILE), F32), h_shape],
        (cores, sides, later_own, later_got, enter, ends, dz, db, dcum, dskip, early, cpart)
        + (dy, zs, xt, bc, cum, step, skip, dt, per_head, x_raw, conv_x, b_raw, conv_b, before),
        [(GROUPS, 2 * SPAN + 16, TILE), (ALL, STATE)]
        + [(LEAD + SPAN, wx), (LEAD + SPAN, wb), (LEAD + SPAN, wx), (LEAD + SPAN, wb)],
        scalars=2,
    )
    peers = lax.axis_size("tp")
    across = [(i, peers - 1 - i) for i in range(peers)]
    arrived = lax.ppermute(give, "tp", across)
    packed = sum_four(packed, CTX)
    packed = fold(packed, "chip", lambda i: i ^ 2)
    arrived, packed = lax.optimization_barrier((arrived, packed))
    mine = keep + arrived
    arrived = lax.ppermute(mine, "tp", [(i, i ^ 1) for i in range(peers)])
    packed = fold(packed, "chip", mirror(RING))
    mine = mine + arrived
    heads = jnp.concatenate([xheads, mine[:, 2 * SPAN :].reshape(32, TILE)], axis=0)
    mine, heads, packed = lax.optimization_barrier((mine, heads, packed))
    heads = lax.ppermute(heads, CTX, [(i + 1, i) for i in range(size - 1)])
    grad_x_raw, half = call(
        settle_kernel,
        "settle",
        [((SPAN, wx), jnp.bfloat16), ((2, 2 * SPAN, TILE), jnp.bfloat16)],
        (xown, mine, heads),
    )
    half, packed = lax.optimization_barrier((half, packed))
    other = lax.ppermute(half, "tp", across)
    half_bc, each = ((SPAN, wb), jnp.bfloat16), ((1, LOCAL), F32)
    grad_b_raw, grad_c_raw = call(
        place_kernel, "place", [half_bc, half_bc], (sides, half, other), scalars=1, flops=20_000_000_000
    )
    packed, grad_b_raw = sum_four(packed, "chip", RING, grad_b_raw)
    bc_taps = sum_four(packed[:32], "tp")
    conv_x_total, conv_b_total, conv_c_total, gain_total, *small = call(
        finish_kernel,
        "finish",
        [((CONV, wx), F32), ((CONV, wb), F32), ((CONV, wb), F32), ((1, wx), F32)] + [each] * 3,
        (bc_taps, packed),
    )
    return (
        grad_x_raw,
        grad_b_raw,
        grad_c_raw,
        grad_z,
        ddt.T,
        conv_x_total,
        conv_b_total,
        conv_c_total,
        *(v.reshape(-1) for v in small),
        gain_total.reshape(-1),
    )


def solution(mesh):
    rows, cols, some = P(CTX, "tp"), P(None, "tp"), P("tp")
    chips, tp = mesh.shape["ctx"] // 2, mesh.shape["tp"]
    mesh = Mesh(mesh.devices.reshape(chips, 2, tp), (*CTX, "tp"))
    return jax.shard_map(
        body,
        mesh=mesh,
        in_specs=(rows, P(CTX, None), P(CTX, None), rows, rows, cols, P(), P(), some, some, some, some, rows),
        out_specs=(rows, P(CTX, None), P(CTX, None), rows, rows, cols, P(), P(), some, some, some, some),
        check_vma=False,
    )
```

```python
import functools

import jax
import jax.numpy as jnp
from jax import lax
from jax.experimental import pallas as pl
from jax.experimental.pallas import tpu as pltpu
from jax.sharding import Mesh, PartitionSpec as P

HEAD_DIM = 32
STATE = 128
GROUPS = 4
CONV = 4
SPAN = 128
TILE = 128
PER = 8
LOCAL = PER * GROUPS
ROWS = PER * HEAD_DIM
ALL = LOCAL * HEAD_DIM
HALF = ALL // 2
CHUNK = 2048
LEAD = 16
GROUP_WIDTH = 1024
EPSILON = 1e-05
F32 = jnp.float32
CTX = ("chip", "core")
RING = 8
PARAMS = pltpu.CompilerParams(vmem_limit_bytes=16 << 20)


def exact(a, b, ca=1, cb=0):
    return lax.dot_general(
        a, b, (((ca,), (cb,)), ((), ())), precision=lax.Precision.HIGHEST, preferred_element_type=F32
    )


def dot(a, b, ca=1, cb=0):
    high_a, high_b = a.astype(jnp.bfloat16), b.astype(jnp.bfloat16)
    low_a = (a - high_a.astype(F32)).astype(jnp.bfloat16)
    low_b = (b - high_b.astype(F32)).astype(jnp.bfloat16)

    def part(x, y):
        return lax.dot_general(x, y, (((ca,), (cb,)), ((), ())), preferred_element_type=F32)

    return part(high_a, high_b) + (part(high_a, low_b) + part(low_a, high_b))


def group(g):
    return slice(g * ROWS, (g + 1) * ROWS)


def lanes(r):
    return slice(r * TILE, (r + 1) * TILE)


def spot(g, r):
    return slice(g * ROWS + r * HEAD_DIM, g * ROWS + (r + 1) * HEAD_DIM)


def put(dst, r, tile):
    turned = tile.T
    for g in range(GROUPS):
        dst[spot(g, r), :] = turned[g * HEAD_DIM : (g + 1) * HEAD_DIM]


def take(values, r):
    rows = slice(r * HEAD_DIM, (r + 1) * HEAD_DIM)
    return jnp.concatenate([v[rows] for v in values], axis=0).T


def heads_out(v, g):
    return jnp.concatenate(
        [jnp.broadcast_to(v[g * PER + r : g * PER + r + 1], (HEAD_DIM, v.shape[1])) for r in range(PER)], axis=0
    )


def heads_in(v):
    return jnp.concatenate(
        [jnp.sum(v[r * HEAD_DIM : (r + 1) * HEAD_DIM], axis=0, keepdims=True) for r in range(PER)], axis=0
    )


def sigmoid(v):
    return 1.0 / (1.0 + jnp.exp(-v))


def silu_slope(v):
    s = sigmoid(v)
    return s * (1.0 + v * (1.0 - s))


def extend(ext, raw, before, at):
    ext[0:LEAD, :] = before[:, at : at + ext.shape[1]].astype(F32)
    ext[LEAD : LEAD + SPAN, :] = raw[...].astype(F32)


def group_order():
    to = lax.broadcasted_iota(jnp.int32, (LOCAL, LOCAL), 0)
    at = lax.broadcasted_iota(jnp.int32, (LOCAL, LOCAL), 1)
    return jnp.where(at == to % PER * GROUPS + to // PER, 1.0, 0.0)


def conv_tile(ext, w, cols):
    total = w[0:1, cols] * ext[LEAD - 3 : LEAD - 3 + SPAN, cols]
    for k in range(1, CONV):
        total = total + w[k : k + 1, cols] * ext[LEAD - 3 + k : LEAD - 3 + k + SPAN, cols]
    return total


def conv_back_tile(ext, pad, w, cols, grad):
    dpre = grad * silu_slope(conv_tile(ext, w, cols))
    pad[8 : 8 + SPAN, cols] = dpre
    taps = [
        jnp.sum(dpre * ext[LEAD - 3 + k : LEAD - 3 + k + SPAN, cols], axis=0, keepdims=True) for k in range(CONV)
    ]
    mine = w[0:1, cols] * pad[11 : 11 + SPAN, cols]
    ahead = w[0:1, cols] * pad[3:11, cols]
    for k in range(1, CONV):
        mine = mine + w[k : k + 1, cols] * pad[11 - k : 11 - k + SPAN, cols]
        ahead = ahead + w[k : k + 1, cols] * pad[3 - k : 11 - k, cols]
    return mine, ahead, taps


def clear_pad(pad):
    pad[0:8, :] = jnp.zeros((8, pad.shape[1]), F32)
    pad[8 + SPAN : 16 + SPAN, :] = jnp.zeros((8, pad.shape[1]), F32)


def halves(core, full, keep, give):
    keep[...] = full[pl.ds(pl.multiple_of(core * HALF, HALF), HALF), :]
    give[0:HALF, :] = full[pl.ds(pl.multiple_of((1 - core) * HALF, HALF), HALF), :]


def unite(core, full, own, got):
    full[pl.ds(pl.multiple_of(core * HALF, HALF), HALF), :] = own[...]
    full[pl.ds(pl.multiple_of((1 - core) * HALF, HALF), HALF), :] = got[...]


def triangle(upper):
    rows = lax.broadcasted_iota(jnp.int32, (SPAN, SPAN), 0)
    cols = lax.broadcasted_iota(jnp.int32, (SPAN, SPAN), 1)
    return rows <= cols if upper else rows >= cols


def steps_kernel(raw, bias, alog, d_skip, dt, heads, step, cum, ends, skip):
    order = group_order()
    dt[...] = exact(order, raw[...])
    rows = jnp.concatenate([bias[...], alog[...], d_skip[...], jnp.zeros((5, LOCAL), F32)], axis=0)
    heads[...] = exact(order, rows, 1, 1)
    v = dt[...] + heads[:, 0:1]
    skip[...] = jnp.broadcast_to(heads[:, 2:3], skip.shape)
    step[...] = jnp.maximum(v, 0.0) + jnp.log1p(jnp.exp(-jnp.abs(v)))
    rates = -jnp.exp(heads[:, 1:2]) * step[...]
    cum[...] = exact(rates, jnp.where(triangle(True), 1.0, 0.0))
    ends[...] = jnp.broadcast_to(jnp.exp(jnp.sum(rates, axis=1, keepdims=True)), ends.shape)


def turn_kernel(z, og, gain, zt, ogt, sgt):
    for r in range(PER):
        put(zt, r, z[:, lanes(r)].astype(F32))
        tile = og[:, lanes(r)].astype(F32)
        put(ogt, r, tile)
        put(sgt, r, tile * gain[:, lanes(r)])


def state_kernel(core, x, b, before, wx, wb, step, cum, ends, xt, zs, bc, keep, give, ext, extb, full):
    extend(ext, x, before, 0)
    extend(extb, b, before, x.shape[1])
    for g in range(GROUPS):
        pre = conv_tile(extb, wb, lanes(g))
        bc[:, lanes(g)] = pre * sigmoid(pre)
    for r in range(PER):
        pre = conv_tile(ext, wx, lanes(r))
        put(xt, r, pre * sigmoid(pre))
    scale = jnp.exp(-cum[...]) * step[...]
    for g in range(GROUPS):
        zg = xt[group(g), :] * heads_out(scale, g)
        zs[group(g), :] = zg
        full[group(g), :] = heads_out(ends[...], g) * dot(zg, bc[:, lanes(g)])
    halves(core[0], full, keep, give)
    give[HALF : HALF + LOCAL, :] = ends[...]


def local_kernel(c, before, wc, bc, xt, zs, cum, skip, cc, mt, y, extc):
    extend(extc, c, before, before.shape[1] - c.shape[1])
    alpha = jnp.exp(cum[...])
    causal = triangle(True)
    for g in range(GROUPS):
        pre = conv_tile(extc, wc, lanes(g))
        cg = pre * sigmoid(pre)
        cc[:, lanes(g)] = cg
        m = jnp.where(causal, dot(bc[:, lanes(g)], cg, 1, 1), 0.0)
        mt[lanes(g), :] = m
        y[group(g), :] = heads_out(alpha, g) * dot(zs[group(g), :], m) + heads_out(skip[...], g) * xt[group(g), :]


def output_kernel(core, own, got, cc, y1, cum, zt, sgt, full, y, sums):
    unite(core[0], full, own, got)
    alpha = jnp.exp(cum[...])
    for g in range(GROUPS):
        yg = y1[group(g), :] + heads_out(alpha, g) * dot(full[group(g), :], cc[:, lanes(g)], 1, 1)
        y[group(g), :] = yg
        z = zt[group(g), :]
        gated = yg * z * sigmoid(z)
        sums[g : g + 1, :] = jnp.sum(gated * gated, axis=0, keepdims=True)
        sums[GROUPS + g : GROUPS + g + 1, :] = jnp.sum(sgt[group(g), :] * gated, axis=0, keepdims=True)


def gate_kernel(core, sums, y, zt, sgt, cum, cc, keep, give, dy, dg, full):
    alpha = jnp.exp(cum[...])
    for g in range(GROUPS):
        inv = lax.rsqrt(sums[g : g + 1, :] / GROUP_WIDTH + EPSILON)
        fix = inv * inv * inv * sums[GROUPS + g : GROUPS + g + 1, :] / GROUP_WIDTH
        z = zt[group(g), :]
        act = z * sigmoid(z)
        dgated = inv * sgt[group(g), :] - y[group(g), :] * act * fix
        dg[group(g), :] = dgated
        dyg = dgated * act
        dy[group(g), :] = dyg
        full[group(g), :] = dot(heads_out(alpha, g) * dyg, cc[:, lanes(g)])
    halves(core[0], full, keep, give)


def middle_kernel(
    sums, y, zt, ogt, dy, dg, full, mt, zs, xt, bc, cc, cum, skip, c, before, wc,
    dz, db, dcum, dskip, gz, early, cpart, extc, padc, dc,
):
    alpha = jnp.exp(cum[...])
    causal = triangle(True)
    slope, shares = [], []
    for g in range(GROUPS):
        z, yg, dyg = zt[group(g), :], y[group(g), :], dy[group(g), :]
        inv = lax.rsqrt(sums[g : g + 1, :] / GROUP_WIDTH + EPSILON)
        slope.append(dg[group(g), :] * yg * silu_slope(z))
        shares.append(ogt[group(g), :] * yg * z * sigmoid(z) * inv)
        heads = slice(g * PER, (g + 1) * PER)
        x = xt[group(g), :]
        passed = heads_in(dyg * x)
        dskip[heads, :] = passed
        dcum[heads, :] = heads_in(dyg * (yg - heads_out(skip[...], g) * x))
        u = heads_out(alpha, g) * dyg
        dz[group(g), :] = dot(u, mt[lanes(g), :], 1, 1)
        dm = jnp.where(causal, dot(zs[group(g), :], u, 0, 0), 0.0)
        dc[:, lanes(g)] = dot(dm, bc[:, lanes(g)], 0, 0) + dot(u, full[group(g), :], 0, 0)
        db[:, lanes(g)] = dot(dm, cc[:, lanes(g)])
    for r in range(PER):
        gz[:, lanes(r)] = take(slope, r).astype(jnp.bfloat16)
        early[16 + r : 17 + r, :] = jnp.sum(take(shares, r), axis=0, keepdims=True)
    extend(extc, c, before, before.shape[1] - c.shape[1])
    clear_pad(padc)
    for g in range(GROUPS):
        mine, ahead, taps = conv_back_tile(extc, padc, wc, lanes(g), dc[:, lanes(g)])
        cpart[g, 0:SPAN, :] = mine
        cpart[g, SPAN : SPAN + 8, :] = ahead
        for k in range(CONV):
            early[k * GROUPS + g : k * GROUPS + g + 1, :] = taps[k]


def last_kernel(
    core, which, own, got, full, ends, dz1, db1, dcum1, dskip, early, cpart, dy, zs, xt, bc, cum, step, skip, dt, per_head,
    x, wx, b, wb, before,
    xown, heads, keep, give, packed, ddt, parts, later, ext, extb, pad, padb,
):
    unite(core[0], later, own, got)
    gamma = jnp.exp(-cum[...])
    scale = gamma * step[...]
    clear_pad(pad)
    clear_pad(padb)
    extend(ext, x, before, 0)
    extend(extb, b, before, x.shape[1])
    dxs, turned, straight = [], [], []
    at_end = lax.broadcasted_iota(jnp.int32, (PER, SPAN), 1) == SPAN - 1
    for g in range(GROUPS):
        here = slice(g * PER, (g + 1) * PER)
        zg, xg = zs[group(g), :], xt[group(g), :]
        d = heads_out(ends[...], g) * later[group(g), :]
        second = dot(d, bc[:, lanes(g)], 1, 1)
        dzg = dz1[group(g), :] + second
        dxs.append(heads_out(scale, g) * dzg + heads_out(skip[...], g) * dy[group(g), :])
        edge = heads_in(zg * second + d * full[group(g), :])
        edge = jnp.sum(edge, axis=1, keepdims=True)
        turned.append(dcum1[here, :] - heads_in(dzg * zg) + jnp.where(at_end, edge, 0.0))
        straight.append(heads_in(dzg * xg))
        dbg = db1[:, lanes(g)] + dot(zg, d, 0, 0)
        mine, ahead, taps = conv_back_tile(extb, padb, wb, lanes(g), dbg)
        parts[g, 0:SPAN, :] = mine
        parts[g, SPAN : 2 * SPAN, :] = cpart[g, 0:SPAN, :]
        parts[g, 2 * SPAN : 2 * SPAN + 8, :] = ahead
        parts[g, 2 * SPAN + 8 : 2 * SPAN + 16, :] = cpart[g, SPAN : SPAN + 8, :]
        for k in range(CONV):
            packed[k * GROUPS + g : k * GROUPS + g + 1, :] = taps[k]
    dlog = exact(jnp.concatenate(turned, axis=0), jnp.where(triangle(False), 1.0, 0.0))
    rate = -jnp.exp(per_head[:, 1:2])
    dstep = jnp.concatenate(straight, axis=0) * gamma + dlog * rate
    draw = dstep * sigmoid(dt[...] + per_head[:, 0:1])
    ddt[...] = exact(group_order(), draw, 0, 0)
    each = jnp.concatenate([draw, dlog * rate * step[...], dskip[...], jnp.zeros((LOCAL, SPAN), F32)], axis=0)
    at = lax.broadcasted_iota(jnp.int32, (SPAN, SPAN), 0)
    to = lax.broadcasted_iota(jnp.int32, (SPAN, SPAN), 1)
    source = to // LOCAL * LOCAL + to % GROUPS * PER + to % LOCAL // GROUPS
    packed[72:80, :] = exact(exact(jnp.ones((8, SPAN), F32), each, 1, 1), jnp.where(at == source, 1.0, 0.0))
    packed[16:32, :] = early[0:16, :]
    packed[64:72, :] = early[16:24, :]
    side = which[0]
    keep[...] = parts[pl.ds(side * 2, 2)]
    give[...] = parts[pl.ds((1 - side) * 2, 2)]
    for r in range(PER):
        mine, ahead, taps = conv_back_tile(ext, pad, wx, lanes(r), take(dxs, r))
        xown[:, lanes(r)] = mine
        heads[8 * r : 8 * r + 8, :] = ahead
        for k in range(CONV):
            packed[32 + k * PER + r : 33 + k * PER + r, :] = taps[k]


def pair_decays(core, pair, lead):
    mine, theirs = pair[0 : LOCAL // 2, :], pair[LOCAL // 2 : LOCAL, :]
    leads = core == lead
    return jnp.where(leads, mine, theirs), jnp.where(leads, theirs, mine), leads


def join_first_kernel(core, keep, got, ends, joint, pair):
    half = LOCAL // 2
    pair[0:half, :] = ends[pl.ds(pl.multiple_of(core[0] * half, half), half), :]
    pair[half:LOCAL, :] = got[pl.ds(pl.multiple_of(HALF + core[0] * half, half), half), :]
    first, second, leads = pair_decays(core[0], pair, 0)
    for h in range(half):
        rows = slice(h * HEAD_DIM, (h + 1) * HEAD_DIM)
        mine, theirs = keep[rows, :], got[rows, :]
        both = second[h : h + 1] * jnp.where(leads, mine, theirs) + jnp.where(leads, theirs, mine)
        for i in range(HEAD_DIM):
            joint[2 * h + i // 16, :, lanes(i % 16)] = both[i : i + 1]
        for i in range(2):
            joint[2 * h + i, :, CHUNK:] = first[h : h + 1] * second[h : h + 1]


def join_again_kernel(core, keep, got, pair, joint):
    _, second, leads = pair_decays(core[0], pair, 1)
    for h in range(LOCAL // 2):
        rows = slice(h * HEAD_DIM, (h + 1) * HEAD_DIM)
        mine, theirs = keep[rows, :], got[rows, :]
        joint[rows, :] = second[h : h + 1] * jnp.where(leads, mine, theirs) + jnp.where(leads, theirs, mine)


def split_kernel(lead, core, ahead, keep, got, pair, own, give):
    first, _, leads = pair_decays(core[0], pair, lead)
    for h in range(LOCAL // 2):
        rows = slice(h * HEAD_DIM, (h + 1) * HEAD_DIM)
        far = ahead[rows, :]
        near = first[h : h + 1] * far + jnp.where(leads, keep[rows, :], got[rows, :])
        own[rows, :] = jnp.where(leads, far, near)
        give[rows, :] = jnp.where(leads, near, far)


def settle_x_kernel(xown, heads, gx):
    last = slice(SPAN - LEAD, SPAN)
    none = jnp.zeros((LEAD - 8, TILE), F32)
    for r in range(PER):
        gx[0 : SPAN - LEAD, lanes(r)] = xown[0 : SPAN - LEAD, lanes(r)].astype(jnp.bfloat16)
        more = jnp.concatenate([none, heads[8 * r : 8 * r + 8, :]], axis=0)
        gx[last, lanes(r)] = (xown[last, lanes(r)] + more).astype(jnp.bfloat16)


def settle_kernel(mine, heads, half):
    none = jnp.zeros((LEAD - 8, TILE), F32)
    for g in range(2):
        for i in range(2):
            at = 64 + 16 * g + 8 * i
            more = jnp.concatenate([none, heads[at : at + 8, :]], axis=0)
            start, stop = i * SPAN, (i + 1) * SPAN
            half[g, start : stop - LEAD, :] = mine[g, start : stop - LEAD, :].astype(jnp.bfloat16)
            half[g, stop - LEAD : stop, :] = (mine[g, stop - LEAD : stop, :] + more).astype(jnp.bfloat16)


def place_kernel(which, half, other, gb, gc):
    left = which[0] == 0
    for g in range(GROUPS):
        first, second = (half, other) if g < 2 else (other, half)
        both = jnp.where(left, first[g % 2].astype(F32), second[g % 2].astype(F32)).astype(jnp.bfloat16)
        gb[:, lanes(g)] = both[0:SPAN]
        gc[:, lanes(g)] = both[SPAN : 2 * SPAN]


def finish_kernel(bc_taps, packed, tx, tb, tc, tgain, bias, rate, skip):
    for k in range(CONV):
        for g in range(GROUPS):
            tb[k : k + 1, lanes(g)] = bc_taps[k * GROUPS + g : k * GROUPS + g + 1, :]
            tc[k : k + 1, lanes(g)] = bc_taps[16 + k * GROUPS + g : 17 + k * GROUPS + g, :]
        for r in range(PER):
            tx[k : k + 1, lanes(r)] = packed[32 + k * PER + r : 33 + k * PER + r, :]
    for r in range(PER):
        tgain[:, lanes(r)] = packed[64 + r : 65 + r, :]
    bias[...] = packed[72:73, 0:LOCAL]
    rate[...] = packed[72:73, LOCAL : 2 * LOCAL]
    skip[...] = packed[72:73, 2 * LOCAL : 3 * LOCAL]


def scan_kernel(backward, s, d, o):
    count = s.shape[0]
    at = d.shape[2] - TILE
    carry = [jnp.zeros((1, TILE), F32)] * (CHUNK // TILE)
    for j in range(count):
        j = count - 1 - j if backward else j
        decay = d[j, :, at:]
        for k in range(CHUNK // TILE):
            o[j, :, lanes(k)] = carry[k]
            carry[k] = decay * carry[k] + s[j, :, lanes(k)]


def call(kernel, name, outs, args, scratch=(), scalars=0, flops=20_000_000):
    smem = pl.BlockSpec(memory_space=pltpu.SMEM)
    vmem = pl.BlockSpec(memory_space=pltpu.VMEM)
    return pl.pallas_call(
        kernel,
        out_shape=[jax.ShapeDtypeStruct(s, d) for s, d in outs],
        in_specs=[smem if i < scalars else vmem for i in range(len(args))],
        out_specs=[vmem] * len(outs),
        scratch_shapes=[pltpu.VMEM(s, F32) for s in scratch],
        compiler_params=PARAMS,
        cost_estimate=pl.CostEstimate(flops=flops, bytes_accessed=4 << 20, transcendentals=1 << 18),
        name=name,
    )(*args)


def swap_cores(v):
    return lax.ppermute(v, "core", [(0, 1), (1, 0)])


def alike(size, by):
    return [(i, i ^ by) for i in range(size)]


def over_chips(v):
    return lax.all_to_all(v, "chip", 0, 0)


def fold(x, axis, partner):
    return x + lax.ppermute(x, axis, [(i, partner(i)) for i in range(lax.axis_size(axis))])


def sum_four(x, axis, block=1, behind=None):
    sent = [
        lax.ppermute(x, axis, [(i, (i // block ^ k) * block + i % block) for i in range(lax.axis_size(axis))])
        for k in range(1, 4)
    ]
    if behind is not None:
        *sent, behind = lax.optimization_barrier((*sent, behind))
    near, far, last = sent
    total = (x + near) + (far + last)
    return total if behind is None else (total, behind)


def mirror(within):
    return lambda i: i // within * within + within - 1 - i % within


def body(
    x_raw, b_raw, c_raw, z_gate, dt_raw, conv_x, conv_b, conv_c, dt_bias, a_log, d_skip, gain, grad_out
):
    size = lax.axis_size(CTX)
    core = lax.axis_index("core")
    side = lax.axis_index("tp") // (lax.axis_size("tp") // 2)
    cores, sides = lax.optimization_barrier((core.reshape(1), side.reshape(1)))
    is_even = core == 0
    t_shape = ((ALL, SPAN), F32)
    bc_shape = ((SPAN, GROUPS * STATE), F32)
    h_shape = ((LOCAL, SPAN), F32)
    tails = jnp.concatenate([v[SPAN - LEAD :] for v in (x_raw, b_raw, c_raw)], axis=1)
    before = lax.ppermute(tails, CTX, [(i, i + 1) for i in range(size - 1)])
    wx, wb = x_raw.shape[1], b_raw.shape[1]

    dt, per_head, step, cum, ends, skip = call(
        steps_kernel,
        "steps",
        [h_shape, ((LOCAL, 8), F32)] + [h_shape] * 4,
        (dt_raw.T, dt_bias[None], a_log[None], d_skip[None]),
    )
    zt, ogt, sgt = call(turn_kernel, "turn", [t_shape] * 3, (z_gate, grad_out, gain[None]))
    before, zt, ogt, sgt = lax.optimization_barrier((before, zt, ogt, sgt))
    xt, zs, bc, keep, give = call(
        state_kernel,
        "state",
        [t_shape, t_shape, bc_shape, ((HALF, STATE), F32), ((HALF + LOCAL, STATE), F32)],
        (cores, x_raw, b_raw, before, conv_x, conv_b, step, cum, ends),
        [(LEAD + SPAN, wx), (LEAD + SPAN, wb), (ALL, STATE)],
        scalars=1,
    )
    got = swap_cores(give)
    half_shape = ((HALF, STATE), F32)
    chips = lax.axis_size("chip")
    joint, pair = call(
        join_first_kernel,
        "join",
        [((chips, 1, CHUNK + TILE), F32), h_shape],
        (cores, keep, got, ends),
        scalars=1,
    )
    firsts = over_chips(joint)
    (entering,) = call(
        functools.partial(scan_kernel, False), "block_scan", [((chips, 1, CHUNK), F32)], (firsts, firsts)
    )
    ahead = over_chips(entering).reshape(HALF, STATE)
    enter_own, enter_give = call(
        functools.partial(split_kernel, 0), "split", [half_shape] * 2, (cores, ahead, keep, got, pair), scalars=1
    )
    enter_got = swap_cores(enter_give)

    cc, mt, y1 = call(
        local_kernel,
        "local",
        [bc_shape, ((GROUPS * SPAN, SPAN), F32), t_shape],
        (c_raw, before, conv_c, bc, xt, zs, cum, skip),
        [(LEAD + SPAN, wb)],
    )
    enter, y, sums = call(
        output_kernel,
        "output",
        [t_shape, t_shape, ((2 * GROUPS, SPAN), F32)],
        (cores, enter_own, enter_got, cc, y1, cum, zt, sgt),
        scalars=1,
    )
    sums = sum_four(sums, "tp")
    keep, give, dy, dg = call(
        gate_kernel,
        "gate",
        [((HALF, STATE), F32)] * 2 + [t_shape, t_shape],
        (cores, sums, y, zt, sgt, cum, cc),
        [(ALL, STATE)],
        scalars=1,
    )
    got = swap_cores(give)
    (joint,) = call(join_again_kernel, "join", [half_shape], (cores, keep, got, pair), scalars=1)
    pieces = over_chips(joint.reshape(chips, 1, CHUNK))
    (leaving,) = call(
        functools.partial(scan_kernel, True), "block_scan", [((chips, 1, CHUNK), F32)], (pieces, firsts)
    )
    ahead = over_chips(leaving).reshape(HALF, STATE)
    later_own, later_give = call(
        functools.partial(split_kernel, 1), "split", [half_shape] * 2, (cores, ahead, keep, got, pair), scalars=1
    )
    later_got = swap_cores(later_give)
    dz, db, dcum, dskip, grad_z, early, cpart = call(
        middle_kernel,
        "middle",
        [t_shape, bc_shape, h_shape, h_shape, ((SPAN, wx), jnp.bfloat16), ((24, TILE), F32)]
        + [((GROUPS, SPAN + 8, TILE), F32)],
        (sums, y, zt, ogt, dy, dg, enter, mt, zs, xt, bc, cc, cum, skip, c_raw, before, conv_c),
        [(LEAD + SPAN, wb), (LEAD + SPAN, wb), (SPAN, wb)],
    )
    half_parts = ((2, 2 * SPAN + 16, TILE), F32)
    xown, xheads, keep, give, packed, ddt = call(
        last_kernel,
        "last",
        [((SPAN, wx), F32), ((64, TILE), F32), half_parts, half_parts, ((80, TILE), F32), h_shape],
        (cores, sides, later_own, later_got, enter, ends, dz, db, dcum, dskip, early, cpart)
        + (dy, zs, xt, bc, cum, step, skip, dt, per_head, x_raw, conv_x, b_raw, conv_b, before),
        [(GROUPS, 2 * SPAN + 16, TILE), (ALL, STATE)]
        + [(LEAD + SPAN, wx), (LEAD + SPAN, wb), (LEAD + SPAN, wx), (LEAD + SPAN, wb)],
        scalars=2,
    )
    peers = lax.axis_size("tp")
    across = [(i, peers - 1 - i) for i in range(peers)]
    arrived = lax.ppermute(give, "tp", across)
    packed = packed + swap_cores(packed)
    packed = fold(packed, "chip", mirror(2))
    packed = fold(packed, "chip", lambda i: i ^ 2)
    arrived, packed = lax.optimization_barrier((arrived, packed))
    mine = keep + arrived
    arrived = lax.ppermute(mine, "tp", [(i, i ^ 1) for i in range(peers)])
    packed = fold(packed, "chip", mirror(RING))
    mine = mine + arrived
    heads = jnp.concatenate([xheads, mine[:, 2 * SPAN :].reshape(32, TILE)], axis=0)
    mine, heads, packed = lax.optimization_barrier((mine, heads, packed))
    heads = lax.ppermute(heads, CTX, [(i + 1, i) for i in range(size - 1)])
    (half,) = call(settle_kernel, "settle", [((2, 2 * SPAN, TILE), jnp.bfloat16)], (mine, heads))
    (grad_x_raw,) = call(settle_x_kernel, "settle_x", [((SPAN, wx), jnp.bfloat16)], (xown, heads))
    half, packed = lax.optimization_barrier((half, packed))
    other = lax.ppermute(half, "tp", across)
    half_bc, each = ((SPAN, wb), jnp.bfloat16), ((1, LOCAL), F32)
    grad_b_raw, grad_c_raw = call(
        place_kernel, "place", [half_bc, half_bc], (sides, half, other), scalars=1, flops=20_000_000_000
    )
    packed, grad_b_raw = sum_four(packed, "chip", RING, grad_b_raw)
    bc_taps = sum_four(packed[:32], "tp")
    conv_x_total, conv_b_total, conv_c_total, gain_total, *small = call(
        finish_kernel,
        "finish",
        [((CONV, wx), F32), ((CONV, wb), F32), ((CONV, wb), F32), ((1, wx), F32)] + [each] * 3,
        (bc_taps, packed),
    )
    return (
        grad_x_raw,
        grad_b_raw,
        grad_c_raw,
        grad_z,
        ddt.T,
        conv_x_total,
        conv_b_total,
        conv_c_total,
        *(v.reshape(-1) for v in small),
        gain_total.reshape(-1),
    )


def solution(mesh):
    rows, cols, some = P(CTX, "tp"), P(None, "tp"), P("tp")
    chips, tp = mesh.shape["ctx"] // 2, mesh.shape["tp"]
    mesh = Mesh(mesh.devices.reshape(chips, 2, tp), (*CTX, "tp"))
    return jax.shard_map(
        body,
        mesh=mesh,
        in_specs=(rows, P(CTX, None), P(CTX, None), rows, rows, cols, P(), P(), some, some, some, some, rows),
        out_specs=(rows, P(CTX, None), P(CTX, None), rows, rows, cols, P(), P(), some, some, some, some),
        check_vma=False,
    )
```
